32 devices in a mesh: seq: 8 (over y, x, core), clip: 4 (over z).
Axes of the slice: x: 2, y: 2, z: 4, core: 2. Of those that a mesh axis runs over, the one named last changes fastest.
Arguments:
- clips: bfloat16 [4, 8, 16, 7, 7, 512], P('clip', 'seq'), may hold values from -6 to 6
- cotangent: bfloat16 [4, 8, 16, 7, 7, 512], P('clip', 'seq'), may hold values from -6 to 6
- qkv_w: float32 [3, 512, 512], P(None, 'clip'), may hold values from -0.25 to 0.25
- proj_w: float32 [512, 512], P('clip'), may hold values from -2 to 2
- fc1_w: float32 [512, 2048], P('clip'), may hold values from -0.25 to 0.25
- fc2_w: float32 [2048, 512], P('clip'), may hold values from -0.25 to 0.25
- qkv_m: float32 [3, 512, 512], P(None, 'clip'), may hold values from -640 to 640
- proj_m: float32 [512, 512], P('clip'), may hold values from -128 to 128
- fc1_m: float32 [512, 2048], P('clip'), may hold values from -512 to 512
- fc2_m: float32 [2048, 512], P('clip'), may hold values from -512 to 512
- vectors: float32 [12, 512], replicated, may hold values from -1 to 1.5
- vector_m: float32 [12, 512], replicated, may hold values from -768 to 768
- table: float32 [2535, 16], replicated, may hold values from -3 to 3
- table_m: float32 [2535, 16], replicated, may hold values from -80 to 80
Outputs:
- output: bfloat16 [4, 8, 16, 7, 7, 512], P('clip', 'seq')
- input_grad: bfloat16 [4, 8, 16, 7, 7, 512], P('clip', 'seq')
- new_qkv_m: float32 [3, 512, 512], P(None, 'clip')
- new_proj_m: float32 [512, 512], P('clip')
- new_fc1_m: float32 [512, 2048], P('clip')
- new_fc2_m: float32 [2048, 512], P('clip')
- new_qkv_w: float32 [3, 512, 512], P(None, 'clip')
- new_proj_w: float32 [512, 512], P('clip')
- new_fc1_w: float32 [512, 2048], P('clip')
- new_fc2_w: float32 [2048, 512], P('clip')
- new_vector_m: float32 [12, 512], replicated
- new_vectors: float32 [12, 512], replicated
- new_table_m: float32 [2535, 16], replicated
- new_table: float32 [2535, 16], replicated
The draws below stay inside these ranges and needn't reach their ends.
All inputs are finite; a program needn't handle non-finite values.
Results may differ from the reference program's by a relative error of at most 0.014.
Values may be sent and summed in bfloat16 or wider, within the bound.
A program may use at most 320 MiB of HBM per device.

```python
import math
import jax
import jax.numpy as jnp
from jax import lax

C = 512
HEADS = 16
HEAD_DIM = 32
MLP_UNITS = 2048
WIN_T = 8
SIDE = 7
SHIFT_T = 4
SHIFT_S = 3
GRID_W = 2
FRAMES = 16
GRID_H = 4
TILES = 8
CLIPS = 4
HEIGHT = 28
WIDTH = 14
WIN = 392
TABLE = 2535
VEC_ROWS = 12
ALL_TOKENS = 25088


def draw_vectors(key, part):
    key = jax.random.fold_in(key, 11)
    noise = jnp.clip(jax.random.normal(key, (VEC_ROWS, C), jnp.float32), -3.0, 3.0)
    slots = jnp.arange(VEC_ROWS)[:, None]
    gains = (slots == 0) | (slots == 5)
    return jnp.where(gains, 1.0 + 0.15 * noise, 0.3 * noise).astype(jnp.float32)


def levels(own_key, dims, cuts, least, largest):
    loudness = 1.0
    for axis_at, blocks in cuts:
        steps = jax.random.uniform(jax.random.fold_in(jax.random.fold_in(own_key, 6), axis_at), (blocks,), jnp.float32, least / len(cuts), largest / len(cuts))
        loudness = loudness * jnp.repeat(jnp.exp(steps), dims[axis_at] // blocks).reshape((-1,) + (1,) * (len(dims) - 1 - axis_at))
    return loudness


def bell_draw(key, shape, scale, most, split=(), kind=jnp.bfloat16):
    drawn = jax.random.normal(key, shape, jnp.float32) * scale
    if len(split) > 0:
        drawn = levels(key, shape, split, -0.22, 0.18) * drawn
    return jnp.clip(drawn, min=-most, max=most).astype(kind)


def setup_inputs(seed: int = 0) -> dict:
    key_of = jax.random.split(jax.random.key(seed), 15)
    clips = bell_draw(key_of[0], (CLIPS, TILES, FRAMES, SIDE, SIDE, C), 1.0, 6.0, ((0, 4), (1, 8)))
    cotangent = bell_draw(key_of[1], (CLIPS, TILES, FRAMES, SIDE, SIDE, C), 1.0, 6.0, ((0, 4), (1, 8)))
    qkv_w = bell_draw(key_of[2], (3, C, C), C ** -0.5, 0.25, ((1, 4),), jnp.float32)
    proj_w = bell_draw(key_of[3], (C, C), (max(C * 8 // WIN, 1)) ** -0.5, 2.0, ((0, 4),), jnp.float32)
    fc1_w = bell_draw(key_of[4], (C, MLP_UNITS), C ** -0.5, 0.25, ((0, 4),), jnp.float32)
    fc2_w = bell_draw(key_of[5], (MLP_UNITS, C), (MLP_UNITS // 4) ** -0.5, 0.25, ((0, 4),), jnp.float32)
    qkv_m = bell_draw(key_of[6], (3, C, C), (0.7 * ALL_TOKENS ** 0.5), 640.0, ((1, 4),), jnp.float32)
    proj_m = bell_draw(key_of[7], (C, C), (0.15 * ALL_TOKENS ** 0.5), 128.0, ((0, 4),), jnp.float32)
    fc1_m = bell_draw(key_of[8], (C, MLP_UNITS), (0.6 * ALL_TOKENS ** 0.5), 512.0, ((0, 4),), jnp.float32)
    fc2_m = bell_draw(key_of[9], (MLP_UNITS, C), (0.6 * ALL_TOKENS ** 0.5), 512.0, ((0, 4),), jnp.float32)
    vectors = draw_vectors(jax.random.fold_in(key_of[14], 71), 0)
    vector_m = bell_draw(key_of[11], (VEC_ROWS, C), (0.8 * ALL_TOKENS ** 0.5), 768.0, (), jnp.float32)
    table = bell_draw(key_of[12], (TABLE, HEADS), 1.0, 3.0, (), jnp.float32)
    table_m = bell_draw(key_of[13], (TABLE, HEADS), (0.2 * (ALL_TOKENS * WIN // TABLE) ** 0.5), 80.0, (), jnp.float32)
    return dict(clips=clips, cotangent=cotangent, qkv_w=qkv_w, proj_w=proj_w, fc1_w=fc1_w, fc2_w=fc2_w, qkv_m=qkv_m, proj_m=proj_m, fc1_m=fc1_m, fc2_m=fc2_m, vectors=vectors, vector_m=vector_m, table=table, table_m=table_m)


epsilon_norm = 1e-05
mask_value = -100.0
momentum_decay = 0.95
vector_decay = 0.9
matrix_rate = 1.0
vector_rate = 0.0006
table_rate = 0.03
quintic_first = 3.4445
quintic_second = -4.775
quintic_third = 2.0315
frobenius_epsilon = 1e-07

@jax.custom_vjp
def low(v):
    return lax.optimization_barrier(v.astype(jnp.bfloat16)).astype(jnp.float32)

@jax.custom_vjp
def low_back(v):
    return v

def low_keep(v):
    return (low(v), None)

def low_pass(kept, grad):
    return (grad,)

def back_keep(v):
    return (v, None)

def back_low(kept, grad):
    return (low(grad),)
low.defvjp(low_keep, low_pass)
low_back.defvjp(back_keep, back_low)

def region_label(position, extent, window, shift):
    return jnp.where(position < extent - window, 0, jnp.where(position < extent - shift, 1, 2)).astype(jnp.int32)

def relative_index():
    frames = jnp.arange(WIN_T, dtype=jnp.int32)
    cells = jnp.arange(SIDE, dtype=jnp.int32)
    frame_grid, row_grid, column_grid = jnp.meshgrid(frames, cells, cells, indexing='ij')
    frame_flat = frame_grid.reshape(-1)
    row_flat = row_grid.reshape(-1)
    column_flat = column_grid.reshape(-1)
    span = 2 * SIDE - 1
    frame_rel = frame_flat[:, None] - frame_flat[None, :] + (WIN_T - 1)
    row_rel = row_flat[:, None] - row_flat[None, :] + (SIDE - 1)
    column_rel = column_flat[:, None] - column_flat[None, :] + (SIDE - 1)
    return (frame_rel * (span * span) + row_rel * span + column_rel).astype(jnp.int32)

def precise(left, right):
    return jnp.dot(left, right, precision=lax.Precision.HIGHEST, preferred_element_type=jnp.float32)

def orthogonalize(matrix):
    height, breadth = matrix.shape
    current = matrix / (jnp.sqrt(jnp.sum(matrix * matrix)) + frobenius_epsilon)
    if height > breadth:
        current = current.T
    for sweep in range(5):
        gram = precise(current, current.T)
        polynomial = quintic_second * gram + quintic_third * precise(gram, gram)
        current = quintic_first * current + precise(polynomial, current)
    if height > breadth:
        current = current.T
    return current * math.sqrt(max(1.0, height / breadth))

def product(left, right):
    return jnp.matmul(left, right, precision=lax.Precision.HIGHEST)

def layer_norm(values, gain, shift):
    mean = lax.optimization_barrier(jnp.mean(values, axis=-1, keepdims=True))
    centred = values - mean
    variance = lax.optimization_barrier(jnp.mean(centred * centred, axis=-1, keepdims=True))
    return centred * lax.rsqrt(variance + epsilon_norm) * gain + shift

def window_cut(field):
    width = field.shape[-1]
    blocks = field.reshape(FRAMES // WIN_T, WIN_T, GRID_H, SIDE, GRID_W, SIDE, width)
    return blocks.transpose(0, 2, 4, 1, 3, 5, 6).reshape(-1, WIN, width)

def window_join(windows):
    width = windows.shape[-1]
    blocks = windows.reshape(FRAMES // WIN_T, GRID_H, GRID_W, WIN_T, SIDE, SIDE, width)
    return blocks.transpose(0, 3, 1, 4, 2, 5, 6).reshape(FRAMES, HEIGHT, WIDTH, width)

def window_labels():
    frame_label = region_label(jnp.arange(FRAMES, dtype=jnp.int32), FRAMES, WIN_T, SHIFT_T)
    row_label = region_label(jnp.arange(HEIGHT, dtype=jnp.int32), HEIGHT, SIDE, SHIFT_S)
    column_label = region_label(jnp.arange(WIDTH, dtype=jnp.int32), WIDTH, SIDE, SHIFT_S)
    grid = 9 * frame_label[:, None, None] + 3 * row_label[None, :, None] + column_label[None, None, :]
    return window_cut(grid[..., None]).reshape(-1, WIN).astype(jnp.int32)

def attend_group(query, keys, values, labels, bias):
    raw = low_back(jnp.einsum('gqhd,gkhd->ghqk', query, keys, precision=lax.Precision.HIGHEST))
    mask = jnp.where(labels[:, :, None] == labels[:, None, :], 0.0, mask_value)
    scores = raw * HEAD_DIM ** (-0.5) + bias[None] + mask[:, None]
    top = lax.optimization_barrier(jnp.max(scores, axis=-1, keepdims=True))
    expo = jnp.exp(scores - top)
    probs = expo / lax.optimization_barrier(jnp.sum(expo, axis=-1, keepdims=True))
    mixed = jnp.einsum('ghqk,gkhd->gqhd', low(probs), values, precision=lax.Precision.HIGHEST)
    return low(low_back(mixed))

def layer(clip_x, weights):
    qkv_w, proj_w, fc1_w, fc2_w, vectors, table = weights
    qkv_low = low(qkv_w)
    proj_low = low(proj_w)
    fc1_low = low(fc1_w)
    fc2_low = low(fc2_w)
    rolled = jnp.roll(clip_x, (-SHIFT_T, -SHIFT_S, -SHIFT_S), axis=(0, 1, 2))
    tokens = window_cut(rolled)
    first_low = low(layer_norm(tokens, vectors[0], vectors[1]))
    query = low(low_back(product(first_low, qkv_low[0]) + vectors[2]))
    keys = low(low_back(product(first_low, qkv_low[1])))
    values = low(low_back(product(first_low, qkv_low[2]) + vectors[3]))
    index = relative_index()
    bias = table[index.reshape(-1)].reshape(WIN, WIN, HEADS).transpose(2, 0, 1)
    labels = window_labels()
    groups = query.shape[0] // GRID_W

    def split_heads(array):
        return array.reshape(groups, GRID_W, WIN, HEADS, HEAD_DIM)

    def attend(parts):
        return attend_group(parts[0], parts[1], parts[2], parts[3], bias)
    mixed = lax.map(jax.checkpoint(attend), (split_heads(query), split_heads(keys), split_heads(values), labels.reshape(groups, GRID_W, WIN)))
    mixed = mixed.reshape(-1, WIN, C)
    branch = low_back(product(mixed, proj_low) + vectors[4])
    middle = tokens + branch
    second_low = low(layer_norm(middle, vectors[5], vectors[6]))
    hidden = low_back(product(second_low, fc1_low) + vectors[8:].reshape(-1))
    activated = low(jax.nn.gelu(hidden, approximate=False))
    result = middle + low_back(product(activated, fc2_low) + vectors[7])
    return jnp.roll(window_join(result), (SHIFT_T, SHIFT_S, SHIFT_S), axis=(0, 1, 2))

def untile(array):
    blocks = array.astype(jnp.float32).reshape(CLIPS, GRID_H, GRID_W, FRAMES, SIDE, SIDE, C)
    return blocks.transpose(0, 3, 1, 4, 2, 5, 6).reshape(CLIPS, FRAMES, HEIGHT, WIDTH, C)

def retile(array):
    blocks = array.reshape(CLIPS, FRAMES, GRID_H, SIDE, GRID_W, SIDE, C)
    return blocks.transpose(0, 2, 4, 1, 3, 5, 6).reshape(CLIPS, TILES, FRAMES, SIDE, SIDE, C)

def reference(clips, cotangent, qkv_w, proj_w, fc1_w, fc2_w, qkv_m, proj_m, fc1_m, fc2_m, vectors, vector_m, table, table_m):
    weights = (qkv_w, proj_w, fc1_w, fc2_w, vectors, table)
    empty = jax.tree.map(jnp.zeros_like, weights)

    def visit(carry, pair):
        output, pullback = jax.vjp(layer, pair[0], weights)
        grad_input, grad_weights = pullback(pair[1])
        return (jax.tree.map(jnp.add, carry, grad_weights), (output, grad_input))
    grads, (outputs, input_grads) = lax.scan(visit, empty, (untile(clips), untile(cotangent)))
    grad_qkv, grad_proj, grad_fc1, grad_fc2, grad_vectors, grad_table = grads
    new_qkv_m = momentum_decay * qkv_m + grad_qkv
    new_proj_m = momentum_decay * proj_m + grad_proj
    new_fc1_m = momentum_decay * fc1_m + grad_fc1
    new_fc2_m = momentum_decay * fc2_m + grad_fc2
    new_qkv_w = qkv_w - matrix_rate * jnp.stack([orthogonalize(new_qkv_m[slot]) for slot in range(3)])
    new_proj_w = proj_w - matrix_rate * orthogonalize(new_proj_m)
    new_fc1_w = fc1_w - matrix_rate * orthogonalize(new_fc1_m)
    new_fc2_w = fc2_w - matrix_rate * orthogonalize(new_fc2_m)
    new_vector_m = vector_decay * vector_m + grad_vectors
    new_vectors = vectors - vector_rate * new_vector_m
    new_table_m = vector_decay * table_m + grad_table
    new_table = table - table_rate * new_table_m
    return (retile(outputs).astype(jnp.bfloat16), retile(input_grads).astype(jnp.bfloat16), new_qkv_m, new_proj_m, new_fc1_m, new_fc2_m, new_qkv_w, new_proj_w, new_fc1_w, new_fc2_w, new_vector_m, new_vectors, new_table_m, new_table)
```

```python
import functools
import math

import jax
import jax.numpy as jnp
import numpy as np
from jax import lax
from jax.experimental import pallas as pl
from jax.experimental.pallas import tpu as pltpu
from jax.sharding import PartitionSpec as P

HEADS = 16
WIN_T = 8
SIDE = 7
CELLS = SIDE * SIDE
WINDOW = WIN_T * CELLS
SHIFT_T = 4
SHIFT_S = 3
GRID_W = 2
TABLE = 2535
SPAN_T = 2 * WIN_T - 1
SPAN = 2 * SIDE - 1
ROW = SIDE * WIN_T
WIDE = SPAN * ROW
GROUPS = 4
GROUP_HEADS = HEADS // GROUPS
HALF = 256
SMALL = 256

epsilon_norm = 1e-05
mask_value = -100.0
momentum_decay = 0.95
vector_decay = 0.9
matrix_rate = 1.0
vector_rate = 0.0006
table_rate = 0.03
quintic_first = 3.4445
quintic_second = -4.775
quintic_third = 2.0315
frobenius_epsilon = 1e-07
log2e = 1.4426950408889634
VMEM_LIMIT = 60 * 1024 * 1024
f32 = jnp.float32
bf16 = jnp.bfloat16


def mm(left, right):
    return lax.dot_general(left, right, (((1,), (0,)), ((), ())), preferred_element_type=f32)


def mm_nt(left, right):
    return lax.dot_general(left, right, (((1,), (1,)), ((), ())), preferred_element_type=f32)


def mm_tn(left, right):
    return lax.dot_general(left, right, (((0,), (0,)), ((), ())), preferred_element_type=f32)


def layer_stats(values):
    mean = jnp.mean(values, axis=-1, keepdims=True)
    centred = values - mean
    variance = jnp.mean(centred * centred, axis=-1, keepdims=True)
    inverse = lax.rsqrt(variance + epsilon_norm)
    return (centred * inverse, inverse)


def norm_backward(grad_norm, normed, inverse, gain):
    scaled = grad_norm * gain
    centred = scaled - jnp.mean(scaled, axis=-1, keepdims=True)
    return (centred - normed * jnp.mean(scaled * normed, axis=-1, keepdims=True)) * inverse


def early_slots(shape):
    return lax.broadcasted_iota(jnp.int32, shape, 1) < SHIFT_T


def split_windows(block):
    low, high = block[:, :WIN_T], block[:, WIN_T:]
    early = early_slots(low.shape)
    first = jnp.where(early, high, low)
    second = jnp.where(early, low, high)
    return (first.reshape(WINDOW, -1), second.reshape(WINDOW, -1))


def join_windows(first, second):
    first = first.reshape(CELLS, WIN_T, -1)
    second = second.reshape(CELLS, WIN_T, -1)
    early = early_slots(first.shape)
    low = jnp.where(early, second, first)
    high = jnp.where(early, first, second)
    return jnp.concatenate((low, high), axis=1)


def slot_frames():
    return (np.arange(WIN_T) + SHIFT_T) % WIN_T


def time_pattern():
    frames = slot_frames()
    lane = np.arange(128)
    column, slot = lane // WIN_T, lane % WIN_T
    flat = (frames[None, slot] - frames[:, None] + WIN_T - 1) * SPAN + column[None, :]
    flat = np.where(column[None, :] < SPAN, flat, -1)
    return jnp.asarray((flat.reshape(-1, 1) == np.arange(HALF)).astype(np.float32), dtype=bf16)


def label_features(labels, weights):
    row = lax.broadcasted_iota(jnp.int32, (32, labels.shape[1]), 0)
    value = jnp.zeros(row.shape, f32)
    for k, weight in enumerate(weights):
        value = jnp.where(jnp.logical_and(row // 8 == k, row % 8 == labels), weight, value)
    return value.astype(bf16)


def halves(values):
    high = values.astype(bf16)
    return (high, (values - high.astype(f32)).astype(bf16))


MESH = pl.DeviceIdType.MESH
ANY = pl.BlockSpec(memory_space=pl.ANY)
WHOLE = pl.BlockSpec(memory_space=pltpu.VMEM)


class Spot:
    def __init__(self):
        self.seq = lax.axis_index("seq")
        self.clip = lax.axis_index("clip")
        self.seqs = lax.axis_size("seq")
        self.clips = lax.axis_size("clip")
        self.chips = self.seqs // 2
        self.chip = self.seq // 2
        self.core = self.seq % 2
        self.sibling = (self.seq + 1 - 2 * self.core, self.clip)

    def across(self, step, core=None):
        core = self.core if core is None else core
        return (((self.chip + step + self.chips) % self.chips) * 2 + core, self.clip)

    def along(self, step):
        return (self.seq, (self.clip + step + self.clips) % self.clips)


def send(src, dst, send_sem, recv_sem, to):
    copy = pltpu.make_async_remote_copy(
        src_ref=src, dst_ref=dst, send_sem=send_sem, recv_sem=recv_sem, device_id=to, device_id_type=MESH
    )
    copy.start()
    return copy


def landing(ref, sem, spot):
    return pltpu.make_async_remote_copy(
        src_ref=ref, dst_ref=ref, send_sem=sem, recv_sem=sem, device_id=spot.sibling, device_id_type=MESH
    )


def greet(targets, count):
    barrier = pltpu.get_barrier_semaphore()
    for to in targets:
        pl.semaphore_signal(barrier, inc=1, device_id=to, device_id_type=MESH)
    pl.semaphore_wait(barrier, count)


def greet_all(spot):
    barrier = pltpu.get_barrier_semaphore()

    def tell(step, carry):
        seq = (spot.seq + step % spot.seqs) % spot.seqs
        clip = (spot.clip + step // spot.seqs) % spot.clips
        pl.semaphore_signal(barrier, inc=1, device_id=(seq, clip), device_id_type=MESH)
        return carry

    others = spot.seqs * spot.clips - 1
    lax.fori_loop(1, others + 1, tell, 0)
    pl.semaphore_wait(barrier, others)


EDGE = SIDE - SHIFT_S


def halo_parts(spot, src, dst, send_sems, recv_sems):
    keep, lead = pl.ds(SHIFT_S, EDGE), pl.ds(0, SHIFT_S)
    front, back = pl.ds(0, EDGE), pl.ds(EDGE, SHIFT_S)
    parts = (
        (src.at[keep, lead], dst.at[front, back], spot.sibling),
        (src.at[lead, keep], dst.at[back, front], spot.across(-1)),
        (src.at[lead, lead], dst.at[back, back], spot.across(-1, 1 - spot.core)),
    )
    return [
        pltpu.make_async_remote_copy(
            src_ref=a, dst_ref=b, send_sem=send_sems.at[k], recv_sem=recv_sems.at[k], device_id=to, device_id_type=MESH
        )
        for k, (a, b, to) in enumerate(parts)
    ]


def halo_in(spot, src, dst, send_sems, recv_sems, local_sem):
    copies = halo_parts(spot, src, dst, send_sems, recv_sems)
    copies.append(
        pltpu.make_async_copy(
            src.at[pl.ds(SHIFT_S, EDGE), pl.ds(SHIFT_S, EDGE)], dst.at[pl.ds(0, EDGE), pl.ds(0, EDGE)], local_sem
        )
    )
    for copy in copies:
        copy.start()
    return copies


def halo_back(spot, src, dst, send_sems, recv_sems, local_sem):
    keep, lead = pl.ds(SHIFT_S, EDGE), pl.ds(0, SHIFT_S)
    front, back = pl.ds(0, EDGE), pl.ds(EDGE, SHIFT_S)
    parts = (
        (src.at[front, back], dst.at[keep, lead], spot.sibling),
        (src.at[back, front], dst.at[lead, keep], spot.across(1)),
        (src.at[back, back], dst.at[lead, lead], spot.across(1, 1 - spot.core)),
    )
    copies = [
        pltpu.make_async_remote_copy(
            src_ref=a, dst_ref=b, send_sem=send_sems.at[k], recv_sem=recv_sems.at[k], device_id=to, device_id_type=MESH
        )
        for k, (a, b, to) in enumerate(parts)
    ]
    return copies + [pltpu.make_async_copy(src.at[front, front], dst.at[keep, keep], local_sem)]


def halo_out(spot, src, dst, send_sems, recv_sems, local_sem):
    copies = halo_back(spot, src, dst, send_sems, recv_sems, local_sem)
    for copy in copies:
        copy.start()
    return copies


def owner_of(unit, part, clips, chips):
    low = clips // 2 - 1
    if unit == 0:
        return (part * chips // 2 + 1, low + part % 2)
    return (0 if unit == 1 else 2 * (chips - 1), low + part)


def matrix_at(matrix, half, share, rows):
    if share == 1:
        part = rows // 2
        start = half * part if isinstance(half, int) else pl.multiple_of(half * part, part)
        return (pl.ds(2 * matrix, 2), pl.ds(start, part)), (2, part)
    return (pl.ds((2 * matrix + half) * share, share), pl.ds(0, rows)), (share, rows)


def pieces_of(share, rows):
    return ((0, rows // 2), (rows // 2, rows // 2)) if share == 1 else ((0, rows),)


def front_kernel(
    x_ref, cot_ref, qkv_ref, proj_ref, fc1_ref, fc2_ref, vec_ref, table_ref, pattern_ref,
    probs_ref, inv_ref, qt_ref, kt_ref, vt_ref, mt_ref, middle_ref, h1t_ref, xo_ref, co_ref, pack0_ref, pack12_ref,
    feat_s, bias_s, wide_s, row_s, table_s, x_s, shard_s, pack_s,
    vect_s, halo_send, halo_recv, halo_own, own_sem, send1, recv1, send2, recv2, send3, recv3,
    wide1_send, wide1_recv, wide2_send, wide2_recv, wide3_send, wide3_recv,
):
    group = pl.program_id(0)
    spot = Spot()
    clips, chips, seqs = spot.clips, spot.chips, spot.seqs
    _, _, rows, _ = shard_s.shape
    lanes = mt_ref.shape[1]
    head_dim = lanes // GROUP_HEADS
    scale = head_dim ** (-0.5) * log2e
    width = vec_ref.shape[-1]
    share = seqs // 8

    pieces = pieces_of(share, rows)

    def slot(piece, clip, seq):
        return pack_s.at[clip, seq, pl.ds(*pieces[piece])]

    def first(piece):
        def step(d, carry):
            send(
                shard_s.at[0, spot.seq, pl.ds(*pieces[piece])], slot(piece, spot.clip, spot.seq),
                send1.at[piece, d - 1], recv1.at[piece, d - 1], spot.along(d),
            )
            return carry

        lax.fori_loop(1, clips, step, 0)

    def second(piece):
        def step(d, carry):
            here = slot(piece, (spot.clip - d + clips) % clips, spot.seq)
            landing(here, recv1.at[piece, d - 1], spot).wait_recv()
            for e in range(1, chips):
                send(here, here, send2.at[piece, d - 1, e - 1], recv2.at[piece, d - 1, e - 1], spot.across(e))
            send(here, here, send3.at[piece, d - 1, 0], recv3.at[piece, d - 1, 0], spot.sibling)
            return carry

        lax.fori_loop(1, clips, step, 0)

    def third(piece):
        def step(d, carry):
            clip = (spot.clip - d + clips) % clips
            for e in range(1, chips):
                here = slot(piece, clip, spot.across(-e)[0])
                landing(here, recv2.at[piece, d - 1, e - 1], spot).wait_recv()
                send(here, here, send3.at[piece, d - 1, e], recv3.at[piece, d - 1, e], spot.sibling)
            return carry

        lax.fori_loop(1, clips, step, 0)

    def arrive(piece):
        def step(d, carry):
            for e in range(chips):
                landing(slot(piece, spot.clip, spot.seq), recv3.at[piece, d - 1, e], spot).wait_recv()
            return carry

        lax.fori_loop(1, clips, step, 0)

    def leave(piece):
        def step(d, carry):
            here = slot(piece, spot.clip, spot.seq)
            landing(here, send1.at[piece, d - 1], spot).wait_send()
            for e in range(chips):
                if e > 0:
                    landing(here, send2.at[piece, d - 1, e - 1], spot).wait_send()
                landing(here, send3.at[piece, d - 1, e], spot).wait_send()
            return carry

        lax.fori_loop(1, clips, step, 0)

    line = chips // 2
    parity = (spot.chip % line + spot.chip // line) % 2
    beside = (
        ((spot.chip + 1 - 2 * (spot.chip % 2)) * 2 + spot.core, spot.clip),
        ((spot.chip + line) % chips * 2 + spot.core, spot.clip),
    )

    def cut(part):
        return pl.ds(part * (seqs // 4) + spot.core * share, share)

    def over_clip(unit):
        def step(d, carry):
            for k in range(2):
                span = cut(2 * parity + k)
                send(
                    shard_s.at[unit + 1, span], pack12_ref.at[unit, spot.clip, span],
                    wide1_send.at[unit, d - 1, k], wide1_recv.at[unit, d - 1, k], spot.along(d),
                )
            return carry

        lax.fori_loop(1, clips, step, 0)

    def over_plane(unit):
        def step(d, carry):
            for k in range(2):
                here = pack12_ref.at[unit, (spot.clip - d + clips) % clips, cut(2 * parity + k)]
                landing(here, wide1_recv.at[unit, d - 1, k], spot).wait_recv()
                send(here, here, wide2_send.at[unit, d - 1, k], wide2_recv.at[unit, d - 1, k], beside[k])
                send(here, here, wide3_send.at[unit, d - 1, k], wide3_recv.at[unit, d - 1, k], spot.sibling)
            return carry

        lax.fori_loop(1, clips, step, 0)

    def over_cores(unit):
        def step(d, carry):
            for k in range(2):
                here = pack12_ref.at[unit, (spot.clip - d + clips) % clips, cut(2 * (1 - parity) + k)]
                landing(here, wide2_recv.at[unit, d - 1, k], spot).wait_recv()
                send(here, here, wide3_send.at[unit, d - 1, 2 + k], wide3_recv.at[unit, d - 1, 2 + k], spot.sibling)
            return carry

        lax.fori_loop(1, clips, step, 0)

    def settle(unit):
        def step(d, carry):
            here = pack12_ref.at[unit, spot.clip, cut(0)]
            for k in range(4):
                landing(here, wide3_recv.at[unit, d - 1, k], spot).wait_recv()
                landing(here, wide3_send.at[unit, d - 1, k], spot).wait_send()
                if k < 2:
                    landing(here, wide1_send.at[unit, d - 1, k], spot).wait_send()
                    landing(here, wide2_send.at[unit, d - 1, k], spot).wait_send()
            return carry

        lax.fori_loop(1, clips, step, 0)

    def halo(index):
        src, dst = ((x_ref, x_s), (cot_ref, co_ref))[index]
        return halo_in(spot, src, dst, halo_send.at[index], halo_recv.at[index], halo_own.at[index])

    def own_copy(unit):
        src = (pack_s, shard_s.at[1], shard_s.at[2], x_s)[unit]
        dst = (pack0_ref, pack12_ref.at[0, spot.clip], pack12_ref.at[1, spot.clip], xo_ref)[unit]
        return pltpu.make_async_copy(src, dst, own_sem.at[unit])

    @pl.when(group == 0)
    def _():
        targets = [spot.sibling, spot.across(1, 1 - spot.core)]
        targets += [spot.across(e) for e in range(1, chips)]
        targets += [spot.along(d) for d in range(1, clips)]
        greet(targets, len(targets))
        copies = halo(0)
        vect_s[...] = vec_ref[0:8, :].T.reshape(vect_s.shape)
        for block in range(8):
            half = block % 2
            src = proj_ref if block >= 6 else qkv_ref.at[block // 2]
            piece = src[:, half * HALF : (half + 1) * HALF].astype(bf16)
            at, shape = matrix_at(block // 2, half, share, rows)
            shard_s[(0, *at)] = piece.reshape(*shape, HALF)
        for k in range(len(pieces)):
            first(k)
        pack_s[spot.clip] = shard_s[0]
        for block in range(8):
            piece = fc1_ref[:, block * HALF : (block + 1) * HALF].astype(bf16)
            shard_s[1, block * share : (block + 1) * share] = piece.reshape(share, rows, HALF)
        for half in range(2):
            piece = fc2_ref[:, half * HALF : (half + 1) * HALF].astype(bf16)
            shard_s[2, half * 4 * share : (half + 1) * 4 * share] = piece.reshape(4 * share, rows, HALF)
        own_copy(1).start()
        own_copy(2).start()

        second(0)
        for unit in range(2):
            over_clip(unit)
        table_s[...] = jnp.zeros_like(table_s)
        for time in range(SPAN_T):
            for step in range(SPAN):
                offset = time * SPAN * SPAN + step * SPAN
                table_s[step * HEADS : (step + 1) * HEADS, time * SPAN : (time + 1) * SPAN] = (
                    table_ref[:, offset : offset + SPAN] * log2e
                )
        high, low = halves(table_s[...])
        for key in range(WIN_T):
            part = pattern_ref[key * 128 : (key + 1) * 128, :]
            wide_s[:, key, :] = mm_nt(high, part) + mm_nt(low, part)

        token = lax.broadcasted_iota(jnp.int32, (32, WINDOW), 1)
        edges = (spot.chip == chips - 1).astype(jnp.int32), (spot.core == GRID_W - 1).astype(jnp.int32)
        for w in range(2):
            labels = token_labels(token, w, edges)
            feat_s[w, 0] = label_features(labels, (1.0, 1.0, 1.0))
            feat_s[w, 1] = label_features(labels, mask_parts(head_dim))

        for k in range(1, len(pieces)):
            second(k)
        for copy in copies:
            copy.wait()
        block = x_s[...].reshape(CELLS, 2 * WIN_T, width).astype(f32)
        for w, tokens in enumerate(split_windows(block)):
            middle_ref[w] = tokens + vec_ref[4:5]
            normed, _ = layer_stats(tokens)
            h1t_ref[w] = (normed * vec_ref[0:1] + vec_ref[1:2]).astype(bf16).T
        own_copy(3).start()
        third(0)
        halo(1)
        arrive(0)

    @pl.when(group == 2)
    def _():
        over_plane(1)
        over_cores(0)

    @pl.when(group == 3)
    def _():
        over_cores(1)

    place = pl.ds(pl.multiple_of((group % 2) * lanes, lanes), lanes)
    weights = []
    for m in range(3):
        at, _ = matrix_at(m, group // 2, share, rows)
        weights.append(pack_s[(slice(None), *at, place)].reshape(width, lanes))
    for w in range(2):
        ht = h1t_ref[w]
        qt_ref[w] = (mm_tn(weights[0], ht) + vect_s[group, :, 2:3]).astype(bf16)
        kt_ref[w] = mm_tn(weights[1], ht).astype(bf16)
        vt_ref[w] = (mm_tn(weights[2], ht) + vect_s[group, :, 3:4]).astype(bf16)

    def head_step(head, carry):
        spread = pl.ds(pl.multiple_of(head * head_dim, head_dim), head_dim)
        for step in range(SPAN):
            folded = wide_s[step * HEADS + group * GROUP_HEADS + head]
            rows = [pltpu.roll(folded, (128 - (SIDE - 1 - key) * WIN_T) % 128, 1) for key in range(SIDE)]
            row_s[:, step * ROW : (step + 1) * ROW] = jnp.concatenate(rows, axis=0)[:, :ROW]
        for cell_row in range(SIDE):
            offset = (SIDE - 1 - cell_row) * ROW
            bias_s[cell_row * ROW : (cell_row + 1) * ROW, :] = row_s[:, offset : offset + WINDOW]
        for w in range(2):
            left = jnp.concatenate((kt_ref[w, spread, :], feat_s[w, 0]), axis=0)
            right = jnp.concatenate((qt_ref[w, spread, :], feat_s[w, 1]), axis=0)
            scores = mm_tn(left, right) * scale + bias_s[...]
            top = jnp.max(scores, axis=0, keepdims=True)
            expo = jnp.exp2(scores - top)
            inverse = 1.0 / jnp.sum(expo, axis=0, keepdims=True)
            low = expo.astype(bf16)
            probs_ref[head, w] = low
            inv_ref[head, w] = inverse
            mt_ref[w, spread, :] = (mm(vt_ref[w, spread, :], low) * inverse).astype(bf16)
        return carry

    lax.fori_loop(0, GROUP_HEADS, head_step, 0)

    @pl.when(group == 0)
    def _():
        for k in range(1, len(pieces)):
            third(k)
            arrive(k)
        own_copy(0).start()
        over_plane(0)

    z_group = clips // GROUPS
    for half in range(2):
        at, _ = matrix_at(3, half, share, rows)
        proj = pack_s[(pl.ds(group * z_group, z_group), *at)].reshape(lanes, HALF)
        cols = slice(half * HALF, (half + 1) * HALF)
        for w in range(2):
            middle_ref[w, :, cols] += mm_tn(mt_ref[w], proj)

    @pl.when(group == GROUPS - 1)
    def _():
        for unit in range(2):
            settle(unit)
        for k in range(len(pieces)):
            leave(k)
        for unit in range(4):
            own_copy(unit).wait()
        for copy in halo_parts(spot, cot_ref, co_ref, halo_send.at[1], halo_recv.at[1]):
            copy.wait()
        own = pltpu.make_async_copy(
            cot_ref.at[pl.ds(SHIFT_S, EDGE), pl.ds(SHIFT_S, EDGE)],
            co_ref.at[pl.ds(0, EDGE), pl.ds(0, EDGE)],
            halo_own.at[1],
        )
        own.wait()


def mask_parts(head_dim):
    rest, parts = -mask_value * math.sqrt(head_dim), []
    for _ in range(3):
        parts.append(float(np.float32(rest).astype(jnp.bfloat16)))
        rest -= parts[-1]
    return parts


def token_labels(index, window, edges):
    cell, frame = index // WIN_T, index % WIN_T
    row = sum((cell >= SIDE * k).astype(jnp.int32) for k in range(1, SIDE))
    column = cell - SIDE * row
    label = 2 * edges[0] * (row >= EDGE).astype(jnp.int32) + edges[1] * (column >= EDGE).astype(jnp.int32)
    if window == 1:
        label = label + 4 * (frame < SHIFT_T).astype(jnp.int32)
    return label


def front(tile_in, tile_cot, weights, vectors, table_t, pattern):
    clips, seqs = lax.axis_size("clip"), lax.axis_size("seq")
    chips, share = seqs // 2, seqs // 8
    rows_z = weights[1].shape[0]
    rows = rows_z // share
    count = len(pieces_of(share, rows))
    width = vectors.shape[-1]
    lanes = width // GROUPS
    tokens = (2, width, WINDOW)
    unit = (clips, seqs, rows, HALF)
    group_block = pl.BlockSpec((2, lanes, WINDOW), lambda g: (0, g, 0))
    dma = pltpu.SemaphoreType.DMA

    def const(shape):
        return pl.BlockSpec(shape, lambda g: (0,) * len(shape))

    return pl.pallas_call(
        front_kernel,
        grid=(GROUPS,),
        in_specs=[
            ANY,
            ANY,
            *[const(w.shape) for w in weights],
            const(vectors.shape),
            const(table_t.shape),
            const(pattern.shape),
        ],
        out_specs=[
            pl.BlockSpec((GROUP_HEADS, 2, WINDOW, WINDOW), lambda g: (g, 0, 0, 0)),
            pl.BlockSpec((GROUP_HEADS, 2, 1, WINDOW), lambda g: (g, 0, 0, 0)),
            group_block,
            group_block,
            group_block,
            group_block,
            const((2, WINDOW, width)),
            const(tokens),
            ANY,
            ANY,
            ANY,
            ANY,
        ],
        out_shape=[
            jax.ShapeDtypeStruct((HEADS, 2, WINDOW, WINDOW), bf16),
            jax.ShapeDtypeStruct((HEADS, 2, 1, WINDOW), f32),
            jax.ShapeDtypeStruct(tokens, bf16),
            jax.ShapeDtypeStruct(tokens, bf16),
            jax.ShapeDtypeStruct(tokens, bf16),
            jax.ShapeDtypeStruct(tokens, bf16),
            jax.ShapeDtypeStruct((2, WINDOW, width), f32),
            jax.ShapeDtypeStruct(tokens, bf16),
            jax.ShapeDtypeStruct(tile_in.shape, bf16),
            jax.ShapeDtypeStruct(tile_in.shape, bf16),
            jax.ShapeDtypeStruct(unit, bf16),
            jax.ShapeDtypeStruct((2, *unit), bf16),
        ],
        scratch_shapes=[
            pltpu.VMEM((2, 2, 32, WINDOW), bf16),
            pltpu.VMEM((WINDOW, WINDOW), f32),
            pltpu.VMEM((HEADS * SPAN, WIN_T, 128), f32),
            pltpu.VMEM((ROW, WIDE), f32),
            pltpu.VMEM((HEADS * SPAN, HALF), f32),
            pltpu.VMEM(tile_in.shape, bf16),
            pltpu.VMEM((3, seqs, rows, HALF), bf16),
            pltpu.VMEM(unit, bf16),
            pltpu.VMEM((GROUPS, lanes, 8), f32),
            dma((2, 3)),
            dma((2, 3)),
            dma((2,)),
            dma((4,)),
            dma((count, clips - 1)),
            dma((count, clips - 1)),
            dma((count, clips - 1, chips - 1)),
            dma((count, clips - 1, chips - 1)),
            dma((count, clips - 1, chips)),
            dma((count, clips - 1, chips)),
            *[dma((2, clips - 1, 2))] * 4,
            *[dma((2, clips - 1, 4))] * 2,
        ],
        compiler_params=pltpu.CompilerParams(
            collective_id=0, has_side_effects=True, vmem_limit_bytes=VMEM_LIMIT
        ),
        name="front",
    )(tile_in, tile_cot, *weights, vectors, table_t, pattern)


def core_kernel(
    middle_ref, cot_ref, w1_ref, w2_ref, vec_ref, probs_ref, inv_ref, qt_ref, kt_ref, vt_ref, mt_ref, h1t_ref,
    x_ref, w_ref, p_ref, pattern_ref, qkvm_ref, projm_ref, fc1m_ref, fc2m_ref,
    din_ref, grad_ref, small_ref, early_ref, out_ref, whole_ref, shard_ref,
    whole_s, shard_s, out_s, leave_sem, h2_s, h2t_s, dout_s, acc_s, dh2_s, rows_s, dmid_s, dbr_s, result_s, g1_s, g2_s,
    dot_s, dqkv_s, dh1t_s, dsum_s, wide_acc, wide_s, sums_s,
    near, sums, far, held, line, total_s, moved, mom_s, near0, sums0, far0, held0, line0,
    sa, ra, sb1, rb1, sb2, rb2, sc, rc, sd, rd, se, re, sg, rg, mom_sem,
    sa0, ra0, sb0, rb0, sc0, rc0, halo_send, halo_recv, halo_own,
):
    step = pl.program_id(0)
    group = jnp.maximum(step - GROUPS, 0)
    spot = Spot()
    chips, clips, seqs = spot.chips, spot.clips, spot.seqs
    rows = moved.shape[1]
    share = seqs // 8
    width = vec_ref.shape[-1]
    fresh = (g1_s, g2_s)
    chip_wide, clip_wide = chips // 4, clips // 4
    owners = fc_owners(clips, chips)
    early = share == 1
    chunk = chunk_of(step, chips)


    def chunk_chips(chunk):
        return pl.ds(chunk * chip_wide, chip_wide)

    def chunk_clips(chunk):
        return pl.ds(chunk * clip_wide, clip_wide)

    def near_parts(chunk, core):
        return (
            (g1_s.at[:, chunk_chips(chunk), core], near.at[0, :, chunk_chips(chunk)]),
            (g2_s.at[chunk_clips(chunk), :, core], near.at[1, chunk_clips(chunk)]),
        )

    def send_near(chunk):
        for u, (src, dst) in enumerate(near_parts(chunk, 1 - spot.core)):
            send(src, dst, sa.at[u, chunk], ra.at[u, chunk], spot.sibling)

    def send_far(chunk):
        for u, (_, dst) in enumerate(near_parts(chunk, spot.core)):
            landing(dst, ra.at[u, chunk], spot).wait_recv()
        here = chunk_chips(chunk)
        total = g1_s[:, here, spot.core].astype(f32) + near[0, :, here].astype(f32)
        sums[0, :, here] = total.astype(bf16)
        here = chunk_clips(chunk)
        total = g2_s[here, :, spot.core].astype(f32) + near[1, here].astype(f32)
        sums[1, here] = total.astype(bf16)
        for k in range(chip_wide):
            chip = chunk * chip_wide + k
            ahead = (chip - spot.chip + chips) % chips

            @pl.when(ahead > 0)
            def _():
                to = (2 * chip + spot.core, spot.clip)
                slot = ahead - 1
                send(sums.at[0, :, chip], far.at[0, slot], sb1.at[slot], rb1.at[slot], to)

        for e in range(1, chips):
            to = spot.across(e)
            send(
                sums.at[1, here, to[0] // 2], far.at[1, e - 1, here],
                sb2.at[chunk, e - 1], rb2.at[chunk, e - 1], to,
            )

    def send_line():
        for u in range(2):
            total = sums[u, :, spot.chip].astype(f32)
            for e in range(1, chips):
                if u == 0:
                    landing(far.at[0, e - 1], rb1.at[e - 1], spot).wait_recv()
                else:
                    for chunk in range(GROUPS):
                        here = far.at[1, e - 1, chunk_clips(chunk)]
                        landing(here, rb2.at[chunk, e - 1], spot).wait_recv()
                total += far[u, e - 1].astype(f32)
            held[u] = total.astype(bf16)
            for d in range(1, clips):
                to = spot.along(d)
                send(held.at[u, to[1]], line.at[u, d - 1], sc.at[u, d - 1], rc.at[u, d - 1], to)

    def at_place(place):
        return jnp.logical_and(place[0] == spot.seq, place[1] == spot.clip)

    def hand_over():
        spare = whole_s.at[spot.clip, spot.seq]
        for u in range(2):
            total = held[u, spot.clip].astype(f32)
            for d in range(1, clips):
                landing(line.at[u, d - 1], rc.at[u, d - 1], spot).wait_recv()
                total += line[u, d - 1].astype(f32)
            momentum_copy(u).wait()
            moved[u] = (momentum_decay * mom_s[u] + total).astype(bf16)
            total_s[u] = total.astype(bf16)
            for k, to in enumerate(owners[u]):

                @pl.when(at_place(to))
                def _():
                    pltpu.make_async_copy(moved.at[u], spare, rg.at[u]).start()

                @pl.when(jnp.logical_not(at_place(to)))
                def _():
                    send(moved.at[u], spare, sg.at[u, k], rg.at[u], to)

        for u in range(2):
            here = shard_s.at[u, spot.seq]
            for e in range(1, chips):
                send(total_s.at[u], here, sd.at[u, e - 1], rd.at[u, e - 1], spot.across(e))
            send(total_s.at[u], here, se.at[u, 0], re.at[u, 0], spot.sibling)
            pltpu.make_async_copy(total_s.at[u], here, mom_sem.at[2 + u]).start()

    def momentum_copy(u):
        return momentum_slice((qkvm_ref, projm_ref, fc1m_ref, fc2m_ref), u + 1, spot, rows, mom_s.at[u], mom_sem.at[u])

    def last_exchanges():
        for u in range(2):
            for e in range(1, chips):
                here = shard_s.at[u, spot.across(-e)[0]]
                landing(here, rd.at[u, e - 1], spot).wait_recv()
                send(here, here, se.at[u, e], re.at[u, e], spot.sibling)
        for u in range(2):
            pltpu.make_async_copy(total_s.at[u], shard_s.at[u, spot.seq], mom_sem.at[2 + u]).wait()
            for e in range(chips):
                landing(shard_s.at[u, 0], re.at[u, e], spot).wait_recv()
                landing(shard_s.at[u, 0], se.at[u, e], spot).wait_send()
                if e > 0:
                    landing(shard_s.at[u, 0], sd.at[u, e - 1], spot).wait_send()
                    if u == 0:
                        landing(far.at[0, e - 1], sb1.at[e - 1], spot).wait_send()
            for chunk in range(GROUPS):
                landing(near_parts(chunk, 0)[u][1], sa.at[u, chunk], spot).wait_send()
                if u == 1:
                    for e in range(1, chips):
                        here = far.at[1, e - 1, chunk_clips(chunk)]
                        landing(here, sb2.at[chunk, e - 1], spot).wait_send()
            for d in range(1, clips):
                landing(line.at[u, d - 1], sc.at[u, d - 1], spot).wait_send()
            for k, to in enumerate(owners[u]):

                @pl.when(jnp.logical_not(at_place(to)))
                def _():
                    landing(moved.at[u], sg.at[u, k], spot).wait_send()

                @pl.when(at_place(to))
                def _():
                    landing(whole_s, rg.at[u], spot).wait_recv()

    def outputs():
        return [
            pltpu.make_async_copy(src, dst, leave_sem.at[k])
            for k, (src, dst) in enumerate(((whole_s, whole_ref), (shard_s, shard_ref), (out_s, out_ref)))
        ]


    part = pl.ds(0, rows // 2)

    def early_near():
        send(grad_ref.at[:, :, 1 - spot.core, part], near0, sa0.at[0], ra0.at[0], spot.sibling)

    def early_far():
        landing(near0, ra0.at[0], spot).wait_recv()
        sums0[...] = (grad_ref[:, :, spot.core, part].astype(f32) + near0[...].astype(f32)).astype(bf16)
        for e in range(1, chips):
            to = spot.across(e)
            send(sums0.at[:, to[0] // 2], far0.at[e - 1], sb0.at[e - 1], rb0.at[e - 1], to)

    def early_line():
        total = sums0[:, spot.chip].astype(f32)
        for e in range(1, chips):
            landing(far0.at[e - 1], rb0.at[e - 1], spot).wait_recv()
            total += far0[e - 1].astype(f32)
        held0[...] = total.astype(bf16)
        for d in range(1, clips):
            to = spot.along(d)
            send(held0.at[to[1]], line0.at[d - 1], sc0.at[d - 1], rc0.at[d - 1], to)

    def early_end():
        total = held0[spot.clip].astype(f32)
        for d in range(1, clips):
            landing(line0.at[d - 1], rc0.at[d - 1], spot).wait_recv()
            total += line0[d - 1].astype(f32)
        early_ref[...] = total
        landing(near0, sa0.at[0], spot).wait_send()
        for e in range(1, chips):
            landing(far0.at[e - 1], sb0.at[e - 1], spot).wait_send()
        for d in range(1, clips):
            landing(line0.at[d - 1], sc0.at[d - 1], spot).wait_send()


    @pl.when(step == 0)
    def _():
        greet_all(spot)
        for u in range(2):
            momentum_copy(u).start()
        first, second = split_windows(cot_ref[...].astype(f32))
        whole = jnp.concatenate((first, second), axis=0)
        dout_s[...] = whole.astype(bf16)
        rows_s[7:8, :] = jnp.sum(whole, axis=0, keepdims=True)
        norms = []
        for w in range(2):
            normed, _ = layer_stats(middle_ref[w])
            norms.append(normed * vec_ref[5:6] + vec_ref[6:7])
        low = jnp.concatenate(norms, axis=0).astype(bf16)
        h2_s[...] = low
        h2t_s[...] = low.T
        acc_s[...] = jnp.zeros_like(acc_s)
        dh2_s[...] = jnp.zeros_like(dh2_s)

    def hidden_part(part):
        h2, dout = h2_s[...], dout_s[...]
        cols = slice(part * HALF, (part + 1) * HALF)
        w1 = w1_ref[0, :, part].reshape(width, HALF)
        w2 = [w2_ref[0, :, half].reshape(width, HALF)[cols] for half in range(2)]
        pre = mm(h2, w1) + vec_ref[pl.ds(8 + chunk, 1), cols]
        cdf = 0.5 * (1.0 + lax.erf(pre * 0.7071067811865476))
        act = (pre * cdf).astype(bf16)
        slope = cdf + pre * jnp.exp(-0.5 * pre * pre) * 0.3989422804014327
        d_act = mm_nt(dout[:, :HALF], w2[0]) + mm_nt(dout[:, HALF:], w2[1])
        d_pre = (d_act * slope).astype(bf16)
        rows_s[pl.ds(8 + chunk, 1), cols] = jnp.sum(d_pre.astype(f32), axis=0, keepdims=True)
        for half in range(2):
            acc_s[:, half * HALF : (half + 1) * HALF] += mm(act, w2[half])
        dh2_s[...] += mm_nt(d_pre, w1)
        g1 = mm(h2t_s[...], d_pre).astype(bf16)
        g2 = mm_tn(act, dout).astype(bf16)
        if early:
            g1_s[:, chunk, part] = g1.reshape(clips, rows, HALF)
        else:
            span = pl.ds((2 * chunk + part) * (share // 2), share // 2)
            g1_s[:, span] = g1.reshape(clips, share // 2, 2, rows, HALF)
        for half in range(2):
            piece = g2[:, half * HALF : (half + 1) * HALF]
            if clip_wide == 1:
                first = half * chips // 2 + part * chips // 4
                g2_s[chunk, first : first + chips // 4] = piece.reshape(chips // 4, 2, rows, HALF)
            else:
                planes = pl.ds(chunk * clip_wide + part * (clip_wide // 2), clip_wide // 2)
                span = slice(half * chips // 2, (half + 1) * chips // 2)
                g2_s[planes, span] = piece.reshape(clip_wide // 2, chips // 2, 2, rows, HALF)

    @pl.when(step < GROUPS)
    def _():
        hidden_part(0)

        @pl.when(step > 0)
        def _():
            send_far(chunk_of(step - 1, chips))

        hidden_part(1)
        send_near(chunk)

    @pl.when(step == GROUPS - 1)
    def _():
        results = []
        gain = jnp.zeros((1, width), f32)
        branch = jnp.zeros((1, width), f32)
        for w in range(2):
            span = slice(w * WINDOW, (w + 1) * WINDOW)
            middle = middle_ref[w]
            results.append(middle + acc_s[span, :] + vec_ref[7:8])
            normed, inverse = layer_stats(middle)
            d_second = dh2_s[span, :]
            gain += jnp.sum(d_second * normed, axis=0, keepdims=True)
            dmid_s[w] = norm_backward(d_second, normed, inverse, vec_ref[5:6])
        for w, rows_w in enumerate(split_windows(cot_ref[...].astype(f32))):
            d_middle = dmid_s[w] + rows_w
            dmid_s[w] = d_middle
            low = d_middle.astype(bf16)
            dbr_s[w] = low
            branch += jnp.sum(low.astype(f32), axis=0, keepdims=True)
        result_s[...] = join_windows(*results).astype(bf16).reshape(result_s.shape)
        rows_s[4:5, :] = branch
        rows_s[5:6, :] = gain
        rows_s[6:7, :] = jnp.sum(dh2_s[...], axis=0, keepdims=True)
        send_far(chunk)
        halo_out(spot, result_s, out_s, halo_send, halo_recv, halo_own.at[0])


    lanes = w_ref.shape[-1]
    head_dim = lanes // GROUP_HEADS
    scale = head_dim ** (-0.5)

    def grad_slices(matrix, half):
        if early:
            return (matrix, slice(None), matrix_at(matrix, half, share, rows)[0][1])
        return (pl.ds((2 * matrix + half) * share // 2, share // 2), slice(None), slice(None))

    def grad_shape(cols):
        return (clips, 2, rows // 2, cols) if early else (clips, share // 2, 2, rows, cols)

    @pl.when(step == GROUPS)
    def _():
        dh1t_s[...] = jnp.zeros_like(dh1t_s)
        for half in range(2):
            cols = slice(half * HALF, (half + 1) * HALF)
            grad = mm(mt_ref[0], dbr_s[0, :, cols]) + mm(mt_ref[1], dbr_s[1, :, cols])
            grad_ref[(slice(None), *grad_slices(3, half))] = grad.astype(bf16).reshape(grad_shape(HALF))

    def attention_group():
        place = pl.ds(pl.multiple_of(group * lanes, lanes), lanes)
        for w in range(2):
            branch = dbr_s[w]
            mixed = jnp.zeros((lanes, WINDOW), f32)
            for half in range(2):
                proj = p_ref[:, 0, :, half].reshape(lanes, HALF)
                mixed += mm_nt(proj, branch[:, half * HALF : (half + 1) * HALF])
            dot_s[w] = mixed

        @pl.when(step == GROUPS + 2)
        def _():
            if early:
                early_near()
            send_line()

        @pl.when(step == 2 * GROUPS - 1)
        def _():
            if early:
                early_line()
            hand_over()

        def head_step(head, carry):
            if early:
                pl.when(jnp.logical_and(step == GROUPS + 2, head == 2))(early_far)
            spread = pl.ds(pl.multiple_of(head * head_dim, head_dim), head_dim)
            in_all = pl.ds(pl.multiple_of(group * lanes + head * head_dim, head_dim), head_dim)
            for w in range(2):
                probs = probs_ref[head, w]
                scaled = dot_s[w, spread, :] * inv_ref[head, w]
                d_mixed = scaled.astype(bf16)
                inner = jnp.sum(scaled * mt_ref[w, in_all, :].astype(f32), axis=0, keepdims=True)
                d_probs = mm_tn(vt_ref[w, spread, :], d_mixed)
                d_scores = probs.astype(f32) * (d_probs - inner)
                if w == 0:
                    dsum_s[...] = d_scores
                else:
                    dsum_s[...] += d_scores
                d_raw = d_scores.astype(bf16)
                dqkv_s[w, 0, spread, :] = (mm(kt_ref[w, spread, :], d_raw) * scale).astype(bf16)
                dqkv_s[w, 1, spread, :] = (mm_nt(qt_ref[w, spread, :], d_raw) * scale).astype(bf16)
                dqkv_s[w, 2, spread, :] = mm_nt(d_mixed, probs).astype(bf16)
            wide_acc[...] = jnp.zeros_like(wide_acc)
            for cell_row in range(SIDE):
                offset = (SIDE - 1 - cell_row) * ROW
                wide_acc[:, offset : offset + WINDOW] += dsum_s[cell_row * ROW : (cell_row + 1) * ROW, :]
            for diff in range(SPAN):
                full = jnp.concatenate(
                    (wide_acc[:, diff * ROW : (diff + 1) * ROW], jnp.zeros((ROW, 128 - ROW), f32)), axis=1
                )
                folded = full[ROW - WIN_T :]
                for key in range(SIDE - 1):
                    folded += pltpu.roll(full[key * WIN_T : (key + 1) * WIN_T], (SIDE - 1 - key) * WIN_T, 1)
                wide_s[diff * HEADS + group * GROUP_HEADS + head] = folded
            return carry

        lax.fori_loop(0, GROUP_HEADS, head_step, 0)
        ones = jnp.ones((8, WINDOW), bf16)
        side = pl.ds(pl.multiple_of((group % 2) * lanes, lanes), lanes)
        for m in range(3):
            weights = w_ref[:, m, :, 0].reshape(width, lanes)
            grad = jnp.zeros((width, lanes), f32)
            total = jnp.zeros((8, lanes), f32)
            for w in range(2):
                piece = dqkv_s[w, m]
                dh1t_s[w] += mm(weights, piece)
                grad += mm_nt(h1t_ref[w], piece)
                total += mm_nt(ones, piece)
            grad_ref[(slice(None), *grad_slices(m, group // 2), side)] = grad.astype(bf16).reshape(grad_shape(lanes))
            sums_s[m, :, place] = total

    @pl.when(step >= GROUPS)
    def _():
        attention_group()

    @pl.when(step == 2 * GROUPS - 1)
    def _():
        gain = jnp.zeros((1, width), f32)
        shift = jnp.zeros((1, width), f32)
        grads = []
        for w, tokens in enumerate(split_windows(x_ref[...].astype(f32))):
            normed, inverse = layer_stats(tokens)
            d_first = dh1t_s[w].T
            gain += jnp.sum(d_first * normed, axis=0, keepdims=True)
            shift += jnp.sum(d_first, axis=0, keepdims=True)
            grads.append(dmid_s[w] + norm_backward(d_first, normed, inverse, vec_ref[0:1]))
        din_ref[...] = join_windows(*grads).astype(bf16)
        base = HEADS * SPAN
        lines = {0: gain, 1: shift, 2: sums_s[0, 0:1, :], 3: sums_s[2, 0:1, :]}
        lines.update({v: rows_s[v : v + 1] for v in range(4, vec_ref.shape[0])})
        for v, row in lines.items():
            for half in range(2):
                line_at = base + 2 * v + half
                small_ref[line_at : line_at + 1, :] = row[:, half * HALF : (half + 1) * HALF]
        spare = base + 2 * vec_ref.shape[0]
        small_ref[spare:, :] = jnp.zeros((small_ref.shape[0] - spare, HALF), f32)
        total = jnp.zeros((base, HALF), f32)
        for key in range(WIN_T):
            total += mm(wide_s[:, key, :].astype(bf16), pattern_ref[key * 128 : (key + 1) * 128, :])
        small_ref[:base, :] = total
        for copy in halo_back(spot, result_s, out_s, halo_send, halo_recv, halo_own.at[0]):
            copy.wait()
        outputs()[2].start()
        last_exchanges()
        for copy in outputs()[:2]:
            copy.start()
        if early:
            early_end()
        for copy in outputs():
            copy.wait()


def chunk_of(step, chips):
    first = lax.axis_index("seq") // 2 // (chips // GROUPS) + 1
    return (first + jnp.minimum(step, GROUPS - 1)) % GROUPS


def momentum_slice(refs, unit, spot, rows, dst, sem):
    _, _, first, second = refs
    share, tall = spot.seqs // 8, spot.seqs // 2
    if unit == 1:
        at = pl.ds(pl.multiple_of((spot.seq % share) * rows, rows), rows)
        cols = pl.ds(pl.multiple_of((spot.seq // share) * HALF, HALF), HALF)
        return pltpu.make_async_copy(first.at[at, cols], dst, sem)
    at = pl.ds(pl.multiple_of((spot.seq % tall) * rows, rows), rows)
    cols = pl.ds(pl.multiple_of((spot.seq // tall) * HALF, HALF), HALF)
    return pltpu.make_async_copy(second.at[at, cols], dst, sem)


def fc_owners(clips, chips):
    return [[owner_of(u, k, clips, chips) for k in range(2)] for u in (1, 2)]


def core(saved, middle, x_cells, cot_cells, packed0, packed12, vectors, pattern, momenta):
    probs, inv, qt, kt, vt, mt, h1t = saved
    clips, seqs, rows = packed0.shape[:3]
    chips, share = seqs // 2, seqs // 8
    rows_z = seqs * rows // 8
    width = x_cells.shape[-1]
    lanes = width // GROUPS
    tokens = 2 * WINDOW
    frames = x_cells.shape[1]
    first = packed12.reshape(2, clips, 8, rows_z, HALF)
    second = packed12.reshape(2, clips, 2, 4 * rows_z, HALF)
    early = share == 1
    split = (2, 2, rows // 2) if early else (1, 2, rows_z)
    mats = packed0.reshape(clips, 4, *split, HALF)
    z_step = clips // GROUPS
    unit = (clips, chips, 2, rows, HALF)
    tile = (SIDE, SIDE, frames, width)
    dma = pltpu.SemaphoreType.DMA

    def const(shape):
        return pl.BlockSpec(shape, lambda s: (0,) * len(shape), pipeline_mode=pl.Buffered(1))

    def hidden(s):
        return chunk_of(s, chips)

    def heads(s):
        return jnp.maximum(s - GROUPS, 0)

    group_block = pl.BlockSpec((2, lanes, WINDOW), lambda s: (0, heads(s), 0))
    vmem = pltpu.VMEM
    return pl.pallas_call(
        core_kernel,
        grid=(2 * GROUPS,),
        in_specs=[
            const(middle.shape),
            const(cot_cells.shape),
            pl.BlockSpec((1, clips, 2, rows_z, HALF), lambda s: (0, 0, hidden(s), 0, 0)),
            pl.BlockSpec((1, z_step, 2, 4 * rows_z, HALF), lambda s: (1, hidden(s), 0, 0, 0)),
            const(vectors.shape),
            pl.BlockSpec((GROUP_HEADS, 2, WINDOW, WINDOW), lambda s: (heads(s), 0, 0, 0)),
            pl.BlockSpec((GROUP_HEADS, 2, 1, WINDOW), lambda s: (heads(s), 0, 0, 0)),
            group_block,
            group_block,
            group_block,
            const(mt.shape),
            const(h1t.shape),
            const(x_cells.shape),
            pl.BlockSpec(
                (clips, 3, split[0], 1, split[2], lanes), lambda s: (0, 0, 0, heads(s) // 2, 0, heads(s) % 2)
            ),
            pl.BlockSpec((z_step, 1, *split, HALF), lambda s: (heads(s), 3, 0, 0, 0, 0)),
            const(pattern.shape),
            *[ANY] * 4,
        ],
        out_specs=[
            const(x_cells.shape),
            const(unit),
            const((SMALL, HALF)),
            const((rows // 2, HALF)),
            ANY,
            ANY,
            ANY,
        ],
        out_shape=[
            jax.ShapeDtypeStruct(x_cells.shape, bf16),
            jax.ShapeDtypeStruct(unit, bf16),
            jax.ShapeDtypeStruct((SMALL, HALF), f32),
            jax.ShapeDtypeStruct((rows // 2, HALF), f32),
            jax.ShapeDtypeStruct(tile, bf16),
            jax.ShapeDtypeStruct((clips, seqs, rows, HALF), bf16),
            jax.ShapeDtypeStruct((2, seqs, rows, HALF), bf16),
        ],
        scratch_shapes=[
            vmem((clips, seqs, rows, HALF), bf16),
            vmem((2, seqs, rows, HALF), bf16),
            vmem(tile, bf16),
            dma((3,)),
            vmem((tokens, width), bf16),
            vmem((width, tokens), bf16),
            vmem((tokens, width), bf16),
            vmem((tokens, width), f32),
            vmem((tokens, width), f32),
            vmem((16, width), f32),
            vmem((2, WINDOW, width), f32),
            vmem((2, WINDOW, width), bf16),
            vmem(tile, bf16),
            vmem(unit, bf16),
            vmem(unit, bf16),
            vmem((2, lanes, WINDOW), f32),
            vmem((2, 3, lanes, WINDOW), bf16),
            vmem((2, width, WINDOW), f32),
            vmem((WINDOW, WINDOW), f32),
            vmem((ROW, WIDE), f32),
            vmem((HEADS * SPAN, WIN_T, 128), f32),
            vmem((3, 8, width), f32),
            vmem((2, clips, chips, rows, HALF), bf16),
            vmem((2, clips, chips, rows, HALF), bf16),
            vmem((2, chips - 1, clips, rows, HALF), bf16),
            vmem((2, clips, rows, HALF), bf16),
            vmem((2, clips - 1, rows, HALF), bf16),
            vmem((2, rows, HALF), bf16),
            vmem((2, rows, HALF), bf16),
            vmem((2, rows, HALF), f32),
            vmem((clips, chips, rows // 2, HALF), bf16),
            vmem((clips, chips, rows // 2, HALF), bf16),
            vmem((chips - 1, clips, rows // 2, HALF), bf16),
            vmem((clips, rows // 2, HALF), bf16),
            vmem((clips - 1, rows // 2, HALF), bf16),
            dma((2, GROUPS)),
            dma((2, GROUPS)),
            dma((chips - 1,)),
            dma((chips - 1,)),
            dma((GROUPS, chips - 1)),
            dma((GROUPS, chips - 1)),
            dma((2, clips - 1)),
            dma((2, clips - 1)),
            dma((2, chips - 1)),
            dma((2, chips - 1)),
            dma((2, chips)),
            dma((2, chips)),
            dma((2, 2)),
            dma((2,)),
            dma((4,)),
            dma((1,)),
            dma((1,)),
            dma((chips - 1,)),
            dma((chips - 1,)),
            dma((clips - 1,)),
            dma((clips - 1,)),
            dma((3,)),
            dma((3,)),
            dma((1,)),
        ],
        compiler_params=pltpu.CompilerParams(
            collective_id=1, has_side_effects=True, vmem_limit_bytes=VMEM_LIMIT
        ),
        name="core",
    )(
        middle, cot_cells, first, second, vectors, probs, inv, qt, kt, vt, mt, h1t, x_cells, mats, mats, pattern,
        *momenta,
    )


def product(left, right):
    (lh, ll), (rh, rl) = halves(left), halves(right)
    return mm(lh, rh) + (mm(lh, rl) + mm(ll, rh))


def ortho_square(whole_ref, update_ref, square_s, number):
    clips, seqs, rows = whole_ref.shape[:3]
    size = clips * seqs * rows // 8
    places = [matrix_at(number, half, seqs // 8, rows) for half in range(2)]
    parts = [whole_ref[(slice(None), *at)].reshape(size, HALF) for at, _ in places]
    low = jnp.concatenate(parts, axis=1)
    matrix = low.astype(f32)
    norm = jnp.sqrt(jnp.sum(matrix * matrix)) + frobenius_epsilon
    square_s[...] = matrix / norm
    for sweep in range(5):
        current = square_s[...]
        if sweep < 2:
            brief = current.astype(bf16)
            gram = mm_nt(brief, brief)
            short = gram.astype(bf16)
            poly = quintic_second * gram + quintic_third * mm(short, short)
            square_s[...] = quintic_first * current + mm(poly.astype(bf16), brief)
        else:
            high, low = halves(current)
            cross = mm_nt(high, low)
            gram = mm_nt(high, high) + (cross + cross.T)
            poly = quintic_second * gram + quintic_third * product(gram, gram)
            square_s[...] = quintic_first * current + product(poly, current)
    final = square_s[...].astype(bf16)
    for half, (at, shape) in enumerate(places):
        piece = final[:, half * HALF : (half + 1) * HALF].reshape(clips, *shape, HALF)
        update_ref[(slice(None), *at)] = piece


def gram_start(whole_ref, gram_s, norm_s, wide):
    clips, seqs, rows = whole_ref.shape[:3]
    size = clips * seqs * rows // 8
    gram = jnp.zeros((size, size), f32)
    for block in range(8 if wide else 4):
        piece = (wide_block if wide else tall_block)(whole_ref, block, size)
        gram += mm_nt(piece, piece) if wide else mm_tn(piece, piece)
    norm = jnp.sqrt(jnp.sum(jnp.where(diagonal(size), gram, 0.0))) + frobenius_epsilon
    inverse = 1.0 / norm
    norm_s[...] = jnp.zeros_like(norm_s) + inverse
    gram_s[...] = gram * (inverse * inverse)


def diagonal(size):
    shape = (size, size)
    return lax.broadcasted_iota(jnp.int32, shape, 0) == lax.broadcasted_iota(jnp.int32, shape, 1)


def gram_sweep(gram_s, poly_s, sweep):
    gram = gram_s[...]
    square = quintic_second * gram + quintic_third * product(gram, gram)
    poly = square + jnp.where(diagonal(gram.shape[0]), quintic_first, 0.0)
    poly_s[...] = poly if sweep == 0 else product(poly, poly_s[...])
    if sweep < 4:
        gram = product(poly, product(poly, gram))
        gram_s[...] = 0.5 * (gram + gram.T)


def gram_finish(whole_ref, update_ref, poly_s, norm_s, wide):
    clips, seqs, rows = whole_ref.shape[:3]
    size = clips * seqs * rows // 8
    high, low = halves(poly_s[...])
    inverse = norm_s[0:1, 0:1]
    for block in range(8 if wide else 4):
        if wide:
            piece = wide_block(whole_ref, block, size)
            store_wide(update_ref, block, ((mm(high, piece) + mm(low, piece)) * inverse).astype(bf16))
        else:
            piece = tall_block(whole_ref, block, size)
            done = (mm(piece, high) + mm(piece, low)) * (2.0 * inverse)
            store_tall(update_ref, block, done.astype(bf16))


def wide_block(ref, block, size):
    clips, seqs, rows = ref.shape[:3]
    count = seqs // 8
    return ref[:, block * count : (block + 1) * count].reshape(size, HALF)


def store_wide(ref, block, values):
    clips, seqs, rows = ref.shape[:3]
    count = seqs // 8
    ref[:, block * count : (block + 1) * count] = values.reshape(clips, count, rows, HALF)


def tall_block(ref, block, size):
    clips, seqs, rows = ref.shape[:3]
    span = slice(block * clips // 4, (block + 1) * clips // 4)
    count = seqs // 2
    parts = [ref[span, half * count : (half + 1) * count].reshape(size, HALF) for half in range(2)]
    return jnp.concatenate(parts, axis=1)


def store_tall(ref, block, values):
    clips, seqs, rows = ref.shape[:3]
    span = slice(block * clips // 4, (block + 1) * clips // 4)
    count = seqs // 2
    for half in range(2):
        piece = values[:, half * HALF : (half + 1) * HALF]
        ref[span, half * count : (half + 1) * count] = piece.reshape(clips // 4, count, rows, HALF)


def tail_kernel(
    g0_ref, small_ref, early_ref, wide_ref, qkv_ref, proj_ref, din_ref,
    dout_ref, shard_ref, step_ref, total_ref,
    near0, near1, sums0, sums1, far0, far1, held0, held1, line0, line1,
    moved, mom_s, edge_s, whole_s, update_s, gram_s, poly_s, norm_s,
    sa, ra, sb, rb, sc, rc, sd, rd, se, re, sf, rf, sg, rg, sh, rh, si, ri, sj, rj,
    halo_send, halo_recv, halo_own, mom_sem,
):
    spot = Spot()
    chips, clips, seqs = spot.chips, spot.clips, spot.seqs
    rows = moved.shape[0]
    share, quarter = seqs // 8, seqs // 4
    early = share == 1
    near, sums = (near0, near1), (sums0, sums1)
    far, held, line = (far0, far1), (held0, held1), (line0, line1)

    part = rows // 2 if early else rows
    rest = pl.ds(rows - part, part)
    matrix = spot.seq // (2 * share)
    if early:
        sub = pl.ds(pl.multiple_of(spot.core * part, part), part)
        cuts = [(sub, pl.ds(half * HALF, HALF), pl.ds(half * part, part)) for half in range(2)]
    else:
        sub = pl.ds(pl.multiple_of((spot.seq % share) * rows, rows), rows)
        cuts = [(sub, pl.ds(pl.multiple_of((spot.seq // share % 2) * HALF, HALF), HALF), pl.ds(0, rows))]

    @pl.when(matrix < 3)
    def _():
        for k, (sub, cols, to) in enumerate(cuts):
            pltpu.make_async_copy(qkv_ref.at[matrix, sub, cols], mom_s.at[to], mom_sem.at[k]).start()

    @pl.when(matrix == 3)
    def _():
        for k, (sub, cols, to) in enumerate(cuts):
            pltpu.make_async_copy(proj_ref.at[sub, cols], mom_s.at[to], mom_sem.at[k]).start()

    greet_all(spot)

    def at_place(place):
        return jnp.logical_and(place[0] == spot.seq, place[1] == spot.clip)

    owners = {(u, m): owner_of(u, m, clips, chips) for u in range(3) for m in range(2 if u else 4)}
    taker = owner_of(0, spot.seq // quarter, clips, chips)

    def hand_over(total, k):
        sub, cols, span = cuts[k]
        pltpu.make_async_copy(proj_ref.at[sub, cols], mom_s.at[span], mom_sem.at[k]).wait()
        moved[span] = (momentum_decay * mom_s[span] + total).astype(bf16)
        shard_ref[0, spot.seq, span] = total.astype(bf16)
        spare = whole_s.at[spot.clip, spot.seq, span]

        @pl.when(at_place(taker))
        def _():
            pltpu.make_async_copy(moved.at[span], spare, rg.at[0]).start()

        @pl.when(jnp.logical_not(at_place(taker)))
        def _():
            send(moved.at[span], spare, sg.at[k], rg.at[0], taker)

    def slot(u, seq):
        return total_ref.at[seq] if u == 1 else shard_ref.at[0, seq]

    def spread(u):
        here = slot(u, spot.seq)
        for e in range(1, chips):
            send(here, here, sd.at[u, e - 1], rd.at[u, e - 1], spot.across(e))
        send(here, here, se.at[u, 0], re.at[u, 0], spot.sibling)

    def forward(u):
        for e in range(1, chips):
            here = slot(u, spot.across(-e)[0])
            landing(here, rd.at[u, e - 1], spot).wait_recv()
            send(here, here, se.at[u, e], re.at[u, e], spot.sibling)

    def for_wide_owners(work):
        for u in (1, 2):

            @pl.when(jnp.logical_or(at_place(owners[u, 0]), at_place(owners[u, 1])))
            def _():
                work(u)

    def wide_sweep(sweep):
        mine = [at_place(owners[u, k]) for u in (1, 2) for k in range(2)]

        @pl.when(functools.reduce(jnp.logical_or, mine))
        def _():
            gram_sweep(gram_s, poly_s, sweep)

    def deal(u, number, settle):
        width, planes = (quarter, clips) if u == 0 else (seqs, clips // 2)

        def step(t, carry):
            if u == 0:
                clip, seq = t // width, number * quarter + t % width
            else:
                clip, seq = number * planes + t // width, t % width
            src, dst = update_s.at[clip, seq], step_ref.at[u, seq]
            mine = at_place((seq, clip))
            if settle:

                @pl.when(jnp.logical_not(mine))
                def _():
                    landing(src, sh.at[clip, seq], spot).wait_send()

            else:

                @pl.when(mine)
                def _():
                    pltpu.make_async_copy(src, dst, rh.at[u]).start()

                @pl.when(jnp.logical_not(mine))
                def _():
                    send(src, dst, sh.at[clip, seq], rh.at[u], (seq, clip))

            return carry

        lax.fori_loop(0, planes * width, step, 0)

    send(g0_ref.at[:, :, 1 - spot.core, rest], near0, sa.at[0], ra.at[0], spot.sibling)
    send(small_ref.at[:, :, 1 - spot.core], near1, sa.at[1], ra.at[1], spot.sibling)
    if early:
        hand_over(early_ref[...], 0)

    def plane_send(k):
        landing(near[k], ra.at[k], spot).wait_recv()
        mine = g0_ref[:, :, spot.core, rest] if k == 0 else small_ref[:, :, spot.core]
        total = mine.astype(f32) + near[k][...].astype(f32)
        sums[k][...] = total.astype(sums[k].dtype)
        for e in range(1, chips):
            to = spot.across(e)
            send(sums[k].at[:, to[0] // 2], far[k].at[e - 1], sb.at[k, e - 1], rb.at[k, e - 1], to)

    def line_send(k):
        total = sums[k][:, spot.chip].astype(f32)
        for e in range(1, chips):
            landing(far[k].at[e - 1], rb.at[k, e - 1], spot).wait_recv()
            total += far[k][e - 1].astype(f32)
        held[k][...] = total.astype(held[k].dtype)
        for d in range(1, clips):
            to = spot.along(d)
            send(held[k].at[to[1]], line[k].at[d - 1], sc.at[k, d - 1], rc.at[k, d - 1], to)

    def line_sum(k):
        total = held[k][spot.clip].astype(f32)
        for d in range(1, clips):
            landing(line[k].at[d - 1], rc.at[k, d - 1], spot).wait_recv()
            total += line[k][d - 1].astype(f32)
        return total

    for k in range(2):
        plane_send(k)
    for_wide_owners(lambda u: gram_start(wide_ref, gram_s, norm_s, u == 1))
    wide_sweep(0)
    for k in range(2):
        line_send(k)
    wide_sweep(1)
    copies = halo_out(spot, din_ref, dout_ref, halo_send, halo_recv, halo_own.at[0])
    hand_over(line_sum(0), len(cuts) - 1)
    spread(0)
    edge_s[spot.clip] = line_sum(1)
    for d in range(1, clips):
        here = edge_s.at[spot.clip]
        send(here, here, sf.at[d - 1], rf.at[d - 1], spot.along(d))

    for sweep in range(2, 5):
        wide_sweep(sweep)

    def conclude(u):
        gram_finish(wide_ref, update_s, poly_s, norm_s, u == 1)
        for number in range(2):

            @pl.when(at_place(owners[u, number]))
            def _():
                deal(u, number, False)

    for_wide_owners(conclude)

    @pl.when(functools.reduce(jnp.logical_or, [at_place(owners[0, m]) for m in range(4)]))
    def _():
        number = spot.seq // quarter
        landing(whole_s.at[:, pl.ds(number * quarter, quarter)], rg.at[0], spot).wait_recv()
        ortho_square(whole_s, update_s, gram_s, number)

    for number in range(4):

        @pl.when(at_place(owners[0, number]))
        def _():
            deal(0, number, False)

    for d in range(1, clips):
        landing(edge_s.at[0], rf.at[d - 1], spot).wait_recv()
    total_ref[spot.seq] = edge_s[...]
    spread(1)
    forward(0)
    forward(1)

    order = (1, 2, 0)
    for u in order:
        here = step_ref.at[u, spot.seq]
        landing(here, rh.at[u], spot).wait_recv()
        for e in range(1, chips):
            send(here, here, si.at[u, e - 1], ri.at[u, e - 1], spot.across(e))
        send(here, here, sj.at[u, 0], rj.at[u, 0], spot.sibling)
    for u in order:
        for e in range(1, chips):
            here = step_ref.at[u, spot.across(-e)[0]]
            landing(here, ri.at[u, e - 1], spot).wait_recv()
            send(here, here, sj.at[u, e], rj.at[u, e], spot.sibling)

    for u in range(2):
        for e in range(chips):
            landing(slot(u, 0), re.at[u, e], spot).wait_recv()
            landing(slot(u, 0), se.at[u, e], spot).wait_send()
            if e > 0:
                landing(slot(u, 0), sd.at[u, e - 1], spot).wait_send()

    @pl.when(jnp.logical_not(at_place(taker)))
    def _():
        for k, (_, _, span) in enumerate(cuts):
            landing(moved.at[span], sg.at[k], spot).wait_send()

    for (u, number), place in owners.items():

        @pl.when(at_place(place))
        def _():
            deal(u, number, True)

    for k in range(2):
        landing(near[k], sa.at[k], spot).wait_send()
        for e in range(1, chips):
            landing(far[k].at[e - 1], sb.at[k, e - 1], spot).wait_send()
        for d in range(1, clips):
            landing(line[k].at[d - 1], sc.at[k, d - 1], spot).wait_send()
    for u in range(3):
        for e in range(chips):
            if e > 0:
                landing(step_ref.at[u, 0], si.at[u, e - 1], spot).wait_send()
            landing(step_ref.at[u, 0], sj.at[u, e], spot).wait_send()
            landing(step_ref.at[u, 0], rj.at[u, e], spot).wait_recv()
    for d in range(1, clips):
        landing(edge_s.at[0], sf.at[d - 1], spot).wait_send()
    for copy in copies:
        copy.wait()


def tail(grad, small, early, wide, qkv_m, proj_m, d_input):
    clips, seqs, rows, _ = wide.shape
    chips = seqs // 2
    size = clips * seqs * rows // 8
    small_rows = 8 * clips * seqs
    small = jnp.pad(small, ((0, small_rows - small.shape[0]), (0, 0)))
    cut = [grad, small.reshape(clips, chips, 2, 8, HALF)]
    kinds = [(bf16, rows // 2 if seqs == 8 else rows), (f32, 8)]
    dma = pltpu.SemaphoreType.DMA
    scratch = [pltpu.VMEM((clips, chips, r, HALF), t) for t, r in kinds]
    scratch += [pltpu.VMEM((clips, chips, r, HALF), t) for t, r in kinds]
    scratch += [pltpu.VMEM((chips - 1, clips, r, HALF), t) for t, r in kinds]
    scratch += [pltpu.VMEM((clips, r, HALF), t) for t, r in kinds]
    scratch += [pltpu.VMEM((clips - 1, r, HALF), t) for t, r in kinds]
    scratch += [
        pltpu.VMEM((rows, HALF), bf16),
        pltpu.VMEM((rows, HALF), f32),
        pltpu.VMEM((clips, 8, HALF), f32),
        pltpu.VMEM((clips, seqs, rows, HALF), bf16),
        pltpu.VMEM((clips, seqs, rows, HALF), bf16),
        pltpu.VMEM((size, size), f32),
        pltpu.VMEM((size, size), f32),
        pltpu.VMEM((8, 128), f32),
    ]
    scratch += [dma((2,)), dma((2,))]
    scratch += [dma((2, chips - 1)), dma((2, chips - 1))]
    scratch += [dma((2, clips - 1)), dma((2, clips - 1))]
    scratch += [dma((2, chips - 1)), dma((2, chips - 1))]
    scratch += [dma((2, chips)), dma((2, chips))]
    scratch += [dma((clips - 1,)), dma((clips - 1,))]
    scratch += [dma((2,)), dma((1,))]
    scratch += [dma((clips, seqs)), dma((3,))]
    scratch += [dma((3, chips - 1)), dma((3, chips - 1))]
    scratch += [dma((3, chips)), dma((3, chips))]
    scratch += [dma((3,)), dma((3,)), dma((1,)), dma((2,))]
    return pl.pallas_call(
        tail_kernel,
        in_specs=[WHOLE] * 4 + [ANY] * 2 + [WHOLE],
        out_specs=[WHOLE] * 4,
        out_shape=[
            jax.ShapeDtypeStruct(d_input.shape, bf16),
            jax.ShapeDtypeStruct((1, seqs, rows, HALF), bf16),
            jax.ShapeDtypeStruct((3, seqs, rows, HALF), bf16),
            jax.ShapeDtypeStruct((seqs, clips, 8, HALF), f32),
        ],
        scratch_shapes=scratch,
        compiler_params=pltpu.CompilerParams(
            collective_id=2, has_side_effects=True, vmem_limit_bytes=VMEM_LIMIT
        ),
        name="tail",
    )(*cut, early, wide, qkv_m, proj_m, d_input)


def blocks_of(shard, unit, at=None):
    seqs, rows = shard.shape[1:3]
    count = 2 if unit == 2 else 8
    share = seqs // count
    at = unit if at is None else at
    if unit == 0:
        places = [matrix_at(b // 2, b % 2, share, rows) for b in range(8)]
        return [shard[(at, *place)].reshape(share * rows, HALF) for place, _ in places]
    return [shard[at, b * share : (b + 1) * share].reshape(share * rows, HALF) for b in range(count)]


def places_of(refs):
    qkv, proj, first, second = refs
    cols = [slice(b * HALF, (b + 1) * HALF) for b in range(8)]
    mats = [(qkv, (b // 2, slice(None), cols[b % 2])) for b in range(6)]
    mats += [(proj, (slice(None), cols[b])) for b in range(2)]
    return (
        mats,
        [(first, (slice(None), cols[b])) for b in range(8)],
        [(second, (slice(None), cols[b])) for b in range(2)],
    )


def finish_kernel(
    first_ref, shard_ref, step_ref, *refs,
):
    old_refs, (out_ref, din_ref, total_ref, vec_ref, vecm_ref, table_ref, tablem_ref) = refs[:8], refs[8:15]
    new_refs, (new_out, new_din, new_vecm, new_vec, new_tablem, new_table) = refs[15:23], refs[23:29]
    first_s, shard_s, step_s = refs[29:32]
    old_s, new_s = refs[32:40], refs[40:48]
    tile_s, flat_s, grad_s, in_sem, old_sem, new_sem, tile_sem = refs[48:]
    slices = [
        pltpu.make_async_copy(src, dst, in_sem.at[k])
        for k, (src, dst) in enumerate(((first_ref, first_s), (shard_ref, shard_s), (step_ref, step_s)))
    ]
    loads = [pltpu.make_async_copy(old_refs[k], old_s[k], old_sem.at[k]) for k in range(8)]
    stores = [pltpu.make_async_copy(new_s[k], new_refs[k], new_sem.at[k]) for k in range(8)]
    arrivals = [pltpu.make_async_copy(src, tile_s.at[k], tile_sem.at[k]) for k, src in enumerate((out_ref, din_ref))]
    tiles = [pltpu.make_async_copy(tile_s.at[k], dst, tile_sem.at[2 + k]) for k, dst in enumerate((new_out, new_din))]
    slices[0].start()
    loads[0].start()
    loads[1].start()
    slices[1].start()
    loads[2].start()
    loads[3].start()
    slices[2].start()
    for k in range(4, 8):
        loads[k].start()
    for copy in arrivals:
        copy.start()

    def place_of(unit, refs):
        return places_of(refs)[unit]

    for group in range(2):
        old, new = old_s[4 * group : 4 * group + 4], new_s[4 * group : 4 * group + 4]
        if group == 1:
            slices[2].wait()
        for unit in range(3):
            if group == 0 and unit < 2:
                slices[unit].wait()
            arrays = ((0, 1), (2,), (3,))[unit]
            for k in arrays:
                loads[4 * group + k].wait()
            if group == 1:
                blocks = blocks_of(step_s, unit)
            else:
                blocks = blocks_of(shard_s, unit, unit - 1) if unit else blocks_of(first_s, 0)
            for block, (src, at), (dst, _) in zip(blocks, place_of(unit, old), place_of(unit, new)):
                if group == 0:
                    dst[at] = momentum_decay * src[at] + block.astype(f32)
                else:
                    dst[at] = src[at] - matrix_rate * block.astype(f32)
            for k in arrays:
                stores[4 * group + k].start()

    for arrival, tile in zip(arrivals, tiles):
        arrival.wait()
        tile.start()
    seqs = total_ref.shape[0]
    for q in range(SMALL // 8):
        flat_s[q * 8 : (q + 1) * 8, :] = total_ref[q % seqs, q // seqs]
    base = HEADS * SPAN
    for v in range(vec_ref.shape[0]):
        for half in range(2):
            line_at = base + 2 * v + half
            grad_s[v : v + 1, half * HALF : (half + 1) * HALF] = flat_s[line_at : line_at + 1, :]
    moved = vector_decay * vecm_ref[...] + grad_s[...]
    new_vecm[...] = moved
    new_vec[...] = vec_ref[...] - vector_rate * moved
    for time in range(SPAN_T):
        for step in range(SPAN):
            offset = time * SPAN * SPAN + step * SPAN
            piece = flat_s[step * HEADS : (step + 1) * HEADS, time * SPAN : (time + 1) * SPAN]
            new_tablem[:, offset : offset + SPAN] = piece
    moved = vector_decay * tablem_ref[...] + new_tablem[...]
    new_tablem[...] = moved
    new_table[...] = table_ref[...] - table_rate * moved
    for copy in stores + tiles:
        copy.wait()


def finish(first, shard, step, momenta, weights, tiles, total, vectors, vector_m, table_t, table_mt):
    olds = (*momenta, *weights)
    small = (vector_m, vectors, table_mt, table_t)
    dma = pltpu.SemaphoreType.DMA
    return pl.pallas_call(
        finish_kernel,
        in_specs=[ANY] * 13 + [WHOLE] * 5,
        out_specs=[ANY] * 10 + [WHOLE] * 4,
        out_shape=[jax.ShapeDtypeStruct(a.shape, a.dtype) for a in (*olds, *tiles, *small)],
        scratch_shapes=[
            *[pltpu.VMEM(a.shape, a.dtype) for a in (first, shard, step, *olds, *olds)],
            pltpu.VMEM((2, *tiles[0].shape), bf16),
            pltpu.VMEM((SMALL, HALF), f32),
            pltpu.VMEM(vectors.shape, f32),
            dma((3,)),
            dma((8,)),
            dma((8,)),
            dma((4,)),
        ],
        compiler_params=pltpu.CompilerParams(vmem_limit_bytes=VMEM_LIMIT),
        name="finish",
    )(first, shard, step, *olds, *tiles, total, vectors, vector_m, table_t, table_mt)


def local(
    clips, cotangent, qkv_w, proj_w, fc1_w, fc2_w, qkv_m, proj_m, fc1_m, fc2_m,
    vectors, vector_m, table, table_m,
):
    frames = clips.shape[2]
    width = clips.shape[-1]
    weights = (qkv_w, proj_w, fc1_w, fc2_w)
    momenta = (qkv_m, proj_m, fc1_m, fc2_m)
    tile_in = clips[0, 0].transpose(1, 2, 0, 3)
    tile_cot = cotangent[0, 0].transpose(1, 2, 0, 3)
    pattern = time_pattern()
    probs, inv, qt, kt, vt, mt, middle, h1t, x_tile, cot_tile, packed0, packed12 = front(
        tile_in, tile_cot, weights, vectors, table.T, pattern
    )
    x_cells = x_tile.reshape(CELLS, frames, width)
    cot_cells = cot_tile.reshape(CELLS, frames, width)
    saved = (probs, inv, qt, kt, vt, mt, h1t)
    d_input, g0, small, early, output, wide, shard = core(
        saved, middle, x_cells, cot_cells, packed0, packed12, vectors, pattern, momenta
    )
    input_grad, first, step, total = tail(g0, small, early, wide, qkv_m, proj_m, d_input.reshape(tile_in.shape))
    *rest, output, input_grad, new_vector_m, new_vectors, new_table_m, new_table = finish(
        first, shard, step, momenta, weights, (output, input_grad), total, vectors, vector_m, table.T, table_m.T
    )
    output = output.transpose(2, 0, 1, 3)[None, None]
    input_grad = input_grad.transpose(2, 0, 1, 3)[None, None]
    return (output, input_grad, *rest, new_vector_m, new_vectors, new_table_m.T, new_table.T)


def solution(mesh):
    tile = P("clip", "seq", None, None, None, None)
    stack = P(None, "clip", None)
    rows = P("clip", None)
    weights = (stack, rows, rows, rows)
    return jax.shard_map(
        local,
        mesh=mesh,
        in_specs=(tile, tile, *weights, *weights, P(), P(), P(), P()),
        out_specs=(tile, tile, *weights, *weights, P(), P(), P(), P()),
        check_vma=False,
    )
```

```python
import functools
import math

import jax
import jax.numpy as jnp
import numpy as np
from jax import lax
from jax.experimental import pallas as pl
from jax.experimental.pallas import tpu as pltpu
from jax.sharding import PartitionSpec as P

HEADS = 16
WIN_T = 8
SIDE = 7
CELLS = SIDE * SIDE
WINDOW = WIN_T * CELLS
SHIFT_T = 4
SHIFT_S = 3
GRID_W = 2
TABLE = 2535
SPAN_T = 2 * WIN_T - 1
SPAN = 2 * SIDE - 1
ROW = SIDE * WIN_T
WIDE = SPAN * ROW
GROUPS = 4
GROUP_HEADS = HEADS // GROUPS
HALF = 256
SMALL = 256

epsilon_norm = 1e-05
mask_value = -100.0
momentum_decay = 0.95
vector_decay = 0.9
matrix_rate = 1.0
vector_rate = 0.0006
table_rate = 0.03
quintic_first = 3.4445
quintic_second = -4.775
quintic_third = 2.0315
frobenius_epsilon = 1e-07
log2e = 1.4426950408889634
VMEM_LIMIT = 60 * 1024 * 1024
f32 = jnp.float32
bf16 = jnp.bfloat16


def mm(left, right):
    return lax.dot_general(left, right, (((1,), (0,)), ((), ())), preferred_element_type=f32)


def mm_nt(left, right):
    return lax.dot_general(left, right, (((1,), (1,)), ((), ())), preferred_element_type=f32)


def mm_tn(left, right):
    return lax.dot_general(left, right, (((0,), (0,)), ((), ())), preferred_element_type=f32)


def layer_stats(values):
    mean = jnp.mean(values, axis=-1, keepdims=True)
    centred = values - mean
    variance = jnp.mean(centred * centred, axis=-1, keepdims=True)
    inverse = lax.rsqrt(variance + epsilon_norm)
    return (centred * inverse, inverse)


def norm_backward(grad_norm, normed, inverse, gain):
    scaled = grad_norm * gain
    centred = scaled - jnp.mean(scaled, axis=-1, keepdims=True)
    return (centred - normed * jnp.mean(scaled * normed, axis=-1, keepdims=True)) * inverse


def early_slots(shape):
    return lax.broadcasted_iota(jnp.int32, shape, 1) < SHIFT_T


def split_windows(block):
    low, high = block[:, :WIN_T], block[:, WIN_T:]
    early = early_slots(low.shape)
    first = jnp.where(early, high, low)
    second = jnp.where(early, low, high)
    return (first.reshape(WINDOW, -1), second.reshape(WINDOW, -1))


def join_windows(first, second):
    first = first.reshape(CELLS, WIN_T, -1)
    second = second.reshape(CELLS, WIN_T, -1)
    early = early_slots(first.shape)
    low = jnp.where(early, second, first)
    high = jnp.where(early, first, second)
    return jnp.concatenate((low, high), axis=1)


def slot_frames():
    return (np.arange(WIN_T) + SHIFT_T) % WIN_T


def time_pattern():
    frames = slot_frames()
    lane = np.arange(128)
    column, slot = lane // WIN_T, lane % WIN_T
    flat = (frames[None, slot] - frames[:, None] + WIN_T - 1) * SPAN + column[None, :]
    flat = np.where(column[None, :] < SPAN, flat, -1)
    return jnp.asarray((flat.reshape(-1, 1) == np.arange(HALF)).astype(np.float32), dtype=bf16)


def label_features(labels, weights):
    row = lax.broadcasted_iota(jnp.int32, (32, labels.shape[1]), 0)
    value = jnp.zeros(row.shape, f32)
    for k, weight in enumerate(weights):
        value = jnp.where(jnp.logical_and(row // 8 == k, row % 8 == labels), weight, value)
    return value.astype(bf16)


def halves(values):
    high = values.astype(bf16)
    return (high, (values - high.astype(f32)).astype(bf16))


MESH = pl.DeviceIdType.MESH
ANY = pl.BlockSpec(memory_space=pl.ANY)
WHOLE = pl.BlockSpec(memory_space=pltpu.VMEM)


class Spot:
    def __init__(self):
        self.seq = lax.axis_index("seq")
        self.clip = lax.axis_index("clip")
        self.seqs = lax.axis_size("seq")
        self.clips = lax.axis_size("clip")
        self.chips = self.seqs // 2
        self.chip = self.seq // 2
        self.core = self.seq % 2
        self.sibling = (self.seq + 1 - 2 * self.core, self.clip)

    def across(self, step, core=None):
        core = self.core if core is None else core
        return (((self.chip + step + self.chips) % self.chips) * 2 + core, self.clip)

    def along(self, step):
        return (self.seq, (self.clip + step + self.clips) % self.clips)


def send(src, dst, send_sem, recv_sem, to):
    copy = pltpu.make_async_remote_copy(
        src_ref=src, dst_ref=dst, send_sem=send_sem, recv_sem=recv_sem, device_id=to, device_id_type=MESH
    )
    copy.start()
    return copy


def landing(ref, sem, spot):
    return pltpu.make_async_remote_copy(
        src_ref=ref, dst_ref=ref, send_sem=sem, recv_sem=sem, device_id=spot.sibling, device_id_type=MESH
    )


def greet(targets, count):
    barrier = pltpu.get_barrier_semaphore()
    for to in targets:
        pl.semaphore_signal(barrier, inc=1, device_id=to, device_id_type=MESH)
    pl.semaphore_wait(barrier, count)


def greet_all(spot):
    barrier = pltpu.get_barrier_semaphore()

    def tell(step, carry):
        seq = (spot.seq + step % spot.seqs) % spot.seqs
        clip = (spot.clip + step // spot.seqs) % spot.clips
        pl.semaphore_signal(barrier, inc=1, device_id=(seq, clip), device_id_type=MESH)
        return carry

    others = spot.seqs * spot.clips - 1
    lax.fori_loop(1, others + 1, tell, 0)
    pl.semaphore_wait(barrier, others)


EDGE = SIDE - SHIFT_S


def halo_parts(spot, src, dst, send_sems, recv_sems):
    keep, lead = pl.ds(SHIFT_S, EDGE), pl.ds(0, SHIFT_S)
    front, back = pl.ds(0, EDGE), pl.ds(EDGE, SHIFT_S)
    parts = (
        (src.at[keep, lead], dst.at[front, back], spot.sibling),
        (src.at[lead, keep], dst.at[back, front], spot.across(-1)),
        (src.at[lead, lead], dst.at[back, back], spot.across(-1, 1 - spot.core)),
    )
    return [
        pltpu.make_async_remote_copy(
            src_ref=a, dst_ref=b, send_sem=send_sems.at[k], recv_sem=recv_sems.at[k], device_id=to, device_id_type=MESH
        )
        for k, (a, b, to) in enumerate(parts)
    ]


def halo_in(spot, src, dst, send_sems, recv_sems, local_sem):
    copies = halo_parts(spot, src, dst, send_sems, recv_sems)
    copies.append(
        pltpu.make_async_copy(
            src.at[pl.ds(SHIFT_S, EDGE), pl.ds(SHIFT_S, EDGE)], dst.at[pl.ds(0, EDGE), pl.ds(0, EDGE)], local_sem
        )
    )
    for copy in copies:
        copy.start()
    return copies


def halo_back(spot, src, dst, send_sems, recv_sems, local_sem):
    keep, lead = pl.ds(SHIFT_S, EDGE), pl.ds(0, SHIFT_S)
    front, back = pl.ds(0, EDGE), pl.ds(EDGE, SHIFT_S)
    parts = (
        (src.at[front, back], dst.at[keep, lead], spot.sibling),
        (src.at[back, front], dst.at[lead, keep], spot.across(1)),
        (src.at[back, back], dst.at[lead, lead], spot.across(1, 1 - spot.core)),
    )
    copies = [
        pltpu.make_async_remote_copy(
            src_ref=a, dst_ref=b, send_sem=send_sems.at[k], recv_sem=recv_sems.at[k], device_id=to, device_id_type=MESH
        )
        for k, (a, b, to) in enumerate(parts)
    ]
    return copies + [pltpu.make_async_copy(src.at[front, front], dst.at[keep, keep], local_sem)]


def halo_out(spot, src, dst, send_sems, recv_sems, local_sem):
    copies = halo_back(spot, src, dst, send_sems, recv_sems, local_sem)
    for copy in copies:
        copy.start()
    return copies


def owner_of(unit, part, clips, chips):
    low = clips // 2 - 1
    if unit == 0:
        return (part * chips // 2 + 1, low + part % 2)
    return (0 if unit == 1 else 2 * (chips - 1), low + part)


def matrix_at(matrix, half, share, rows):
    if share == 1:
        part = rows // 2
        start = half * part if isinstance(half, int) else pl.multiple_of(half * part, part)
        return (pl.ds(2 * matrix, 2), pl.ds(start, part)), (2, part)
    return (pl.ds((2 * matrix + half) * share, share), pl.ds(0, rows)), (share, rows)


def pieces_of(share, rows):
    return ((0, rows // 2), (rows // 2, rows // 2)) if share == 1 else ((0, rows),)


def front_kernel(
    x_ref, cot_ref, qkv_ref, proj_ref, fc1_ref, fc2_ref, vec_ref, table_ref, pattern_ref,
    probs_ref, inv_ref, qt_ref, kt_ref, vt_ref, mt_ref, middle_ref, h1t_ref, xo_ref, co_ref, pack0_ref, pack12_ref,
    feat_s, bias_s, wide_s, row_s, table_s, x_s, shard_s, pack_s,
    vect_s, halo_send, halo_recv, halo_own, own_sem, send1, recv1, send2, recv2, send3, recv3,
    wide1_send, wide1_recv, wide2_send, wide2_recv, wide3_send, wide3_recv,
):
    group = pl.program_id(0)
    spot = Spot()
    clips, chips, seqs = spot.clips, spot.chips, spot.seqs
    _, _, rows, _ = shard_s.shape
    lanes = mt_ref.shape[1]
    head_dim = lanes // GROUP_HEADS
    scale = head_dim ** (-0.5) * log2e
    width = vec_ref.shape[-1]
    share = seqs // 8

    pieces = pieces_of(share, rows)

    def slot(piece, clip, seq):
        return pack_s.at[clip, seq, pl.ds(*pieces[piece])]

    def first(piece):
        def step(d, carry):
            send(
                shard_s.at[0, spot.seq, pl.ds(*pieces[piece])], slot(piece, spot.clip, spot.seq),
                send1.at[piece, d - 1], recv1.at[piece, d - 1], spot.along(d),
            )
            return carry

        lax.fori_loop(1, clips, step, 0)

    def second(piece):
        def step(d, carry):
            here = slot(piece, (spot.clip - d + clips) % clips, spot.seq)
            landing(here, recv1.at[piece, d - 1], spot).wait_recv()
            for e in range(1, chips):
                send(here, here, send2.at[piece, d - 1, e - 1], recv2.at[piece, d - 1, e - 1], spot.across(e))
            send(here, here, send3.at[piece, d - 1, 0], recv3.at[piece, d - 1, 0], spot.sibling)
            return carry

        lax.fori_loop(1, clips, step, 0)

    def third(piece):
        def step(d, carry):
            clip = (spot.clip - d + clips) % clips
            for e in range(1, chips):
                here = slot(piece, clip, spot.across(-e)[0])
                landing(here, recv2.at[piece, d - 1, e - 1], spot).wait_recv()
                send(here, here, send3.at[piece, d - 1, e], recv3.at[piece, d - 1, e], spot.sibling)
            return carry

        lax.fori_loop(1, clips, step, 0)

    def arrive(piece):
        def step(d, carry):
            for e in range(chips):
                landing(slot(piece, spot.clip, spot.seq), recv3.at[piece, d - 1, e], spot).wait_recv()
            return carry

        lax.fori_loop(1, clips, step, 0)

    def leave(piece):
        def step(d, carry):
            here = slot(piece, spot.clip, spot.seq)
            landing(here, send1.at[piece, d - 1], spot).wait_send()
            for e in range(chips):
                if e > 0:
                    landing(here, send2.at[piece, d - 1, e - 1], spot).wait_send()
                landing(here, send3.at[piece, d - 1, e], spot).wait_send()
            return carry

        lax.fori_loop(1, clips, step, 0)

    line = chips // 2
    parity = (spot.chip % line + spot.chip // line) % 2
    beside = (
        ((spot.chip + 1 - 2 * (spot.chip % 2)) * 2 + spot.core, spot.clip),
        ((spot.chip + line) % chips * 2 + spot.core, spot.clip),
    )

    def cut(part):
        return pl.ds(part * (seqs // 4) + spot.core * share, share)

    def over_clip(unit):
        def step(d, carry):
            for k in range(2):
                span = cut(2 * parity + k)
                send(
                    shard_s.at[unit + 1, span], pack12_ref.at[unit, spot.clip, span],
                    wide1_send.at[unit, d - 1, k], wide1_recv.at[unit, d - 1, k], spot.along(d),
                )
            return carry

        lax.fori_loop(1, clips, step, 0)

    def over_plane(unit):
        def step(d, carry):
            for k in range(2):
                here = pack12_ref.at[unit, (spot.clip - d + clips) % clips, cut(2 * parity + k)]
                landing(here, wide1_recv.at[unit, d - 1, k], spot).wait_recv()
                send(here, here, wide2_send.at[unit, d - 1, k], wide2_recv.at[unit, d - 1, k], beside[k])
                send(here, here, wide3_send.at[unit, d - 1, k], wide3_recv.at[unit, d - 1, k], spot.sibling)
            return carry

        lax.fori_loop(1, clips, step, 0)

    def over_cores(unit):
        def step(d, carry):
            for k in range(2):
                here = pack12_ref.at[unit, (spot.clip - d + clips) % clips, cut(2 * (1 - parity) + k)]
                landing(here, wide2_recv.at[unit, d - 1, k], spot).wait_recv()
                send(here, here, wide3_send.at[unit, d - 1, 2 + k], wide3_recv.at[unit, d - 1, 2 + k], spot.sibling)
            return carry

        lax.fori_loop(1, clips, step, 0)

    def settle(unit):
        def step(d, carry):
            here = pack12_ref.at[unit, spot.clip, cut(0)]
            for k in range(4):
                landing(here, wide3_recv.at[unit, d - 1, k], spot).wait_recv()
                landing(here, wide3_send.at[unit, d - 1, k], spot).wait_send()
                if k < 2:
                    landing(here, wide1_send.at[unit, d - 1, k], spot).wait_send()
                    landing(here, wide2_send.at[unit, d - 1, k], spot).wait_send()
            return carry

        lax.fori_loop(1, clips, step, 0)

    def halo(index):
        src, dst = ((x_ref, x_s), (cot_ref, co_ref))[index]
        return halo_in(spot, src, dst, halo_send.at[index], halo_recv.at[index], halo_own.at[index])

    def own_copy(unit):
        src = (pack_s, shard_s.at[1], shard_s.at[2], x_s)[unit]
        dst = (pack0_ref, pack12_ref.at[0, spot.clip], pack12_ref.at[1, spot.clip], xo_ref)[unit]
        return pltpu.make_async_copy(src, dst, own_sem.at[unit])

    @pl.when(group == 0)
    def _():
        targets = [spot.sibling, spot.across(1, 1 - spot.core)]
        targets += [spot.across(e) for e in range(1, chips)]
        targets += [spot.along(d) for d in range(1, clips)]
        greet(targets, len(targets))
        copies = halo(0)
        vect_s[...] = vec_ref[0:8, :].T.reshape(vect_s.shape)
        for block in range(8):
            half = block % 2
            src = proj_ref if block >= 6 else qkv_ref.at[block // 2]
            piece = src[:, half * HALF : (half + 1) * HALF].astype(bf16)
            at, shape = matrix_at(block // 2, half, share, rows)
            shard_s[(0, *at)] = piece.reshape(*shape, HALF)
        for k in range(len(pieces)):
            first(k)
        pack_s[spot.clip] = shard_s[0]
        for block in range(8):
            piece = fc1_ref[:, block * HALF : (block + 1) * HALF].astype(bf16)
            shard_s[1, block * share : (block + 1) * share] = piece.reshape(share, rows, HALF)
        for half in range(2):
            piece = fc2_ref[:, half * HALF : (half + 1) * HALF].astype(bf16)
            shard_s[2, half * 4 * share : (half + 1) * 4 * share] = piece.reshape(4 * share, rows, HALF)
        own_copy(1).start()
        own_copy(2).start()

        second(0)
        for unit in range(2):
            over_clip(unit)
        table_s[...] = jnp.zeros_like(table_s)
        for time in range(SPAN_T):
            for step in range(SPAN):
                offset = time * SPAN * SPAN + step * SPAN
                table_s[step * HEADS : (step + 1) * HEADS, time * SPAN : (time + 1) * SPAN] = (
                    table_ref[:, offset : offset + SPAN] * log2e
                )
        high, low = halves(table_s[...])
        for key in range(WIN_T):
            part = pattern_ref[key * 128 : (key + 1) * 128, :]
            wide_s[:, key, :] = mm_nt(high, part) + mm_nt(low, part)

        token = lax.broadcasted_iota(jnp.int32, (32, WINDOW), 1)
        edges = (spot.chip == chips - 1).astype(jnp.int32), (spot.core == GRID_W - 1).astype(jnp.int32)
        for w in range(2):
            labels = token_labels(token, w, edges)
            feat_s[w, 0] = label_features(labels, (1.0, 1.0, 1.0))
            feat_s[w, 1] = label_features(labels, mask_parts(head_dim))

        for k in range(1, len(pieces)):
            second(k)
        for copy in copies:
            copy.wait()
        block = x_s[...].reshape(CELLS, 2 * WIN_T, width).astype(f32)
        for w, tokens in enumerate(split_windows(block)):
            middle_ref[w] = tokens + vec_ref[4:5]
            normed, _ = layer_stats(tokens)
            h1t_ref[w] = (normed * vec_ref[0:1] + vec_ref[1:2]).astype(bf16).T
        own_copy(3).start()
        third(0)
        halo(1)
        arrive(0)

    @pl.when(group == 2)
    def _():
        over_plane(1)
        over_cores(0)

    @pl.when(group == 3)
    def _():
        over_cores(1)

    place = pl.ds(pl.multiple_of((group % 2) * lanes, lanes), lanes)
    weights = []
    for m in range(3):
        at, _ = matrix_at(m, group // 2, share, rows)
        weights.append(pack_s[(slice(None), *at, place)].reshape(width, lanes))
    for w in range(2):
        ht = h1t_ref[w]
        qt_ref[w] = (mm_tn(weights[0], ht) + vect_s[group, :, 2:3]).astype(bf16)
        kt_ref[w] = mm_tn(weights[1], ht).astype(bf16)
        vt_ref[w] = (mm_tn(weights[2], ht) + vect_s[group, :, 3:4]).astype(bf16)

    def head_step(head, carry):
        spread = pl.ds(pl.multiple_of(head * head_dim, head_dim), head_dim)
        for step in range(SPAN):
            folded = wide_s[step * HEADS + group * GROUP_HEADS + head]
            rows = [pltpu.roll(folded, (128 - (SIDE - 1 - key) * WIN_T) % 128, 1) for key in range(SIDE)]
            row_s[:, step * ROW : (step + 1) * ROW] = jnp.concatenate(rows, axis=0)[:, :ROW]
        for cell_row in range(SIDE):
            offset = (SIDE - 1 - cell_row) * ROW
            bias_s[cell_row * ROW : (cell_row + 1) * ROW, :] = row_s[:, offset : offset + WINDOW]
        for w in range(2):
            left = jnp.concatenate((kt_ref[w, spread, :], feat_s[w, 0]), axis=0)
            right = jnp.concatenate((qt_ref[w, spread, :], feat_s[w, 1]), axis=0)
            scores = mm_tn(left, right) * scale + bias_s[...]
            top = jnp.max(scores, axis=0, keepdims=True)
            expo = jnp.exp2(scores - top)
            inverse = 1.0 / jnp.sum(expo, axis=0, keepdims=True)
            low = expo.astype(bf16)
            probs_ref[head, w] = low
            inv_ref[head, w] = inverse
            mt_ref[w, spread, :] = (mm(vt_ref[w, spread, :], low) * inverse).astype(bf16)
        return carry

    lax.fori_loop(0, GROUP_HEADS, head_step, 0)

    @pl.when(group == 0)
    def _():
        for k in range(1, len(pieces)):
            third(k)
            arrive(k)
        own_copy(0).start()
        over_plane(0)

    z_group = clips // GROUPS
    for half in range(2):
        at, _ = matrix_at(3, half, share, rows)
        proj = pack_s[(pl.ds(group * z_group, z_group), *at)].reshape(lanes, HALF)
        cols = slice(half * HALF, (half + 1) * HALF)
        for w in range(2):
            middle_ref[w, :, cols] += mm_tn(mt_ref[w], proj)

    @pl.when(group == GROUPS - 1)
    def _():
        for unit in range(2):
            settle(unit)
        for k in range(len(pieces)):
            leave(k)
        for unit in range(4):
            own_copy(unit).wait()
        for copy in halo_parts(spot, cot_ref, co_ref, halo_send.at[1], halo_recv.at[1]):
            copy.wait()
        own = pltpu.make_async_copy(
            cot_ref.at[pl.ds(SHIFT_S, EDGE), pl.ds(SHIFT_S, EDGE)],
            co_ref.at[pl.ds(0, EDGE), pl.ds(0, EDGE)],
            halo_own.at[1],
        )
        own.wait()


def mask_parts(head_dim):
    rest, parts = -mask_value * math.sqrt(head_dim), []
    for _ in range(3):
        parts.append(float(np.float32(rest).astype(jnp.bfloat16)))
        rest -= parts[-1]
    return parts


def token_labels(index, window, edges):
    cell, frame = index // WIN_T, index % WIN_T
    row = sum((cell >= SIDE * k).astype(jnp.int32) for k in range(1, SIDE))
    column = cell - SIDE * row
    label = 2 * edges[0] * (row >= EDGE).astype(jnp.int32) + edges[1] * (column >= EDGE).astype(jnp.int32)
    if window == 1:
        label = label + 4 * (frame < SHIFT_T).astype(jnp.int32)
    return label


def front(tile_in, tile_cot, weights, vectors, table_t, pattern):
    clips, seqs = lax.axis_size("clip"), lax.axis_size("seq")
    chips, share = seqs // 2, seqs // 8
    rows_z = weights[1].shape[0]
    rows = rows_z // share
    count = len(pieces_of(share, rows))
    width = vectors.shape[-1]
    lanes = width // GROUPS
    tokens = (2, width, WINDOW)
    unit = (clips, seqs, rows, HALF)
    group_block = pl.BlockSpec((2, lanes, WINDOW), lambda g: (0, g, 0))
    dma = pltpu.SemaphoreType.DMA

    def const(shape):
        return pl.BlockSpec(shape, lambda g: (0,) * len(shape))

    return pl.pallas_call(
        front_kernel,
        grid=(GROUPS,),
        in_specs=[
            ANY,
            ANY,
            *[const(w.shape) for w in weights],
            const(vectors.shape),
            const(table_t.shape),
            const(pattern.shape),
        ],
        out_specs=[
            pl.BlockSpec((GROUP_HEADS, 2, WINDOW, WINDOW), lambda g: (g, 0, 0, 0)),
            pl.BlockSpec((GROUP_HEADS, 2, 1, WINDOW), lambda g: (g, 0, 0, 0)),
            group_block,
            group_block,
            group_block,
            group_block,
            const((2, WINDOW, width)),
            const(tokens),
            ANY,
            ANY,
            ANY,
            ANY,
        ],
        out_shape=[
            jax.ShapeDtypeStruct((HEADS, 2, WINDOW, WINDOW), bf16),
            jax.ShapeDtypeStruct((HEADS, 2, 1, WINDOW), f32),
            jax.ShapeDtypeStruct(tokens, bf16),
            jax.ShapeDtypeStruct(tokens, bf16),
            jax.ShapeDtypeStruct(tokens, bf16),
            jax.ShapeDtypeStruct(tokens, bf16),
            jax.ShapeDtypeStruct((2, WINDOW, width), f32),
            jax.ShapeDtypeStruct(tokens, bf16),
            jax.ShapeDtypeStruct(tile_in.shape, bf16),
            jax.ShapeDtypeStruct(tile_in.shape, bf16),
            jax.ShapeDtypeStruct(unit, bf16),
            jax.ShapeDtypeStruct((2, *unit), bf16),
        ],
        scratch_shapes=[
            pltpu.VMEM((2, 2, 32, WINDOW), bf16),
            pltpu.VMEM((WINDOW, WINDOW), f32),
            pltpu.VMEM((HEADS * SPAN, WIN_T, 128), f32),
            pltpu.VMEM((ROW, WIDE), f32),
            pltpu.VMEM((HEADS * SPAN, HALF), f32),
            pltpu.VMEM(tile_in.shape, bf16),
            pltpu.VMEM((3, seqs, rows, HALF), bf16),
            pltpu.VMEM(unit, bf16),
            pltpu.VMEM((GROUPS, lanes, 8), f32),
            dma((2, 3)),
            dma((2, 3)),
            dma((2,)),
            dma((4,)),
            dma((count, clips - 1)),
            dma((count, clips - 1)),
            dma((count, clips - 1, chips - 1)),
            dma((count, clips - 1, chips - 1)),
            dma((count, clips - 1, chips)),
            dma((count, clips - 1, chips)),
            *[dma((2, clips - 1, 2))] * 4,
            *[dma((2, clips - 1, 4))] * 2,
        ],
        compiler_params=pltpu.CompilerParams(
            collective_id=0, has_side_effects=True, vmem_limit_bytes=VMEM_LIMIT
        ),
        name="front",
    )(tile_in, tile_cot, *weights, vectors, table_t, pattern)


def core_kernel(
    middle_ref, cot_ref, w1_ref, w2_ref, vec_ref, probs_ref, inv_ref, qt_ref, kt_ref, vt_ref, mt_ref, h1t_ref,
    x_ref, w_ref, p_ref, pattern_ref, qkvm_ref, projm_ref, fc1m_ref, fc2m_ref,
    din_ref, grad_ref, small_ref, early_ref, out_ref, whole_ref, shard_ref,
    whole_s, shard_s, out_s, leave_sem, h2_s, h2t_s, dout_s, acc_s, dh2_s, rows_s, dmid_s, dbr_s, result_s, g1_s, g2_s,
    dot_s, dqkv_s, dh1t_s, dsum_s, wide_acc, wide_s, sums_s,
    near, sums, far, held, line, total_s, moved, mom_s, near0, sums0, far0, held0, line0,
    sa, ra, sb1, rb1, sb2, rb2, sc, rc, sd, rd, se, re, sg, rg, mom_sem,
    sa0, ra0, sb0, rb0, sc0, rc0, halo_send, halo_recv, halo_own,
):
    step = pl.program_id(0)
    group = jnp.maximum(step - GROUPS, 0)
    spot = Spot()
    chips, clips, seqs = spot.chips, spot.clips, spot.seqs
    rows = moved.shape[1]
    share = seqs // 8
    width = vec_ref.shape[-1]
    fresh = (g1_s, g2_s)
    chip_wide, clip_wide = chips // 4, clips // 4
    owners = fc_owners(clips, chips)
    early = share == 1
    chunk = chunk_of(step, chips)


    def chunk_chips(chunk):
        return pl.ds(chunk * chip_wide, chip_wide)

    def chunk_clips(chunk):
        return pl.ds(chunk * clip_wide, clip_wide)

    def near_parts(chunk, core):
        return (
            (g1_s.at[:, chunk_chips(chunk), core], near.at[0, :, chunk_chips(chunk)]),
            (g2_s.at[chunk_clips(chunk), :, core], near.at[1, chunk_clips(chunk)]),
        )

    def send_near(chunk):
        for u, (src, dst) in enumerate(near_parts(chunk, 1 - spot.core)):
            send(src, dst, sa.at[u, chunk], ra.at[u, chunk], spot.sibling)

    def send_far(chunk):
        for u, (_, dst) in enumerate(near_parts(chunk, spot.core)):
            landing(dst, ra.at[u, chunk], spot).wait_recv()
        here = chunk_chips(chunk)
        total = g1_s[:, here, spot.core].astype(f32) + near[0, :, here].astype(f32)
        sums[0, :, here] = total.astype(bf16)
        here = chunk_clips(chunk)
        total = g2_s[here, :, spot.core].astype(f32) + near[1, here].astype(f32)
        sums[1, here] = total.astype(bf16)
        for k in range(chip_wide):
            chip = chunk * chip_wide + k
            ahead = (chip - spot.chip + chips) % chips

            @pl.when(ahead > 0)
            def _():
                to = (2 * chip + spot.core, spot.clip)
                slot = ahead - 1
                send(sums.at[0, :, chip], far.at[0, slot], sb1.at[slot], rb1.at[slot], to)

        for e in range(1, chips):
            to = spot.across(e)
            send(
                sums.at[1, here, to[0] // 2], far.at[1, e - 1, here],
                sb2.at[chunk, e - 1], rb2.at[chunk, e - 1], to,
            )

    def send_line():
        for u in range(2):
            total = sums[u, :, spot.chip].astype(f32)
            for e in range(1, chips):
                if u == 0:
                    landing(far.at[0, e - 1], rb1.at[e - 1], spot).wait_recv()
                else:
                    for chunk in range(GROUPS):
                        here = far.at[1, e - 1, chunk_clips(chunk)]
                        landing(here, rb2.at[chunk, e - 1], spot).wait_recv()
                total += far[u, e - 1].astype(f32)
            held[u] = total.astype(bf16)
            for d in range(1, clips):
                to = spot.along(d)
                send(held.at[u, to[1]], line.at[u, d - 1], sc.at[u, d - 1], rc.at[u, d - 1], to)

    def at_place(place):
        return jnp.logical_and(place[0] == spot.seq, place[1] == spot.clip)

    def hand_over():
        spare = whole_s.at[spot.clip, spot.seq]
        for u in range(2):
            total = held[u, spot.clip].astype(f32)
            for d in range(1, clips):
                landing(line.at[u, d - 1], rc.at[u, d - 1], spot).wait_recv()
                total += line[u, d - 1].astype(f32)
            momentum_copy(u).wait()
            moved[u] = (momentum_decay * mom_s[u] + total).astype(bf16)
            total_s[u] = total.astype(bf16)
            for k, to in enumerate(owners[u]):

                @pl.when(at_place(to))
                def _():
                    pltpu.make_async_copy(moved.at[u], spare, rg.at[u]).start()

                @pl.when(jnp.logical_not(at_place(to)))
                def _():
                    send(moved.at[u], spare, sg.at[u, k], rg.at[u], to)

        for u in range(2):
            here = shard_s.at[u, spot.seq]
            for e in range(1, chips):
                send(total_s.at[u], here, sd.at[u, e - 1], rd.at[u, e - 1], spot.across(e))
            send(total_s.at[u], here, se.at[u, 0], re.at[u, 0], spot.sibling)
            pltpu.make_async_copy(total_s.at[u], here, mom_sem.at[2 + u]).start()

    def momentum_copy(u):
        return momentum_slice((qkvm_ref, projm_ref, fc1m_ref, fc2m_ref), u + 1, spot, rows, mom_s.at[u], mom_sem.at[u])

    def last_exchanges():
        for u in range(2):
            for e in range(1, chips):
                here = shard_s.at[u, spot.across(-e)[0]]
                landing(here, rd.at[u, e - 1], spot).wait_recv()
                send(here, here, se.at[u, e], re.at[u, e], spot.sibling)
        for u in range(2):
            pltpu.make_async_copy(total_s.at[u], shard_s.at[u, spot.seq], mom_sem.at[2 + u]).wait()
            for e in range(chips):
                landing(shard_s.at[u, 0], re.at[u, e], spot).wait_recv()
                landing(shard_s.at[u, 0], se.at[u, e], spot).wait_send()
                if e > 0:
                    landing(shard_s.at[u, 0], sd.at[u, e - 1], spot).wait_send()
                    if u == 0:
                        landing(far.at[0, e - 1], sb1.at[e - 1], spot).wait_send()
            for chunk in range(GROUPS):
                landing(near_parts(chunk, 0)[u][1], sa.at[u, chunk], spot).wait_send()
                if u == 1:
                    for e in range(1, chips):
                        here = far.at[1, e - 1, chunk_clips(chunk)]
                        landing(here, sb2.at[chunk, e - 1], spot).wait_send()
            for d in range(1, clips):
                landing(line.at[u, d - 1], sc.at[u, d - 1], spot).wait_send()
            for k, to in enumerate(owners[u]):

                @pl.when(jnp.logical_not(at_place(to)))
                def _():
                    landing(moved.at[u], sg.at[u, k], spot).wait_send()

                @pl.when(at_place(to))
                def _():
                    landing(whole_s, rg.at[u], spot).wait_recv()

    def outputs():
        return [
            pltpu.make_async_copy(src, dst, leave_sem.at[k])
            for k, (src, dst) in enumerate(((whole_s, whole_ref), (shard_s, shard_ref), (out_s, out_ref)))
        ]


    part = pl.ds(0, rows // 2)

    def early_near():
        send(grad_ref.at[:, :, 1 - spot.core, part], near0, sa0.at[0], ra0.at[0], spot.sibling)

    def early_far():
        landing(near0, ra0.at[0], spot).wait_recv()
        sums0[...] = (grad_ref[:, :, spot.core, part].astype(f32) + near0[...].astype(f32)).astype(bf16)
        for e in range(1, chips):
            to = spot.across(e)
            send(sums0.at[:, to[0] // 2], far0.at[e - 1], sb0.at[e - 1], rb0.at[e - 1], to)

    def early_line():
        total = sums0[:, spot.chip].astype(f32)
        for e in range(1, chips):
            landing(far0.at[e - 1], rb0.at[e - 1], spot).wait_recv()
            total += far0[e - 1].astype(f32)
        held0[...] = total.astype(bf16)
        for d in range(1, clips):
            to = spot.along(d)
            send(held0.at[to[1]], line0.at[d - 1], sc0.at[d - 1], rc0.at[d - 1], to)

    def early_end():
        total = held0[spot.clip].astype(f32)
        for d in range(1, clips):
            landing(line0.at[d - 1], rc0.at[d - 1], spot).wait_recv()
            total += line0[d - 1].astype(f32)
        early_ref[...] = total
        landing(near0, sa0.at[0], spot).wait_send()
        for e in range(1, chips):
            landing(far0.at[e - 1], sb0.at[e - 1], spot).wait_send()
        for d in range(1, clips):
            landing(line0.at[d - 1], sc0.at[d - 1], spot).wait_send()


    @pl.when(step == 0)
    def _():
        greet_all(spot)
        for u in range(2):
            momentum_copy(u).start()
        first, second = split_windows(cot_ref[...].astype(f32))
        whole = jnp.concatenate((first, second), axis=0)
        dout_s[...] = whole.astype(bf16)
        rows_s[7:8, :] = jnp.sum(whole, axis=0, keepdims=True)
        norms = []
        for w in range(2):
            normed, _ = layer_stats(middle_ref[w])
            norms.append(normed * vec_ref[5:6] + vec_ref[6:7])
        low = jnp.concatenate(norms, axis=0).astype(bf16)
        h2_s[...] = low
        h2t_s[...] = low.T
        acc_s[...] = jnp.zeros_like(acc_s)
        dh2_s[...] = jnp.zeros_like(dh2_s)

    def hidden_part(part):
        h2, dout = h2_s[...], dout_s[...]
        cols = slice(part * HALF, (part + 1) * HALF)
        w1 = w1_ref[0, :, part].reshape(width, HALF)
        w2 = [w2_ref[0, :, half].reshape(width, HALF)[cols] for half in range(2)]
        pre = mm(h2, w1) + vec_ref[pl.ds(8 + chunk, 1), cols]
        cdf = 0.5 * (1.0 + lax.erf(pre * 0.7071067811865476))
        act = (pre * cdf).astype(bf16)
        slope = cdf + pre * jnp.exp(-0.5 * pre * pre) * 0.3989422804014327
        d_act = mm_nt(dout[:, :HALF], w2[0]) + mm_nt(dout[:, HALF:], w2[1])
        d_pre = (d_act * slope).astype(bf16)
        rows_s[pl.ds(8 + chunk, 1), cols] = jnp.sum(d_pre.astype(f32), axis=0, keepdims=True)
        for half in range(2):
            acc_s[:, half * HALF : (half + 1) * HALF] += mm(act, w2[half])
        dh2_s[...] += mm_nt(d_pre, w1)
        g1 = mm(h2t_s[...], d_pre).astype(bf16)
        g2 = mm_tn(act, dout).astype(bf16)
        if early:
            g1_s[:, chunk, part] = g1.reshape(clips, rows, HALF)
        else:
            span = pl.ds((2 * chunk + part) * (share // 2), share // 2)
            g1_s[:, span] = g1.reshape(clips, share // 2, 2, rows, HALF)
        for half in range(2):
            piece = g2[:, half * HALF : (half + 1) * HALF]
            if clip_wide == 1:
                first = half * chips // 2 + part * chips // 4
                g2_s[chunk, first : first + chips // 4] = piece.reshape(chips // 4, 2, rows, HALF)
            else:
                planes = pl.ds(chunk * clip_wide + part * (clip_wide // 2), clip_wide // 2)
                span = slice(half * chips // 2, (half + 1) * chips // 2)
                g2_s[planes, span] = piece.reshape(clip_wide // 2, chips // 2, 2, rows, HALF)

    @pl.when(step < GROUPS)
    def _():
        hidden_part(0)

        @pl.when(step > 0)
        def _():
            send_far(chunk_of(step - 1, chips))

        hidden_part(1)
        send_near(chunk)

    @pl.when(step == GROUPS - 1)
    def _():
        results = []
        gain = jnp.zeros((1, width), f32)
        branch = jnp.zeros((1, width), f32)
        for w in range(2):
            span = slice(w * WINDOW, (w + 1) * WINDOW)
            middle = middle_ref[w]
            results.append(middle + acc_s[span, :] + vec_ref[7:8])
            normed, inverse = layer_stats(middle)
            d_second = dh2_s[span, :]
            gain += jnp.sum(d_second * normed, axis=0, keepdims=True)
            dmid_s[w] = norm_backward(d_second, normed, inverse, vec_ref[5:6])
        for w, rows_w in enumerate(split_windows(cot_ref[...].astype(f32))):
            d_middle = dmid_s[w] + rows_w
            dmid_s[w] = d_middle
            low = d_middle.astype(bf16)
            dbr_s[w] = low
            branch += jnp.sum(low.astype(f32), axis=0, keepdims=True)
        result_s[...] = join_windows(*results).astype(bf16).reshape(result_s.shape)
        rows_s[4:5, :] = branch
        rows_s[5:6, :] = gain
        rows_s[6:7, :] = jnp.sum(dh2_s[...], axis=0, keepdims=True)
        send_far(chunk)


    lanes = w_ref.shape[-1]
    head_dim = lanes // GROUP_HEADS
    scale = head_dim ** (-0.5)

    def grad_slices(matrix, half):
        if early:
            return (matrix, slice(None), matrix_at(matrix, half, share, rows)[0][1])
        return (pl.ds((2 * matrix + half) * share // 2, share // 2), slice(None), slice(None))

    def grad_shape(cols):
        return (clips, 2, rows // 2, cols) if early else (clips, share // 2, 2, rows, cols)

    @pl.when(step == GROUPS)
    def _():
        dh1t_s[...] = jnp.zeros_like(dh1t_s)
        for half in range(2):
            cols = slice(half * HALF, (half + 1) * HALF)
            grad = mm(mt_ref[0], dbr_s[0, :, cols]) + mm(mt_ref[1], dbr_s[1, :, cols])
            grad_ref[(slice(None), *grad_slices(3, half))] = grad.astype(bf16).reshape(grad_shape(HALF))

    def attention_group():
        place = pl.ds(pl.multiple_of(group * lanes, lanes), lanes)
        for w in range(2):
            branch = dbr_s[w]
            mixed = jnp.zeros((lanes, WINDOW), f32)
            for half in range(2):
                proj = p_ref[:, 0, :, half].reshape(lanes, HALF)
                mixed += mm_nt(proj, branch[:, half * HALF : (half + 1) * HALF])
            dot_s[w] = mixed

        @pl.when(step == GROUPS + 2)
        def _():
            if early:
                early_near()

        @pl.when(step == 2 * GROUPS - 1)
        def _():
            if early:
                early_line()
            hand_over()

        def head_step(head, carry):
            if early:
                pl.when(jnp.logical_and(step == GROUPS + 2, head == 2))(early_far)

            @pl.when(jnp.logical_and(step == GROUPS + 1, head == 2))
            def _():
                send_line()
                halo_out(spot, result_s, out_s, halo_send, halo_recv, halo_own.at[0])

            spread = pl.ds(pl.multiple_of(head * head_dim, head_dim), head_dim)
            in_all = pl.ds(pl.multiple_of(group * lanes + head * head_dim, head_dim), head_dim)
            for w in range(2):
                probs = probs_ref[head, w]
                scaled = dot_s[w, spread, :] * inv_ref[head, w]
                d_mixed = scaled.astype(bf16)
                inner = jnp.sum(scaled * mt_ref[w, in_all, :].astype(f32), axis=0, keepdims=True)
                d_probs = mm_tn(vt_ref[w, spread, :], d_mixed)
                d_scores = probs.astype(f32) * (d_probs - inner)
                if w == 0:
                    dsum_s[...] = d_scores
                else:
                    dsum_s[...] += d_scores
                d_raw = d_scores.astype(bf16)
                dqkv_s[w, 0, spread, :] = (mm(kt_ref[w, spread, :], d_raw) * scale).astype(bf16)
                dqkv_s[w, 1, spread, :] = (mm_nt(qt_ref[w, spread, :], d_raw) * scale).astype(bf16)
                dqkv_s[w, 2, spread, :] = mm_nt(d_mixed, probs).astype(bf16)
            wide_acc[...] = jnp.zeros_like(wide_acc)
            for cell_row in range(SIDE):
                offset = (SIDE - 1 - cell_row) * ROW
                wide_acc[:, offset : offset + WINDOW] += dsum_s[cell_row * ROW : (cell_row + 1) * ROW, :]
            for diff in range(SPAN):
                full = jnp.concatenate(
                    (wide_acc[:, diff * ROW : (diff + 1) * ROW], jnp.zeros((ROW, 128 - ROW), f32)), axis=1
                )
                folded = full[ROW - WIN_T :]
                for key in range(SIDE - 1):
                    folded += pltpu.roll(full[key * WIN_T : (key + 1) * WIN_T], (SIDE - 1 - key) * WIN_T, 1)
                wide_s[diff * HEADS + group * GROUP_HEADS + head] = folded
            return carry

        lax.fori_loop(0, GROUP_HEADS, head_step, 0)
        ones = jnp.ones((8, WINDOW), bf16)
        side = pl.ds(pl.multiple_of((group % 2) * lanes, lanes), lanes)
        for m in range(3):
            weights = w_ref[:, m, :, 0].reshape(width, lanes)
            grad = jnp.zeros((width, lanes), f32)
            total = jnp.zeros((8, lanes), f32)
            for w in range(2):
                piece = dqkv_s[w, m]
                dh1t_s[w] += mm(weights, piece)
                grad += mm_nt(h1t_ref[w], piece)
                total += mm_nt(ones, piece)
            grad_ref[(slice(None), *grad_slices(m, group // 2), side)] = grad.astype(bf16).reshape(grad_shape(lanes))
            sums_s[m, :, place] = total

    @pl.when(step >= GROUPS)
    def _():
        attention_group()

    @pl.when(step == 2 * GROUPS - 1)
    def _():
        gain = jnp.zeros((1, width), f32)
        shift = jnp.zeros((1, width), f32)
        grads = []
        for w, tokens in enumerate(split_windows(x_ref[...].astype(f32))):
            normed, inverse = layer_stats(tokens)
            d_first = dh1t_s[w].T
            gain += jnp.sum(d_first * normed, axis=0, keepdims=True)
            shift += jnp.sum(d_first, axis=0, keepdims=True)
            grads.append(dmid_s[w] + norm_backward(d_first, normed, inverse, vec_ref[0:1]))
        din_ref[...] = join_windows(*grads).astype(bf16)
        base = HEADS * SPAN
        lines = {0: gain, 1: shift, 2: sums_s[0, 0:1, :], 3: sums_s[2, 0:1, :]}
        lines.update({v: rows_s[v : v + 1] for v in range(4, vec_ref.shape[0])})
        for v, row in lines.items():
            for half in range(2):
                line_at = base + 2 * v + half
                small_ref[line_at : line_at + 1, :] = row[:, half * HALF : (half + 1) * HALF]
        spare = base + 2 * vec_ref.shape[0]
        small_ref[spare:, :] = jnp.zeros((small_ref.shape[0] - spare, HALF), f32)
        total = jnp.zeros((base, HALF), f32)
        for key in range(WIN_T):
            total += mm(wide_s[:, key, :].astype(bf16), pattern_ref[key * 128 : (key + 1) * 128, :])
        small_ref[:base, :] = total
        for copy in halo_back(spot, result_s, out_s, halo_send, halo_recv, halo_own.at[0]):
            copy.wait()
        outputs()[2].start()
        last_exchanges()
        for copy in outputs()[:2]:
            copy.start()
        if early:
            early_end()
        for copy in outputs():
            copy.wait()


def chunk_of(step, chips):
    first = lax.axis_index("seq") // 2 // (chips // GROUPS) + 1
    return (first + jnp.minimum(step, GROUPS - 1)) % GROUPS


def momentum_slice(refs, unit, spot, rows, dst, sem):
    _, _, first, second = refs
    share, tall = spot.seqs // 8, spot.seqs // 2
    if unit == 1:
        at = pl.ds(pl.multiple_of((spot.seq % share) * rows, rows), rows)
        cols = pl.ds(pl.multiple_of((spot.seq // share) * HALF, HALF), HALF)
        return pltpu.make_async_copy(first.at[at, cols], dst, sem)
    at = pl.ds(pl.multiple_of((spot.seq % tall) * rows, rows), rows)
    cols = pl.ds(pl.multiple_of((spot.seq // tall) * HALF, HALF), HALF)
    return pltpu.make_async_copy(second.at[at, cols], dst, sem)


def fc_owners(clips, chips):
    return [[owner_of(u, k, clips, chips) for k in range(2)] for u in (1, 2)]


def core(saved, middle, x_cells, cot_cells, packed0, packed12, vectors, pattern, momenta):
    probs, inv, qt, kt, vt, mt, h1t = saved
    clips, seqs, rows = packed0.shape[:3]
    chips, share = seqs // 2, seqs // 8
    rows_z = seqs * rows // 8
    width = x_cells.shape[-1]
    lanes = width // GROUPS
    tokens = 2 * WINDOW
    frames = x_cells.shape[1]
    first = packed12.reshape(2, clips, 8, rows_z, HALF)
    second = packed12.reshape(2, clips, 2, 4 * rows_z, HALF)
    early = share == 1
    split = (2, 2, rows // 2) if early else (1, 2, rows_z)
    mats = packed0.reshape(clips, 4, *split, HALF)
    z_step = clips // GROUPS
    unit = (clips, chips, 2, rows, HALF)
    tile = (SIDE, SIDE, frames, width)
    dma = pltpu.SemaphoreType.DMA

    def const(shape):
        return pl.BlockSpec(shape, lambda s: (0,) * len(shape), pipeline_mode=pl.Buffered(1))

    def hidden(s):
        return chunk_of(s, chips)

    def heads(s):
        return jnp.maximum(s - GROUPS, 0)

    group_block = pl.BlockSpec((2, lanes, WINDOW), lambda s: (0, heads(s), 0))
    vmem = pltpu.VMEM
    return pl.pallas_call(
        core_kernel,
        grid=(2 * GROUPS,),
        in_specs=[
            const(middle.shape),
            const(cot_cells.shape),
            pl.BlockSpec((1, clips, 2, rows_z, HALF), lambda s: (0, 0, hidden(s), 0, 0)),
            pl.BlockSpec((1, z_step, 2, 4 * rows_z, HALF), lambda s: (1, hidden(s), 0, 0, 0)),
            const(vectors.shape),
            pl.BlockSpec((GROUP_HEADS, 2, WINDOW, WINDOW), lambda s: (heads(s), 0, 0, 0)),
            pl.BlockSpec((GROUP_HEADS, 2, 1, WINDOW), lambda s: (heads(s), 0, 0, 0)),
            group_block,
            group_block,
            group_block,
            const(mt.shape),
            const(h1t.shape),
            const(x_cells.shape),
            pl.BlockSpec(
                (clips, 3, split[0], 1, split[2], lanes), lambda s: (0, 0, 0, heads(s) // 2, 0, heads(s) % 2)
            ),
            pl.BlockSpec((z_step, 1, *split, HALF), lambda s: (heads(s), 3, 0, 0, 0, 0)),
            const(pattern.shape),
            *[ANY] * 4,
        ],
        out_specs=[
            const(x_cells.shape),
            const(unit),
            const((SMALL, HALF)),
            const((rows // 2, HALF)),
            ANY,
            ANY,
            ANY,
        ],
        out_shape=[
            jax.ShapeDtypeStruct(x_cells.shape, bf16),
            jax.ShapeDtypeStruct(unit, bf16),
            jax.ShapeDtypeStruct((SMALL, HALF), f32),
            jax.ShapeDtypeStruct((rows // 2, HALF), f32),
            jax.ShapeDtypeStruct(tile, bf16),
            jax.ShapeDtypeStruct((clips, seqs, rows, HALF), bf16),
            jax.ShapeDtypeStruct((2, seqs, rows, HALF), bf16),
        ],
        scratch_shapes=[
            vmem((clips, seqs, rows, HALF), bf16),
            vmem((2, seqs, rows, HALF), bf16),
            vmem(tile, bf16),
            dma((3,)),
            vmem((tokens, width), bf16),
            vmem((width, tokens), bf16),
            vmem((tokens, width), bf16),
            vmem((tokens, width), f32),
            vmem((tokens, width), f32),
            vmem((16, width), f32),
            vmem((2, WINDOW, width), f32),
            vmem((2, WINDOW, width), bf16),
            vmem(tile, bf16),
            vmem(unit, bf16),
            vmem(unit, bf16),
            vmem((2, lanes, WINDOW), f32),
            vmem((2, 3, lanes, WINDOW), bf16),
            vmem((2, width, WINDOW), f32),
            vmem((WINDOW, WINDOW), f32),
            vmem((ROW, WIDE), f32),
            vmem((HEADS * SPAN, WIN_T, 128), f32),
            vmem((3, 8, width), f32),
            vmem((2, clips, chips, rows, HALF), bf16),
            vmem((2, clips, chips, rows, HALF), bf16),
            vmem((2, chips - 1, clips, rows, HALF), bf16),
            vmem((2, clips, rows, HALF), bf16),
            vmem((2, clips - 1, rows, HALF), bf16),
            vmem((2, rows, HALF), bf16),
            vmem((2, rows, HALF), bf16),
            vmem((2, rows, HALF), f32),
            vmem((clips, chips, rows // 2, HALF), bf16),
            vmem((clips, chips, rows // 2, HALF), bf16),
            vmem((chips - 1, clips, rows // 2, HALF), bf16),
            vmem((clips, rows // 2, HALF), bf16),
            vmem((clips - 1, rows // 2, HALF), bf16),
            dma((2, GROUPS)),
            dma((2, GROUPS)),
            dma((chips - 1,)),
            dma((chips - 1,)),
            dma((GROUPS, chips - 1)),
            dma((GROUPS, chips - 1)),
            dma((2, clips - 1)),
            dma((2, clips - 1)),
            dma((2, chips - 1)),
            dma((2, chips - 1)),
            dma((2, chips)),
            dma((2, chips)),
            dma((2, 2)),
            dma((2,)),
            dma((4,)),
            dma((1,)),
            dma((1,)),
            dma((chips - 1,)),
            dma((chips - 1,)),
            dma((clips - 1,)),
            dma((clips - 1,)),
            dma((3,)),
            dma((3,)),
            dma((1,)),
        ],
        compiler_params=pltpu.CompilerParams(
            collective_id=1, has_side_effects=True, vmem_limit_bytes=VMEM_LIMIT
        ),
        name="core",
    )(
        middle, cot_cells, first, second, vectors, probs, inv, qt, kt, vt, mt, h1t, x_cells, mats, mats, pattern,
        *momenta,
    )


def product(left, right):
    (lh, ll), (rh, rl) = halves(left), halves(right)
    return mm(lh, rh) + (mm(lh, rl) + mm(ll, rh))


def ortho_square(whole_ref, update_ref, square_s, number):
    clips, seqs, rows = whole_ref.shape[:3]
    size = clips * seqs * rows // 8
    places = [matrix_at(number, half, seqs // 8, rows) for half in range(2)]
    parts = [whole_ref[(slice(None), *at)].reshape(size, HALF) for at, _ in places]
    low = jnp.concatenate(parts, axis=1)
    matrix = low.astype(f32)
    norm = jnp.sqrt(jnp.sum(matrix * matrix)) + frobenius_epsilon
    square_s[...] = matrix / norm
    for sweep in range(5):
        current = square_s[...]
        if sweep < 2:
            brief = current.astype(bf16)
            gram = mm_nt(brief, brief)
            short = gram.astype(bf16)
            poly = quintic_second * gram + quintic_third * mm(short, short)
            square_s[...] = quintic_first * current + mm(poly.astype(bf16), brief)
        else:
            high, low = halves(current)
            cross = mm_nt(high, low)
            gram = mm_nt(high, high) + (cross + cross.T)
            poly = quintic_second * gram + quintic_third * product(gram, gram)
            square_s[...] = quintic_first * current + product(poly, current)
    final = square_s[...].astype(bf16)
    for half, (at, shape) in enumerate(places):
        piece = final[:, half * HALF : (half + 1) * HALF].reshape(clips, *shape, HALF)
        update_ref[(slice(None), *at)] = piece


def gram_start(whole_ref, gram_s, norm_s, wide):
    clips, seqs, rows = whole_ref.shape[:3]
    size = clips * seqs * rows // 8
    gram = jnp.zeros((size, size), f32)
    for block in range(8 if wide else 4):
        piece = (wide_block if wide else tall_block)(whole_ref, block, size)
        gram += mm_nt(piece, piece) if wide else mm_tn(piece, piece)
    norm = jnp.sqrt(jnp.sum(jnp.where(diagonal(size), gram, 0.0))) + frobenius_epsilon
    inverse = 1.0 / norm
    norm_s[...] = jnp.zeros_like(norm_s) + inverse
    gram_s[...] = gram * (inverse * inverse)


def diagonal(size):
    shape = (size, size)
    return lax.broadcasted_iota(jnp.int32, shape, 0) == lax.broadcasted_iota(jnp.int32, shape, 1)


def gram_sweep(gram_s, poly_s, sweep):
    gram = gram_s[...]
    square = quintic_second * gram + quintic_third * product(gram, gram)
    poly = square + jnp.where(diagonal(gram.shape[0]), quintic_first, 0.0)
    poly_s[...] = poly if sweep == 0 else product(poly, poly_s[...])
    if sweep < 4:
        gram = product(poly, product(poly, gram))
        gram_s[...] = 0.5 * (gram + gram.T)


def gram_finish(whole_ref, update_ref, poly_s, norm_s, wide):
    clips, seqs, rows = whole_ref.shape[:3]
    size = clips * seqs * rows // 8
    high, low = halves(poly_s[...])
    inverse = norm_s[0:1, 0:1]
    for block in range(8 if wide else 4):
        if wide:
            piece = wide_block(whole_ref, block, size)
            store_wide(update_ref, block, ((mm(high, piece) + mm(low, piece)) * inverse).astype(bf16))
        else:
            piece = tall_block(whole_ref, block, size)
            done = (mm(piece, high) + mm(piece, low)) * (2.0 * inverse)
            store_tall(update_ref, block, done.astype(bf16))


def wide_block(ref, block, size):
    clips, seqs, rows = ref.shape[:3]
    count = seqs // 8
    return ref[:, block * count : (block + 1) * count].reshape(size, HALF)


def store_wide(ref, block, values):
    clips, seqs, rows = ref.shape[:3]
    count = seqs // 8
    ref[:, block * count : (block + 1) * count] = values.reshape(clips, count, rows, HALF)


def tall_block(ref, block, size):
    clips, seqs, rows = ref.shape[:3]
    span = slice(block * clips // 4, (block + 1) * clips // 4)
    count = seqs // 2
    parts = [ref[span, half * count : (half + 1) * count].reshape(size, HALF) for half in range(2)]
    return jnp.concatenate(parts, axis=1)


def store_tall(ref, block, values):
    clips, seqs, rows = ref.shape[:3]
    span = slice(block * clips // 4, (block + 1) * clips // 4)
    count = seqs // 2
    for half in range(2):
        piece = values[:, half * HALF : (half + 1) * HALF]
        ref[span, half * count : (half + 1) * count] = piece.reshape(clips // 4, count, rows, HALF)


def tail_kernel(
    g0_ref, small_ref, early_ref, wide_ref, qkv_ref, proj_ref, din_ref,
    dout_ref, shard_ref, step_ref, total_ref,
    near0, near1, sums0, sums1, far0, far1, held0, held1, line0, line1,
    moved, mom_s, edge_s, whole_s, update_s, gram_s, poly_s, norm_s,
    sa, ra, sb, rb, sc, rc, sd, rd, se, re, sf, rf, sg, rg, sh, rh, si, ri, sj, rj,
    halo_send, halo_recv, halo_own, mom_sem,
):
    spot = Spot()
    chips, clips, seqs = spot.chips, spot.clips, spot.seqs
    rows = moved.shape[0]
    share, quarter = seqs // 8, seqs // 4
    early = share == 1
    near, sums = (near0, near1), (sums0, sums1)
    far, held, line = (far0, far1), (held0, held1), (line0, line1)

    part = rows // 2 if early else rows
    rest = pl.ds(rows - part, part)
    matrix = spot.seq // (2 * share)
    if early:
        sub = pl.ds(pl.multiple_of(spot.core * part, part), part)
        cuts = [(sub, pl.ds(half * HALF, HALF), pl.ds(half * part, part)) for half in range(2)]
    else:
        sub = pl.ds(pl.multiple_of((spot.seq % share) * rows, rows), rows)
        cuts = [(sub, pl.ds(pl.multiple_of((spot.seq // share % 2) * HALF, HALF), HALF), pl.ds(0, rows))]

    @pl.when(matrix < 3)
    def _():
        for k, (sub, cols, to) in enumerate(cuts):
            pltpu.make_async_copy(qkv_ref.at[matrix, sub, cols], mom_s.at[to], mom_sem.at[k]).start()

    @pl.when(matrix == 3)
    def _():
        for k, (sub, cols, to) in enumerate(cuts):
            pltpu.make_async_copy(proj_ref.at[sub, cols], mom_s.at[to], mom_sem.at[k]).start()

    greet_all(spot)

    def at_place(place):
        return jnp.logical_and(place[0] == spot.seq, place[1] == spot.clip)

    owners = {(u, m): owner_of(u, m, clips, chips) for u in range(3) for m in range(2 if u else 4)}
    taker = owner_of(0, spot.seq // quarter, clips, chips)

    def hand_over(total, k):
        sub, cols, span = cuts[k]
        pltpu.make_async_copy(proj_ref.at[sub, cols], mom_s.at[span], mom_sem.at[k]).wait()
        moved[span] = (momentum_decay * mom_s[span] + total).astype(bf16)
        shard_ref[0, spot.seq, span] = total.astype(bf16)
        spare = whole_s.at[spot.clip, spot.seq, span]

        @pl.when(at_place(taker))
        def _():
            pltpu.make_async_copy(moved.at[span], spare, rg.at[0]).start()

        @pl.when(jnp.logical_not(at_place(taker)))
        def _():
            send(moved.at[span], spare, sg.at[k], rg.at[0], taker)

    def slot(u, seq):
        return total_ref.at[seq] if u == 1 else shard_ref.at[0, seq]

    def spread(u):
        here = slot(u, spot.seq)
        for e in range(1, chips):
            send(here, here, sd.at[u, e - 1], rd.at[u, e - 1], spot.across(e))
        send(here, here, se.at[u, 0], re.at[u, 0], spot.sibling)

    def forward(u):
        for e in range(1, chips):
            here = slot(u, spot.across(-e)[0])
            landing(here, rd.at[u, e - 1], spot).wait_recv()
            send(here, here, se.at[u, e], re.at[u, e], spot.sibling)

    def for_wide_owners(work):
        for u in (1, 2):

            @pl.when(jnp.logical_or(at_place(owners[u, 0]), at_place(owners[u, 1])))
            def _():
                work(u)

    def wide_sweep(sweep):
        mine = [at_place(owners[u, k]) for u in (1, 2) for k in range(2)]

        @pl.when(functools.reduce(jnp.logical_or, mine))
        def _():
            gram_sweep(gram_s, poly_s, sweep)

    def deal(u, number, settle):
        width, planes = (quarter, clips) if u == 0 else (seqs, clips // 2)

        def step(t, carry):
            if u == 0:
                clip, seq = t // width, number * quarter + t % width
            else:
                clip, seq = number * planes + t // width, t % width
            src, dst = update_s.at[clip, seq], step_ref.at[u, seq]
            mine = at_place((seq, clip))
            if settle:

                @pl.when(jnp.logical_not(mine))
                def _():
                    landing(src, sh.at[clip, seq], spot).wait_send()

            else:

                @pl.when(mine)
                def _():
                    pltpu.make_async_copy(src, dst, rh.at[u]).start()

                @pl.when(jnp.logical_not(mine))
                def _():
                    send(src, dst, sh.at[clip, seq], rh.at[u], (seq, clip))

            return carry

        lax.fori_loop(0, planes * width, step, 0)

    send(g0_ref.at[:, :, 1 - spot.core, rest], near0, sa.at[0], ra.at[0], spot.sibling)
    send(small_ref.at[:, :, 1 - spot.core], near1, sa.at[1], ra.at[1], spot.sibling)
    if early:
        hand_over(early_ref[...], 0)

    def plane_send(k):
        landing(near[k], ra.at[k], spot).wait_recv()
        mine = g0_ref[:, :, spot.core, rest] if k == 0 else small_ref[:, :, spot.core]
        total = mine.astype(f32) + near[k][...].astype(f32)
        sums[k][...] = total.astype(sums[k].dtype)
        for e in range(1, chips):
            to = spot.across(e)
            send(sums[k].at[:, to[0] // 2], far[k].at[e - 1], sb.at[k, e - 1], rb.at[k, e - 1], to)

    def line_send(k):
        total = sums[k][:, spot.chip].astype(f32)
        for e in range(1, chips):
            landing(far[k].at[e - 1], rb.at[k, e - 1], spot).wait_recv()
            total += far[k][e - 1].astype(f32)
        held[k][...] = total.astype(held[k].dtype)
        for d in range(1, clips):
            to = spot.along(d)
            send(held[k].at[to[1]], line[k].at[d - 1], sc.at[k, d - 1], rc.at[k, d - 1], to)

    def line_sum(k):
        total = held[k][spot.clip].astype(f32)
        for d in range(1, clips):
            landing(line[k].at[d - 1], rc.at[k, d - 1], spot).wait_recv()
            total += line[k][d - 1].astype(f32)
        return total

    for_wide_owners(lambda u: gram_start(wide_ref, gram_s, norm_s, u == 1))
    for k in range(2):
        plane_send(k)
    wide_sweep(0)
    for k in range(2):
        line_send(k)
    wide_sweep(1)
    copies = halo_out(spot, din_ref, dout_ref, halo_send, halo_recv, halo_own.at[0])
    hand_over(line_sum(0), len(cuts) - 1)
    spread(0)
    edge_s[spot.clip] = line_sum(1)
    for d in range(1, clips):
        here = edge_s.at[spot.clip]
        send(here, here, sf.at[d - 1], rf.at[d - 1], spot.along(d))

    for sweep in range(2, 5):
        wide_sweep(sweep)

    def conclude(u):
        gram_finish(wide_ref, update_s, poly_s, norm_s, u == 1)
        for number in range(2):

            @pl.when(at_place(owners[u, number]))
            def _():
                deal(u, number, False)

    for_wide_owners(conclude)

    @pl.when(functools.reduce(jnp.logical_or, [at_place(owners[0, m]) for m in range(4)]))
    def _():
        number = spot.seq // quarter
        landing(whole_s.at[:, pl.ds(number * quarter, quarter)], rg.at[0], spot).wait_recv()
        ortho_square(whole_s, update_s, gram_s, number)

    for number in range(4):

        @pl.when(at_place(owners[0, number]))
        def _():
            deal(0, number, False)

    for d in range(1, clips):
        landing(edge_s.at[0], rf.at[d - 1], spot).wait_recv()
    total_ref[spot.seq] = edge_s[...]
    spread(1)
    forward(0)
    forward(1)

    order = (1, 2, 0)
    for u in order:
        here = step_ref.at[u, spot.seq]
        landing(here, rh.at[u], spot).wait_recv()
        for e in range(1, chips):
            send(here, here, si.at[u, e - 1], ri.at[u, e - 1], spot.across(e))
        send(here, here, sj.at[u, 0], rj.at[u, 0], spot.sibling)
    for u in order:
        for e in range(1, chips):
            here = step_ref.at[u, spot.across(-e)[0]]
            landing(here, ri.at[u, e - 1], spot).wait_recv()
            send(here, here, sj.at[u, e], rj.at[u, e], spot.sibling)

    for u in range(2):
        for e in range(chips):
            landing(slot(u, 0), re.at[u, e], spot).wait_recv()
            landing(slot(u, 0), se.at[u, e], spot).wait_send()
            if e > 0:
                landing(slot(u, 0), sd.at[u, e - 1], spot).wait_send()

    @pl.when(jnp.logical_not(at_place(taker)))
    def _():
        for k, (_, _, span) in enumerate(cuts):
            landing(moved.at[span], sg.at[k], spot).wait_send()

    for (u, number), place in owners.items():

        @pl.when(at_place(place))
        def _():
            deal(u, number, True)

    for k in range(2):
        landing(near[k], sa.at[k], spot).wait_send()
        for e in range(1, chips):
            landing(far[k].at[e - 1], sb.at[k, e - 1], spot).wait_send()
        for d in range(1, clips):
            landing(line[k].at[d - 1], sc.at[k, d - 1], spot).wait_send()
    for u in range(3):
        for e in range(chips):
            if e > 0:
                landing(step_ref.at[u, 0], si.at[u, e - 1], spot).wait_send()
            landing(step_ref.at[u, 0], sj.at[u, e], spot).wait_send()
            landing(step_ref.at[u, 0], rj.at[u, e], spot).wait_recv()
    for d in range(1, clips):
        landing(edge_s.at[0], sf.at[d - 1], spot).wait_send()
    for copy in copies:
        copy.wait()


def tail(grad, small, early, wide, qkv_m, proj_m, d_input):
    clips, seqs, rows, _ = wide.shape
    chips = seqs // 2
    size = clips * seqs * rows // 8
    small_rows = 8 * clips * seqs
    small = jnp.pad(small, ((0, small_rows - small.shape[0]), (0, 0)))
    cut = [grad, small.reshape(clips, chips, 2, 8, HALF)]
    kinds = [(bf16, rows // 2 if seqs == 8 else rows), (f32, 8)]
    dma = pltpu.SemaphoreType.DMA
    scratch = [pltpu.VMEM((clips, chips, r, HALF), t) for t, r in kinds]
    scratch += [pltpu.VMEM((clips, chips, r, HALF), t) for t, r in kinds]
    scratch += [pltpu.VMEM((chips - 1, clips, r, HALF), t) for t, r in kinds]
    scratch += [pltpu.VMEM((clips, r, HALF), t) for t, r in kinds]
    scratch += [pltpu.VMEM((clips - 1, r, HALF), t) for t, r in kinds]
    scratch += [
        pltpu.VMEM((rows, HALF), bf16),
        pltpu.VMEM((rows, HALF), f32),
        pltpu.VMEM((clips, 8, HALF), f32),
        pltpu.VMEM((clips, seqs, rows, HALF), bf16),
        pltpu.VMEM((clips, seqs, rows, HALF), bf16),
        pltpu.VMEM((size, size), f32),
        pltpu.VMEM((size, size), f32),
        pltpu.VMEM((8, 128), f32),
    ]
    scratch += [dma((2,)), dma((2,))]
    scratch += [dma((2, chips - 1)), dma((2, chips - 1))]
    scratch += [dma((2, clips - 1)), dma((2, clips - 1))]
    scratch += [dma((2, chips - 1)), dma((2, chips - 1))]
    scratch += [dma((2, chips)), dma((2, chips))]
    scratch += [dma((clips - 1,)), dma((clips - 1,))]
    scratch += [dma((2,)), dma((1,))]
    scratch += [dma((clips, seqs)), dma((3,))]
    scratch += [dma((3, chips - 1)), dma((3, chips - 1))]
    scratch += [dma((3, chips)), dma((3, chips))]
    scratch += [dma((3,)), dma((3,)), dma((1,)), dma((2,))]
    return pl.pallas_call(
        tail_kernel,
        in_specs=[WHOLE] * 4 + [ANY] * 2 + [WHOLE],
        out_specs=[WHOLE] * 4,
        out_shape=[
            jax.ShapeDtypeStruct(d_input.shape, bf16),
            jax.ShapeDtypeStruct((1, seqs, rows, HALF), bf16),
            jax.ShapeDtypeStruct((3, seqs, rows, HALF), bf16),
            jax.ShapeDtypeStruct((seqs, clips, 8, HALF), f32),
        ],
        scratch_shapes=scratch,
        compiler_params=pltpu.CompilerParams(
            collective_id=2, has_side_effects=True, vmem_limit_bytes=VMEM_LIMIT
        ),
        name="tail",
    )(*cut, early, wide, qkv_m, proj_m, d_input)


def blocks_of(shard, unit, at=None):
    seqs, rows = shard.shape[1:3]
    count = 2 if unit == 2 else 8
    share = seqs // count
    at = unit if at is None else at
    if unit == 0:
        places = [matrix_at(b // 2, b % 2, share, rows) for b in range(8)]
        return [shard[(at, *place)].reshape(share * rows, HALF) for place, _ in places]
    return [shard[at, b * share : (b + 1) * share].reshape(share * rows, HALF) for b in range(count)]


def places_of(refs):
    qkv, proj, first, second = refs
    cols = [slice(b * HALF, (b + 1) * HALF) for b in range(8)]
    mats = [(qkv, (b // 2, slice(None), cols[b % 2])) for b in range(6)]
    mats += [(proj, (slice(None), cols[b])) for b in range(2)]
    return (
        mats,
        [(first, (slice(None), cols[b])) for b in range(8)],
        [(second, (slice(None), cols[b])) for b in range(2)],
    )


def finish_kernel(
    first_ref, shard_ref, step_ref, *refs,
):
    old_refs, (out_ref, din_ref, total_ref, vec_ref, vecm_ref, table_ref, tablem_ref) = refs[:8], refs[8:15]
    new_refs, (new_out, new_din, new_vecm, new_vec, new_tablem, new_table) = refs[15:23], refs[23:29]
    first_s, shard_s, step_s = refs[29:32]
    old_s, new_s = refs[32:40], refs[40:48]
    tile_s, flat_s, grad_s, in_sem, old_sem, new_sem, tile_sem = refs[48:]
    slices = [
        pltpu.make_async_copy(src, dst, in_sem.at[k])
        for k, (src, dst) in enumerate(((first_ref, first_s), (shard_ref, shard_s), (step_ref, step_s)))
    ]
    loads = [pltpu.make_async_copy(old_refs[k], old_s[k], old_sem.at[k]) for k in range(8)]
    stores = [pltpu.make_async_copy(new_s[k], new_refs[k], new_sem.at[k]) for k in range(8)]
    arrivals = [pltpu.make_async_copy(src, tile_s.at[k], tile_sem.at[k]) for k, src in enumerate((out_ref, din_ref))]
    tiles = [pltpu.make_async_copy(tile_s.at[k], dst, tile_sem.at[2 + k]) for k, dst in enumerate((new_out, new_din))]
    slices[0].start()
    loads[0].start()
    loads[1].start()
    slices[1].start()
    loads[2].start()
    loads[3].start()
    slices[2].start()
    for k in range(4, 8):
        loads[k].start()
    for copy in arrivals:
        copy.start()

    def place_of(unit, refs):
        return places_of(refs)[unit]

    for group in range(2):
        old, new = old_s[4 * group : 4 * group + 4], new_s[4 * group : 4 * group + 4]
        if group == 1:
            slices[2].wait()
        for unit in range(3):
            if group == 0 and unit < 2:
                slices[unit].wait()
            arrays = ((0, 1), (2,), (3,))[unit]
            for k in arrays:
                loads[4 * group + k].wait()
            if group == 1:
                blocks = blocks_of(step_s, unit)
            else:
                blocks = blocks_of(shard_s, unit, unit - 1) if unit else blocks_of(first_s, 0)
            for block, (src, at), (dst, _) in zip(blocks, place_of(unit, old), place_of(unit, new)):
                if group == 0:
                    dst[at] = momentum_decay * src[at] + block.astype(f32)
                else:
                    dst[at] = src[at] - matrix_rate * block.astype(f32)
            for k in arrays:
                stores[4 * group + k].start()

    for arrival, tile in zip(arrivals, tiles):
        arrival.wait()
        tile.start()
    seqs = total_ref.shape[0]
    for q in range(SMALL // 8):
        flat_s[q * 8 : (q + 1) * 8, :] = total_ref[q % seqs, q // seqs]
    base = HEADS * SPAN
    for v in range(vec_ref.shape[0]):
        for half in range(2):
            line_at = base + 2 * v + half
            grad_s[v : v + 1, half * HALF : (half + 1) * HALF] = flat_s[line_at : line_at + 1, :]
    moved = vector_decay * vecm_ref[...] + grad_s[...]
    new_vecm[...] = moved
    new_vec[...] = vec_ref[...] - vector_rate * moved
    for time in range(SPAN_T):
        for step in range(SPAN):
            offset = time * SPAN * SPAN + step * SPAN
            piece = flat_s[step * HEADS : (step + 1) * HEADS, time * SPAN : (time + 1) * SPAN]
            new_tablem[:, offset : offset + SPAN] = piece
    moved = vector_decay * tablem_ref[...] + new_tablem[...]
    new_tablem[...] = moved
    new_table[...] = table_ref[...] - table_rate * moved
    for copy in stores + tiles:
        copy.wait()


def finish(first, shard, step, momenta, weights, tiles, total, vectors, vector_m, table_t, table_mt):
    olds = (*momenta, *weights)
    small = (vector_m, vectors, table_mt, table_t)
    dma = pltpu.SemaphoreType.DMA
    return pl.pallas_call(
        finish_kernel,
        in_specs=[ANY] * 13 + [WHOLE] * 5,
        out_specs=[ANY] * 10 + [WHOLE] * 4,
        out_shape=[jax.ShapeDtypeStruct(a.shape, a.dtype) for a in (*olds, *tiles, *small)],
        scratch_shapes=[
            *[pltpu.VMEM(a.shape, a.dtype) for a in (first, shard, step, *olds, *olds)],
            pltpu.VMEM((2, *tiles[0].shape), bf16),
            pltpu.VMEM((SMALL, HALF), f32),
            pltpu.VMEM(vectors.shape, f32),
            dma((3,)),
            dma((8,)),
            dma((8,)),
            dma((4,)),
        ],
        compiler_params=pltpu.CompilerParams(vmem_limit_bytes=VMEM_LIMIT),
        name="finish",
    )(first, shard, step, *olds, *tiles, total, vectors, vector_m, table_t, table_mt)


def local(
    clips, cotangent, qkv_w, proj_w, fc1_w, fc2_w, qkv_m, proj_m, fc1_m, fc2_m,
    vectors, vector_m, table, table_m,
):
    frames = clips.shape[2]
    width = clips.shape[-1]
    weights = (qkv_w, proj_w, fc1_w, fc2_w)
    momenta = (qkv_m, proj_m, fc1_m, fc2_m)
    tile_in = clips[0, 0].transpose(1, 2, 0, 3)
    tile_cot = cotangent[0, 0].transpose(1, 2, 0, 3)
    pattern = time_pattern()
    probs, inv, qt, kt, vt, mt, middle, h1t, x_tile, cot_tile, packed0, packed12 = front(
        tile_in, tile_cot, weights, vectors, table.T, pattern
    )
    x_cells = x_tile.reshape(CELLS, frames, width)
    cot_cells = cot_tile.reshape(CELLS, frames, width)
    saved = (probs, inv, qt, kt, vt, mt, h1t)
    d_input, g0, small, early, output, wide, shard = core(
        saved, middle, x_cells, cot_cells, packed0, packed12, vectors, pattern, momenta
    )
    input_grad, first, step, total = tail(g0, small, early, wide, qkv_m, proj_m, d_input.reshape(tile_in.shape))
    *rest, output, input_grad, new_vector_m, new_vectors, new_table_m, new_table = finish(
        first, shard, step, momenta, weights, (output, input_grad), total, vectors, vector_m, table.T, table_m.T
    )
    output = output.transpose(2, 0, 1, 3)[None, None]
    input_grad = input_grad.transpose(2, 0, 1, 3)[None, None]
    return (output, input_grad, *rest, new_vector_m, new_vectors, new_table_m.T, new_table.T)


def solution(mesh):
    tile = P("clip", "seq", None, None, None, None)
    stack = P(None, "clip", None)
    rows = P("clip", None)
    weights = (stack, rows, rows, rows)
    return jax.shard_map(
        local,
        mesh=mesh,
        in_specs=(tile, tile, *weights, *weights, P(), P(), P(), P()),
        out_specs=(tile, tile, *weights, *weights, P(), P(), P(), P()),
        check_vma=False,
    )
```

```python
import functools
import math

import jax
import jax.numpy as jnp
import numpy as np
from jax import lax
from jax.experimental import pallas as pl
from jax.experimental.pallas import tpu as pltpu
from jax.sharding import PartitionSpec as P

HEADS = 16
WIN_T = 8
SIDE = 7
CELLS = SIDE * SIDE
WINDOW = WIN_T * CELLS
SHIFT_T = 4
SHIFT_S = 3
GRID_W = 2
TABLE = 2535
SPAN_T = 2 * WIN_T - 1
SPAN = 2 * SIDE - 1
ROW = SIDE * WIN_T
WIDE = SPAN * ROW
GROUPS = 4
GROUP_HEADS = HEADS // GROUPS
HALF = 256
SMALL = 256

epsilon_norm = 1e-05
mask_value = -100.0
momentum_decay = 0.95
vector_decay = 0.9
matrix_rate = 1.0
vector_rate = 0.0006
table_rate = 0.03
quintic_first = 3.4445
quintic_second = -4.775
quintic_third = 2.0315
frobenius_epsilon = 1e-07
log2e = 1.4426950408889634
VMEM_LIMIT = 60 * 1024 * 1024
f32 = jnp.float32
bf16 = jnp.bfloat16


def mm(left, right):
    return lax.dot_general(left, right, (((1,), (0,)), ((), ())), preferred_element_type=f32)


def mm_nt(left, right):
    return lax.dot_general(left, right, (((1,), (1,)), ((), ())), preferred_element_type=f32)


def mm_tn(left, right):
    return lax.dot_general(left, right, (((0,), (0,)), ((), ())), preferred_element_type=f32)


def layer_stats(values):
    mean = jnp.mean(values, axis=-1, keepdims=True)
    centred = values - mean
    variance = jnp.mean(centred * centred, axis=-1, keepdims=True)
    inverse = lax.rsqrt(variance + epsilon_norm)
    return (centred * inverse, inverse)


def norm_backward(grad_norm, normed, inverse, gain):
    scaled = grad_norm * gain
    centred = scaled - jnp.mean(scaled, axis=-1, keepdims=True)
    return (centred - normed * jnp.mean(scaled * normed, axis=-1, keepdims=True)) * inverse


def early_slots(shape):
    return lax.broadcasted_iota(jnp.int32, shape, 1) < SHIFT_T


def split_windows(block):
    low, high = block[:, :WIN_T], block[:, WIN_T:]
    early = early_slots(low.shape)
    first = jnp.where(early, high, low)
    second = jnp.where(early, low, high)
    return (first.reshape(WINDOW, -1), second.reshape(WINDOW, -1))


def join_windows(first, second):
    first = first.reshape(CELLS, WIN_T, -1)
    second = second.reshape(CELLS, WIN_T, -1)
    early = early_slots(first.shape)
    low = jnp.where(early, second, first)
    high = jnp.where(early, first, second)
    return jnp.concatenate((low, high), axis=1)


def slot_frames():
    return (np.arange(WIN_T) + SHIFT_T) % WIN_T


def time_pattern():
    frames = slot_frames()
    lane = np.arange(128)
    column, slot = lane // WIN_T, lane % WIN_T
    flat = (frames[None, slot] - frames[:, None] + WIN_T - 1) * SPAN + column[None, :]
    flat = np.where(column[None, :] < SPAN, flat, -1)
    return jnp.asarray((flat.reshape(-1, 1) == np.arange(HALF)).astype(np.float32), dtype=bf16)


def label_features(labels, weights):
    row = lax.broadcasted_iota(jnp.int32, (32, labels.shape[1]), 0)
    value = jnp.zeros(row.shape, f32)
    for k, weight in enumerate(weights):
        value = jnp.where(jnp.logical_and(row // 8 == k, row % 8 == labels), weight, value)
    return value.astype(bf16)


def halves(values):
    high = values.astype(bf16)
    return (high, (values - high.astype(f32)).astype(bf16))


MESH = pl.DeviceIdType.MESH
ANY = pl.BlockSpec(memory_space=pl.ANY)
WHOLE = pl.BlockSpec(memory_space=pltpu.VMEM)


class Spot:
    def __init__(self):
        self.seq = lax.axis_index("seq")
        self.clip = lax.axis_index("clip")
        self.seqs = lax.axis_size("seq")
        self.clips = lax.axis_size("clip")
        self.chips = self.seqs // 2
        self.chip = self.seq // 2
        self.core = self.seq % 2
        self.sibling = (self.seq + 1 - 2 * self.core, self.clip)

    def across(self, step, core=None):
        core = self.core if core is None else core
        return (((self.chip + step + self.chips) % self.chips) * 2 + core, self.clip)

    def along(self, step):
        return (self.seq, (self.clip + step + self.clips) % self.clips)


def send(src, dst, send_sem, recv_sem, to):
    copy = pltpu.make_async_remote_copy(
        src_ref=src, dst_ref=dst, send_sem=send_sem, recv_sem=recv_sem, device_id=to, device_id_type=MESH
    )
    copy.start()
    return copy


def landing(ref, sem, spot):
    return pltpu.make_async_remote_copy(
        src_ref=ref, dst_ref=ref, send_sem=sem, recv_sem=sem, device_id=spot.sibling, device_id_type=MESH
    )


def greet(targets, count):
    barrier = pltpu.get_barrier_semaphore()
    for to in targets:
        pl.semaphore_signal(barrier, inc=1, device_id=to, device_id_type=MESH)
    pl.semaphore_wait(barrier, count)


def greet_all(spot):
    barrier = pltpu.get_barrier_semaphore()

    def tell(step, carry):
        seq = (spot.seq + step % spot.seqs) % spot.seqs
        clip = (spot.clip + step // spot.seqs) % spot.clips
        pl.semaphore_signal(barrier, inc=1, device_id=(seq, clip), device_id_type=MESH)
        return carry

    others = spot.seqs * spot.clips - 1
    lax.fori_loop(1, others + 1, tell, 0)
    pl.semaphore_wait(barrier, others)


EDGE = SIDE - SHIFT_S


def halo_parts(spot, src, dst, send_sems, recv_sems):
    keep, lead = pl.ds(SHIFT_S, EDGE), pl.ds(0, SHIFT_S)
    front, back = pl.ds(0, EDGE), pl.ds(EDGE, SHIFT_S)
    parts = (
        (src.at[keep, lead], dst.at[front, back], spot.sibling),
        (src.at[lead, keep], dst.at[back, front], spot.across(-1)),
        (src.at[lead, lead], dst.at[back, back], spot.across(-1, 1 - spot.core)),
    )
    return [
        pltpu.make_async_remote_copy(
            src_ref=a, dst_ref=b, send_sem=send_sems.at[k], recv_sem=recv_sems.at[k], device_id=to, device_id_type=MESH
        )
        for k, (a, b, to) in enumerate(parts)
    ]


def halo_in(spot, src, dst, send_sems, recv_sems, local_sem):
    copies = halo_parts(spot, src, dst, send_sems, recv_sems)
    copies.append(
        pltpu.make_async_copy(
            src.at[pl.ds(SHIFT_S, EDGE), pl.ds(SHIFT_S, EDGE)], dst.at[pl.ds(0, EDGE), pl.ds(0, EDGE)], local_sem
        )
    )
    for copy in copies:
        copy.start()
    return copies


def halo_back(spot, src, dst, send_sems, recv_sems, local_sem):
    keep, lead = pl.ds(SHIFT_S, EDGE), pl.ds(0, SHIFT_S)
    front, back = pl.ds(0, EDGE), pl.ds(EDGE, SHIFT_S)
    parts = (
        (src.at[front, back], dst.at[keep, lead], spot.sibling),
        (src.at[back, front], dst.at[lead, keep], spot.across(1)),
        (src.at[back, back], dst.at[lead, lead], spot.across(1, 1 - spot.core)),
    )
    copies = [
        pltpu.make_async_remote_copy(
            src_ref=a, dst_ref=b, send_sem=send_sems.at[k], recv_sem=recv_sems.at[k], device_id=to, device_id_type=MESH
        )
        for k, (a, b, to) in enumerate(parts)
    ]
    return copies + [pltpu.make_async_copy(src.at[front, front], dst.at[keep, keep], local_sem)]


def halo_out(spot, src, dst, send_sems, recv_sems, local_sem):
    copies = halo_back(spot, src, dst, send_sems, recv_sems, local_sem)
    for copy in copies:
        copy.start()
    return copies


def owner_of(unit, part, clips, chips):
    low = clips // 2 - 1
    if unit == 0:
        return (part * chips // 2 + 1, low + part % 2)
    return (0 if unit == 1 else 2 * (chips - 1), low + part)


def matrix_at(matrix, half, share, rows):
    if share == 1:
        part = rows // 2
        start = half * part if isinstance(half, int) else pl.multiple_of(half * part, part)
        return (pl.ds(2 * matrix, 2), pl.ds(start, part)), (2, part)
    return (pl.ds((2 * matrix + half) * share, share), pl.ds(0, rows)), (share, rows)


def pieces_of(share, rows):
    return ((0, rows // 2), (rows // 2, rows // 2)) if share == 1 else ((0, rows),)


def front_kernel(
    x_ref, cot_ref, qkv_ref, proj_ref, fc1_ref, fc2_ref, vec_ref, table_ref, pattern_ref,
    probs_ref, inv_ref, qt_ref, kt_ref, vt_ref, mt_ref, middle_ref, h1t_ref, xo_ref, co_ref, pack0_ref, pack12_ref,
    feat_s, bias_s, wide_s, row_s, table_s, x_s, shard_s, pack_s,
    vect_s, halo_send, halo_recv, halo_own, own_sem, send1, recv1, send2, recv2, send3, recv3,
    wide1_send, wide1_recv, wide2_send, wide2_recv, wide3_send, wide3_recv,
):
    group = pl.program_id(0)
    spot = Spot()
    clips, chips, seqs = spot.clips, spot.chips, spot.seqs
    _, _, rows, _ = shard_s.shape
    lanes = mt_ref.shape[1]
    head_dim = lanes // GROUP_HEADS
    scale = head_dim ** (-0.5) * log2e
    width = vec_ref.shape[-1]
    share = seqs // 8

    pieces = pieces_of(share, rows)

    def slot(piece, clip, seq):
        return pack_s.at[clip, seq, pl.ds(*pieces[piece])]

    def first(piece):
        def step(d, carry):
            send(
                shard_s.at[0, spot.seq, pl.ds(*pieces[piece])], slot(piece, spot.clip, spot.seq),
                send1.at[piece, d - 1], recv1.at[piece, d - 1], spot.along(d),
            )
            return carry

        lax.fori_loop(1, clips, step, 0)

    def second(piece):
        def step(d, carry):
            here = slot(piece, (spot.clip - d + clips) % clips, spot.seq)
            landing(here, recv1.at[piece, d - 1], spot).wait_recv()
            for e in range(1, chips):
                send(here, here, send2.at[piece, d - 1, e - 1], recv2.at[piece, d - 1, e - 1], spot.across(e))
            send(here, here, send3.at[piece, d - 1, 0], recv3.at[piece, d - 1, 0], spot.sibling)
            return carry

        lax.fori_loop(1, clips, step, 0)

    def third(piece):
        def step(d, carry):
            clip = (spot.clip - d + clips) % clips
            for e in range(1, chips):
                here = slot(piece, clip, spot.across(-e)[0])
                landing(here, recv2.at[piece, d - 1, e - 1], spot).wait_recv()
                send(here, here, send3.at[piece, d - 1, e], recv3.at[piece, d - 1, e], spot.sibling)
            return carry

        lax.fori_loop(1, clips, step, 0)

    def arrive(piece):
        def step(d, carry):
            for e in range(chips):
                landing(slot(piece, spot.clip, spot.seq), recv3.at[piece, d - 1, e], spot).wait_recv()
            return carry

        lax.fori_loop(1, clips, step, 0)

    def leave(piece):
        def step(d, carry):
            here = slot(piece, spot.clip, spot.seq)
            landing(here, send1.at[piece, d - 1], spot).wait_send()
            for e in range(chips):
                if e > 0:
                    landing(here, send2.at[piece, d - 1, e - 1], spot).wait_send()
                landing(here, send3.at[piece, d - 1, e], spot).wait_send()
            return carry

        lax.fori_loop(1, clips, step, 0)

    line = chips // 2
    parity = (spot.chip % line + spot.chip // line) % 2
    beside = (
        ((spot.chip + 1 - 2 * (spot.chip % 2)) * 2 + spot.core, spot.clip),
        ((spot.chip + line) % chips * 2 + spot.core, spot.clip),
    )

    def cut(part):
        return pl.ds(part * (seqs // 4) + spot.core * share, share)

    def over_clip(unit):
        def step(d, carry):
            for k in range(2):
                span = cut(2 * parity + k)
                send(
                    shard_s.at[unit + 1, span], pack12_ref.at[unit, spot.clip, span],
                    wide1_send.at[unit, d - 1, k], wide1_recv.at[unit, d - 1, k], spot.along(d),
                )
            return carry

        lax.fori_loop(1, clips, step, 0)

    def over_plane(unit):
        def step(d, carry):
            for k in range(2):
                here = pack12_ref.at[unit, (spot.clip - d + clips) % clips, cut(2 * parity + k)]
                landing(here, wide1_recv.at[unit, d - 1, k], spot).wait_recv()
                send(here, here, wide2_send.at[unit, d - 1, k], wide2_recv.at[unit, d - 1, k], beside[k])
                send(here, here, wide3_send.at[unit, d - 1, k], wide3_recv.at[unit, d - 1, k], spot.sibling)
            return carry

        lax.fori_loop(1, clips, step, 0)

    def over_cores(unit):
        def step(d, carry):
            for k in range(2):
                here = pack12_ref.at[unit, (spot.clip - d + clips) % clips, cut(2 * (1 - parity) + k)]
                landing(here, wide2_recv.at[unit, d - 1, k], spot).wait_recv()
                send(here, here, wide3_send.at[unit, d - 1, 2 + k], wide3_recv.at[unit, d - 1, 2 + k], spot.sibling)
            return carry

        lax.fori_loop(1, clips, step, 0)

    def settle(unit):
        def step(d, carry):
            here = pack12_ref.at[unit, spot.clip, cut(0)]
            for k in range(4):
                landing(here, wide3_recv.at[unit, d - 1, k], spot).wait_recv()
                landing(here, wide3_send.at[unit, d - 1, k], spot).wait_send()
                if k < 2:
                    landing(here, wide1_send.at[unit, d - 1, k], spot).wait_send()
                    landing(here, wide2_send.at[unit, d - 1, k], spot).wait_send()
            return carry

        lax.fori_loop(1, clips, step, 0)

    def halo(index):
        src, dst = ((x_ref, x_s), (cot_ref, co_ref))[index]
        return halo_in(spot, src, dst, halo_send.at[index], halo_recv.at[index], halo_own.at[index])

    def own_copy(unit):
        src = (pack_s, shard_s.at[1], shard_s.at[2], x_s)[unit]
        dst = (pack0_ref, pack12_ref.at[0, spot.clip], pack12_ref.at[1, spot.clip], xo_ref)[unit]
        return pltpu.make_async_copy(src, dst, own_sem.at[unit])

    @pl.when(group == 0)
    def _():
        targets = [spot.sibling, spot.across(1, 1 - spot.core)]
        targets += [spot.across(e) for e in range(1, chips)]
        targets += [spot.along(d) for d in range(1, clips)]
        greet(targets, len(targets))
        copies = halo(0)
        vect_s[...] = vec_ref[0:8, :].T.reshape(vect_s.shape)
        for block in range(8):
            half = block % 2
            src = proj_ref if block >= 6 else qkv_ref.at[block // 2]
            piece = src[:, half * HALF : (half + 1) * HALF].astype(bf16)
            at, shape = matrix_at(block // 2, half, share, rows)
            shard_s[(0, *at)] = piece.reshape(*shape, HALF)
        for k in range(len(pieces)):
            first(k)
        pack_s[spot.clip] = shard_s[0]
        for block in range(8):
            piece = fc1_ref[:, block * HALF : (block + 1) * HALF].astype(bf16)
            shard_s[1, block * share : (block + 1) * share] = piece.reshape(share, rows, HALF)
        for half in range(2):
            piece = fc2_ref[:, half * HALF : (half + 1) * HALF].astype(bf16)
            shard_s[2, half * 4 * share : (half + 1) * 4 * share] = piece.reshape(4 * share, rows, HALF)
        own_copy(1).start()
        own_copy(2).start()

        second(0)
        for unit in range(2):
            over_clip(unit)
        table_s[...] = jnp.zeros_like(table_s)
        for time in range(SPAN_T):
            for step in range(SPAN):
                offset = time * SPAN * SPAN + step * SPAN
                table_s[step * HEADS : (step + 1) * HEADS, time * SPAN : (time + 1) * SPAN] = (
                    table_ref[:, offset : offset + SPAN] * log2e
                )
        high, low = halves(table_s[...])
        for key in range(WIN_T):
            part = pattern_ref[key * 128 : (key + 1) * 128, :]
            wide_s[:, key, :] = mm_nt(high, part) + mm_nt(low, part)

        token = lax.broadcasted_iota(jnp.int32, (32, WINDOW), 1)
        edges = (spot.chip == chips - 1).astype(jnp.int32), (spot.core == GRID_W - 1).astype(jnp.int32)
        for w in range(2):
            labels = token_labels(token, w, edges)
            feat_s[w, 0] = label_features(labels, (1.0, 1.0, 1.0))
            feat_s[w, 1] = label_features(labels, mask_parts(head_dim))

        for k in range(1, len(pieces)):
            second(k)
        for copy in copies:
            copy.wait()
        block = x_s[...].reshape(CELLS, 2 * WIN_T, width).astype(f32)
        for w, tokens in enumerate(split_windows(block)):
            middle_ref[w] = tokens + vec_ref[4:5]
            normed, _ = layer_stats(tokens)
            h1t_ref[w] = (normed * vec_ref[0:1] + vec_ref[1:2]).astype(bf16).T
        own_copy(3).start()
        third(0)
        halo(1)
        arrive(0)

    @pl.when(group == 2)
    def _():
        over_plane(1)
        over_cores(0)

    @pl.when(group == 3)
    def _():
        over_cores(1)

    place = pl.ds(pl.multiple_of((group % 2) * lanes, lanes), lanes)
    weights = []
    for m in range(3):
        at, _ = matrix_at(m, group // 2, share, rows)
        weights.append(pack_s[(slice(None), *at, place)].reshape(width, lanes))
    for w in range(2):
        ht = h1t_ref[w]
        qt_ref[w] = (mm_tn(weights[0], ht) + vect_s[group, :, 2:3]).astype(bf16)
        kt_ref[w] = mm_tn(weights[1], ht).astype(bf16)
        vt_ref[w] = (mm_tn(weights[2], ht) + vect_s[group, :, 3:4]).astype(bf16)

    def head_step(head, carry):
        spread = pl.ds(pl.multiple_of(head * head_dim, head_dim), head_dim)
        for step in range(SPAN):
            folded = wide_s[step * HEADS + group * GROUP_HEADS + head]
            rows = [pltpu.roll(folded, (128 - (SIDE - 1 - key) * WIN_T) % 128, 1) for key in range(SIDE)]
            row_s[:, step * ROW : (step + 1) * ROW] = jnp.concatenate(rows, axis=0)[:, :ROW]
        for cell_row in range(SIDE):
            offset = (SIDE - 1 - cell_row) * ROW
            bias_s[cell_row * ROW : (cell_row + 1) * ROW, :] = row_s[:, offset : offset + WINDOW]
        for w in range(2):
            left = jnp.concatenate((kt_ref[w, spread, :], feat_s[w, 0]), axis=0)
            right = jnp.concatenate((qt_ref[w, spread, :], feat_s[w, 1]), axis=0)
            scores = mm_tn(left, right) * scale + bias_s[...]
            top = jnp.max(scores, axis=0, keepdims=True)
            expo = jnp.exp2(scores - top)
            inverse = 1.0 / jnp.sum(expo, axis=0, keepdims=True)
            low = expo.astype(bf16)
            probs_ref[head, w] = low
            inv_ref[head, w] = inverse
            mt_ref[w, spread, :] = (mm(vt_ref[w, spread, :], low) * inverse).astype(bf16)
        return carry

    lax.fori_loop(0, GROUP_HEADS, head_step, 0)

    @pl.when(group == 0)
    def _():
        for k in range(1, len(pieces)):
            third(k)
            arrive(k)
        own_copy(0).start()
        over_plane(0)

    z_group = clips // GROUPS
    for half in range(2):
        at, _ = matrix_at(3, half, share, rows)
        proj = pack_s[(pl.ds(group * z_group, z_group), *at)].reshape(lanes, HALF)
        cols = slice(half * HALF, (half + 1) * HALF)
        for w in range(2):
            middle_ref[w, :, cols] += mm_tn(mt_ref[w], proj)

    @pl.when(group == GROUPS - 1)
    def _():
        for unit in range(2):
            settle(unit)
        for k in range(len(pieces)):
            leave(k)
        for unit in range(4):
            own_copy(unit).wait()
        for copy in halo_parts(spot, cot_ref, co_ref, halo_send.at[1], halo_recv.at[1]):
            copy.wait()
        own = pltpu.make_async_copy(
            cot_ref.at[pl.ds(SHIFT_S, EDGE), pl.ds(SHIFT_S, EDGE)],
            co_ref.at[pl.ds(0, EDGE), pl.ds(0, EDGE)],
            halo_own.at[1],
        )
        own.wait()


def mask_parts(head_dim):
    rest, parts = -mask_value * math.sqrt(head_dim), []
    for _ in range(3):
        parts.append(float(np.float32(rest).astype(jnp.bfloat16)))
        rest -= parts[-1]
    return parts


def token_labels(index, window, edges):
    cell, frame = index // WIN_T, index % WIN_T
    row = sum((cell >= SIDE * k).astype(jnp.int32) for k in range(1, SIDE))
    column = cell - SIDE * row
    label = 2 * edges[0] * (row >= EDGE).astype(jnp.int32) + edges[1] * (column >= EDGE).astype(jnp.int32)
    if window == 1:
        label = label + 4 * (frame < SHIFT_T).astype(jnp.int32)
    return label


def front(tile_in, tile_cot, weights, vectors, table_t, pattern):
    clips, seqs = lax.axis_size("clip"), lax.axis_size("seq")
    chips, share = seqs // 2, seqs // 8
    rows_z = weights[1].shape[0]
    rows = rows_z // share
    count = len(pieces_of(share, rows))
    width = vectors.shape[-1]
    lanes = width // GROUPS
    tokens = (2, width, WINDOW)
    unit = (clips, seqs, rows, HALF)
    group_block = pl.BlockSpec((2, lanes, WINDOW), lambda g: (0, g, 0))
    dma = pltpu.SemaphoreType.DMA

    def const(shape):
        return pl.BlockSpec(shape, lambda g: (0,) * len(shape))

    return pl.pallas_call(
        front_kernel,
        grid=(GROUPS,),
        in_specs=[
            ANY,
            ANY,
            *[const(w.shape) for w in weights],
            const(vectors.shape),
            const(table_t.shape),
            const(pattern.shape),
        ],
        out_specs=[
            pl.BlockSpec((GROUP_HEADS, 2, WINDOW, WINDOW), lambda g: (g, 0, 0, 0)),
            pl.BlockSpec((GROUP_HEADS, 2, 1, WINDOW), lambda g: (g, 0, 0, 0)),
            group_block,
            group_block,
            group_block,
            group_block,
            const((2, WINDOW, width)),
            const(tokens),
            ANY,
            ANY,
            ANY,
            ANY,
        ],
        out_shape=[
            jax.ShapeDtypeStruct((HEADS, 2, WINDOW, WINDOW), bf16),
            jax.ShapeDtypeStruct((HEADS, 2, 1, WINDOW), f32),
            jax.ShapeDtypeStruct(tokens, bf16),
            jax.ShapeDtypeStruct(tokens, bf16),
            jax.ShapeDtypeStruct(tokens, bf16),
            jax.ShapeDtypeStruct(tokens, bf16),
            jax.ShapeDtypeStruct((2, WINDOW, width), f32),
            jax.ShapeDtypeStruct(tokens, bf16),
            jax.ShapeDtypeStruct(tile_in.shape, bf16),
            jax.ShapeDtypeStruct(tile_in.shape, bf16),
            jax.ShapeDtypeStruct(unit, bf16),
            jax.ShapeDtypeStruct((2, *unit), bf16),
        ],
        scratch_shapes=[
            pltpu.VMEM((2, 2, 32, WINDOW), bf16),
            pltpu.VMEM((WINDOW, WINDOW), f32),
            pltpu.VMEM((HEADS * SPAN, WIN_T, 128), f32),
            pltpu.VMEM((ROW, WIDE), f32),
            pltpu.VMEM((HEADS * SPAN, HALF), f32),
            pltpu.VMEM(tile_in.shape, bf16),
            pltpu.VMEM((3, seqs, rows, HALF), bf16),
            pltpu.VMEM(unit, bf16),
            pltpu.VMEM((GROUPS, lanes, 8), f32),
            dma((2, 3)),
            dma((2, 3)),
            dma((2,)),
            dma((4,)),
            dma((count, clips - 1)),
            dma((count, clips - 1)),
            dma((count, clips - 1, chips - 1)),
            dma((count, clips - 1, chips - 1)),
            dma((count, clips - 1, chips)),
            dma((count, clips - 1, chips)),
            *[dma((2, clips - 1, 2))] * 4,
            *[dma((2, clips - 1, 4))] * 2,
        ],
        compiler_params=pltpu.CompilerParams(
            collective_id=0, has_side_effects=True, vmem_limit_bytes=VMEM_LIMIT
        ),
        name="front",
    )(tile_in, tile_cot, *weights, vectors, table_t, pattern)


def core_kernel(
    middle_ref, cot_ref, w1_ref, w2_ref, vec_ref, probs_ref, inv_ref, qt_ref, kt_ref, vt_ref, mt_ref, h1t_ref,
    x_ref, w_ref, p_ref, pattern_ref, qkvm_ref, projm_ref, fc1m_ref, fc2m_ref,
    din_ref, grad_ref, small_ref, early_ref, out_ref, whole_ref, shard_ref,
    whole_s, shard_s, out_s, leave_sem, h2_s, h2t_s, dout_s, acc_s, dh2_s, rows_s, dmid_s, dbr_s, result_s, g1_s, g2_s,
    dot_s, dqkv_s, dh1t_s, dsum_s, wide_acc, wide_s, sums_s,
    near, sums, far, held, line, total_s, moved, mom_s, near0, sums0, far0, held0, line0,
    sa, ra, sb1, rb1, sb2, rb2, sc, rc, sd, rd, se, re, sg, rg, mom_sem,
    sa0, ra0, sb0, rb0, sc0, rc0, halo_send, halo_recv, halo_own,
):
    step = pl.program_id(0)
    group = jnp.maximum(step - GROUPS, 0)
    spot = Spot()
    chips, clips, seqs = spot.chips, spot.clips, spot.seqs
    rows = moved.shape[1]
    share = seqs // 8
    width = vec_ref.shape[-1]
    fresh = (g1_s, g2_s)
    chip_wide, clip_wide = chips // 4, clips // 4
    owners = fc_owners(clips, chips)
    early = share == 1
    chunk = chunk_of(step, chips)


    def chunk_chips(chunk):
        return pl.ds(chunk * chip_wide, chip_wide)

    def chunk_clips(chunk):
        return pl.ds(chunk * clip_wide, clip_wide)

    def near_parts(chunk, core):
        return (
            (g1_s.at[:, chunk_chips(chunk), core], near.at[0, :, chunk_chips(chunk)]),
            (g2_s.at[chunk_clips(chunk), :, core], near.at[1, chunk_clips(chunk)]),
        )

    def send_near(chunk):
        for u, (src, dst) in enumerate(near_parts(chunk, 1 - spot.core)):
            send(src, dst, sa.at[u, chunk], ra.at[u, chunk], spot.sibling)

    def send_far(chunk):
        for u, (_, dst) in enumerate(near_parts(chunk, spot.core)):
            landing(dst, ra.at[u, chunk], spot).wait_recv()
        here = chunk_chips(chunk)
        total = g1_s[:, here, spot.core].astype(f32) + near[0, :, here].astype(f32)
        sums[0, :, here] = total.astype(bf16)
        here = chunk_clips(chunk)
        total = g2_s[here, :, spot.core].astype(f32) + near[1, here].astype(f32)
        sums[1, here] = total.astype(bf16)
        for k in range(chip_wide):
            chip = chunk * chip_wide + k
            ahead = (chip - spot.chip + chips) % chips

            @pl.when(ahead > 0)
            def _():
                to = (2 * chip + spot.core, spot.clip)
                slot = ahead - 1
                send(sums.at[0, :, chip], far.at[0, slot], sb1.at[slot], rb1.at[slot], to)

        for e in range(1, chips):
            to = spot.across(e)
            send(
                sums.at[1, here, to[0] // 2], far.at[1, e - 1, here],
                sb2.at[chunk, e - 1], rb2.at[chunk, e - 1], to,
            )

    def send_line():
        for u in range(2):
            total = sums[u, :, spot.chip].astype(f32)
            for e in range(1, chips):
                if u == 0:
                    landing(far.at[0, e - 1], rb1.at[e - 1], spot).wait_recv()
                else:
                    for chunk in range(GROUPS):
                        here = far.at[1, e - 1, chunk_clips(chunk)]
                        landing(here, rb2.at[chunk, e - 1], spot).wait_recv()
                total += far[u, e - 1].astype(f32)
            held[u] = total.astype(bf16)
            for d in range(1, clips):
                to = spot.along(d)
                send(held.at[u, to[1]], line.at[u, d - 1], sc.at[u, d - 1], rc.at[u, d - 1], to)

    def at_place(place):
        return jnp.logical_and(place[0] == spot.seq, place[1] == spot.clip)

    def hand_over():
        spare = whole_s.at[spot.clip, spot.seq]
        for u in range(2):
            total = held[u, spot.clip].astype(f32)
            for d in range(1, clips):
                landing(line.at[u, d - 1], rc.at[u, d - 1], spot).wait_recv()
                total += line[u, d - 1].astype(f32)
            momentum_copy(u).wait()
            moved[u] = (momentum_decay * mom_s[u] + total).astype(bf16)
            total_s[u] = total.astype(bf16)
            for k, to in enumerate(owners[u]):

                @pl.when(at_place(to))
                def _():
                    pltpu.make_async_copy(moved.at[u], spare, rg.at[u]).start()

                @pl.when(jnp.logical_not(at_place(to)))
                def _():
                    send(moved.at[u], spare, sg.at[u, k], rg.at[u], to)

        for u in range(2):
            here = shard_s.at[u, spot.seq]
            for e in range(1, chips):
                send(total_s.at[u], here, sd.at[u, e - 1], rd.at[u, e - 1], spot.across(e))
            send(total_s.at[u], here, se.at[u, 0], re.at[u, 0], spot.sibling)
            pltpu.make_async_copy(total_s.at[u], here, mom_sem.at[2 + u]).start()

    def momentum_copy(u):
        return momentum_slice((qkvm_ref, projm_ref, fc1m_ref, fc2m_ref), u + 1, spot, rows, mom_s.at[u], mom_sem.at[u])

    def last_exchanges():
        for u in range(2):
            for e in range(1, chips):
                here = shard_s.at[u, spot.across(-e)[0]]
                landing(here, rd.at[u, e - 1], spot).wait_recv()
                send(here, here, se.at[u, e], re.at[u, e], spot.sibling)
        for u in range(2):
            pltpu.make_async_copy(total_s.at[u], shard_s.at[u, spot.seq], mom_sem.at[2 + u]).wait()
            for e in range(chips):
                landing(shard_s.at[u, 0], re.at[u, e], spot).wait_recv()
                landing(shard_s.at[u, 0], se.at[u, e], spot).wait_send()
                if e > 0:
                    landing(shard_s.at[u, 0], sd.at[u, e - 1], spot).wait_send()
                    if u == 0:
                        landing(far.at[0, e - 1], sb1.at[e - 1], spot).wait_send()
            for chunk in range(GROUPS):
                landing(near_parts(chunk, 0)[u][1], sa.at[u, chunk], spot).wait_send()
                if u == 1:
                    for e in range(1, chips):
                        here = far.at[1, e - 1, chunk_clips(chunk)]
                        landing(here, sb2.at[chunk, e - 1], spot).wait_send()
            for d in range(1, clips):
                landing(line.at[u, d - 1], sc.at[u, d - 1], spot).wait_send()
            for k, to in enumerate(owners[u]):

                @pl.when(jnp.logical_not(at_place(to)))
                def _():
                    landing(moved.at[u], sg.at[u, k], spot).wait_send()

                @pl.when(at_place(to))
                def _():
                    landing(whole_s, rg.at[u], spot).wait_recv()

    def outputs():
        return [
            pltpu.make_async_copy(src, dst, leave_sem.at[k])
            for k, (src, dst) in enumerate(((whole_s, whole_ref), (shard_s, shard_ref), (out_s, out_ref)))
        ]


    part = pl.ds(0, rows // 2)

    def early_near():
        send(grad_ref.at[:, :, 1 - spot.core, part], near0, sa0.at[0], ra0.at[0], spot.sibling)

    def early_far():
        landing(near0, ra0.at[0], spot).wait_recv()
        sums0[...] = (grad_ref[:, :, spot.core, part].astype(f32) + near0[...].astype(f32)).astype(bf16)
        for e in range(1, chips):
            to = spot.across(e)
            send(sums0.at[:, to[0] // 2], far0.at[e - 1], sb0.at[e - 1], rb0.at[e - 1], to)

    def early_line():
        total = sums0[:, spot.chip].astype(f32)
        for e in range(1, chips):
            landing(far0.at[e - 1], rb0.at[e - 1], spot).wait_recv()
            total += far0[e - 1].astype(f32)
        held0[...] = total.astype(bf16)
        for d in range(1, clips):
            to = spot.along(d)
            send(held0.at[to[1]], line0.at[d - 1], sc0.at[d - 1], rc0.at[d - 1], to)

    def early_end():
        total = held0[spot.clip].astype(f32)
        for d in range(1, clips):
            landing(line0.at[d - 1], rc0.at[d - 1], spot).wait_recv()
            total += line0[d - 1].astype(f32)
        early_ref[...] = total
        landing(near0, sa0.at[0], spot).wait_send()
        for e in range(1, chips):
            landing(far0.at[e - 1], sb0.at[e - 1], spot).wait_send()
        for d in range(1, clips):
            landing(line0.at[d - 1], sc0.at[d - 1], spot).wait_send()


    @pl.when(step == 0)
    def _():
        greet_all(spot)
        for u in range(2):
            momentum_copy(u).start()
        first, second = split_windows(cot_ref[...].astype(f32))
        whole = jnp.concatenate((first, second), axis=0)
        dout_s[...] = whole.astype(bf16)
        rows_s[7:8, :] = jnp.sum(whole, axis=0, keepdims=True)
        norms = []
        for w in range(2):
            normed, _ = layer_stats(middle_ref[w])
            norms.append(normed * vec_ref[5:6] + vec_ref[6:7])
        low = jnp.concatenate(norms, axis=0).astype(bf16)
        h2_s[...] = low
        h2t_s[...] = low.T
        acc_s[...] = jnp.zeros_like(acc_s)
        dh2_s[...] = jnp.zeros_like(dh2_s)

    def hidden_part(part):
        h2, dout = h2_s[...], dout_s[...]
        cols = slice(part * HALF, (part + 1) * HALF)
        w1 = w1_ref[0, :, part].reshape(width, HALF)
        w2 = [w2_ref[0, :, half].reshape(width, HALF)[cols] for half in range(2)]
        pre = mm(h2, w1) + vec_ref[pl.ds(8 + chunk, 1), cols]
        cdf = 0.5 * (1.0 + lax.erf(pre * 0.7071067811865476))
        act = (pre * cdf).astype(bf16)
        slope = cdf + pre * jnp.exp(-0.5 * pre * pre) * 0.3989422804014327
        d_act = mm_nt(dout[:, :HALF], w2[0]) + mm_nt(dout[:, HALF:], w2[1])
        d_pre = (d_act * slope).astype(bf16)
        rows_s[pl.ds(8 + chunk, 1), cols] = jnp.sum(d_pre.astype(f32), axis=0, keepdims=True)
        for half in range(2):
            acc_s[:, half * HALF : (half + 1) * HALF] += mm(act, w2[half])
        dh2_s[...] += mm_nt(d_pre, w1)
        g1 = mm(h2t_s[...], d_pre).astype(bf16)
        g2 = mm_tn(act, dout).astype(bf16)
        if early:
            g1_s[:, chunk, part] = g1.reshape(clips, rows, HALF)
        else:
            span = pl.ds((2 * chunk + part) * (share // 2), share // 2)
            g1_s[:, span] = g1.reshape(clips, share // 2, 2, rows, HALF)
        for half in range(2):
            piece = g2[:, half * HALF : (half + 1) * HALF]
            if clip_wide == 1:
                first = half * chips // 2 + part * chips // 4
                g2_s[chunk, first : first + chips // 4] = piece.reshape(chips // 4, 2, rows, HALF)
            else:
                planes = pl.ds(chunk * clip_wide + part * (clip_wide // 2), clip_wide // 2)
                span = slice(half * chips // 2, (half + 1) * chips // 2)
                g2_s[planes, span] = piece.reshape(clip_wide // 2, chips // 2, 2, rows, HALF)

    @pl.when(step < GROUPS)
    def _():
        hidden_part(0)

        @pl.when(step > 0)
        def _():
            send_far(chunk_of(step - 1, chips))

        hidden_part(1)
        send_near(chunk)

    @pl.when(step == GROUPS - 1)
    def _():
        results = []
        gain = jnp.zeros((1, width), f32)
        branch = jnp.zeros((1, width), f32)
        for w in range(2):
            span = slice(w * WINDOW, (w + 1) * WINDOW)
            middle = middle_ref[w]
            results.append(middle + acc_s[span, :] + vec_ref[7:8])
            normed, inverse = layer_stats(middle)
            d_second = dh2_s[span, :]
            gain += jnp.sum(d_second * normed, axis=0, keepdims=True)
            dmid_s[w] = norm_backward(d_second, normed, inverse, vec_ref[5:6])
        for w, rows_w in enumerate(split_windows(cot_ref[...].astype(f32))):
            d_middle = dmid_s[w] + rows_w
            dmid_s[w] = d_middle
            low = d_middle.astype(bf16)
            dbr_s[w] = low
            branch += jnp.sum(low.astype(f32), axis=0, keepdims=True)
        result_s[...] = join_windows(*results).astype(bf16).reshape(result_s.shape)
        rows_s[4:5, :] = branch
        rows_s[5:6, :] = gain
        rows_s[6:7, :] = jnp.sum(dh2_s[...], axis=0, keepdims=True)
        send_far(chunk)


    lanes = w_ref.shape[-1]
    head_dim = lanes // GROUP_HEADS
    scale = head_dim ** (-0.5)

    def grad_slices(matrix, half):
        if early:
            return (matrix, slice(None), matrix_at(matrix, half, share, rows)[0][1])
        return (pl.ds((2 * matrix + half) * share // 2, share // 2), slice(None), slice(None))

    def grad_shape(cols):
        return (clips, 2, rows // 2, cols) if early else (clips, share // 2, 2, rows, cols)

    @pl.when(step == GROUPS)
    def _():
        dh1t_s[...] = jnp.zeros_like(dh1t_s)
        for half in range(2):
            cols = slice(half * HALF, (half + 1) * HALF)
            grad = mm(mt_ref[0], dbr_s[0, :, cols]) + mm(mt_ref[1], dbr_s[1, :, cols])
            grad_ref[(slice(None), *grad_slices(3, half))] = grad.astype(bf16).reshape(grad_shape(HALF))

    def attention_group():
        place = pl.ds(pl.multiple_of(group * lanes, lanes), lanes)
        for w in range(2):
            branch = dbr_s[w]
            mixed = jnp.zeros((lanes, WINDOW), f32)
            for half in range(2):
                proj = p_ref[:, 0, :, half].reshape(lanes, HALF)
                mixed += mm_nt(proj, branch[:, half * HALF : (half + 1) * HALF])
            dot_s[w] = mixed

        @pl.when(step == GROUPS + 2)
        def _():
            if early:
                early_near()

        @pl.when(step == 2 * GROUPS - 1)
        def _():
            if early:
                early_line()
            hand_over()

        def head_step(head, carry):
            if early:
                pl.when(jnp.logical_and(step == GROUPS + 2, head == 2))(early_far)

            @pl.when(jnp.logical_and(step == GROUPS + 1, head == 2))
            def _():
                send_line()
                halo_out(spot, result_s, out_s, halo_send, halo_recv, halo_own.at[0])

            spread = pl.ds(pl.multiple_of(head * head_dim, head_dim), head_dim)
            in_all = pl.ds(pl.multiple_of(group * lanes + head * head_dim, head_dim), head_dim)
            for w in range(2):
                probs = probs_ref[head, w]
                scaled = dot_s[w, spread, :] * inv_ref[head, w]
                d_mixed = scaled.astype(bf16)
                inner = jnp.sum(scaled * mt_ref[w, in_all, :].astype(f32), axis=0, keepdims=True)
                d_probs = mm_tn(vt_ref[w, spread, :], d_mixed)
                d_scores = probs.astype(f32) * (d_probs - inner)
                if w == 0:
                    dsum_s[...] = d_scores
                else:
                    dsum_s[...] += d_scores
                d_raw = d_scores.astype(bf16)
                dqkv_s[w, 0, spread, :] = (mm(kt_ref[w, spread, :], d_raw) * scale).astype(bf16)
                dqkv_s[w, 1, spread, :] = (mm_nt(qt_ref[w, spread, :], d_raw) * scale).astype(bf16)
                dqkv_s[w, 2, spread, :] = mm_nt(d_mixed, probs).astype(bf16)
            wide_acc[...] = jnp.zeros_like(wide_acc)
            for cell_row in range(SIDE):
                offset = (SIDE - 1 - cell_row) * ROW
                wide_acc[:, offset : offset + WINDOW] += dsum_s[cell_row * ROW : (cell_row + 1) * ROW, :]
            for diff in range(SPAN):
                full = jnp.concatenate(
                    (wide_acc[:, diff * ROW : (diff + 1) * ROW], jnp.zeros((ROW, 128 - ROW), f32)), axis=1
                )
                folded = full[ROW - WIN_T :]
                for key in range(SIDE - 1):
                    folded += pltpu.roll(full[key * WIN_T : (key + 1) * WIN_T], (SIDE - 1 - key) * WIN_T, 1)
                wide_s[diff * HEADS + group * GROUP_HEADS + head] = folded
            return carry

        lax.fori_loop(0, GROUP_HEADS, head_step, 0)
        ones = jnp.ones((8, WINDOW), bf16)
        side = pl.ds(pl.multiple_of((group % 2) * lanes, lanes), lanes)
        for m in range(3):
            weights = w_ref[:, m, :, 0].reshape(width, lanes)
            grad = jnp.zeros((width, lanes), f32)
            total = jnp.zeros((8, lanes), f32)
            for w in range(2):
                piece = dqkv_s[w, m]
                dh1t_s[w] += mm(weights, piece)
                grad += mm_nt(h1t_ref[w], piece)
                total += mm_nt(ones, piece)
            grad_ref[(slice(None), *grad_slices(m, group // 2), side)] = grad.astype(bf16).reshape(grad_shape(lanes))
            sums_s[m, :, place] = total

    @pl.when(step >= GROUPS)
    def _():
        attention_group()

    @pl.when(step == 2 * GROUPS - 1)
    def _():
        gain = jnp.zeros((1, width), f32)
        shift = jnp.zeros((1, width), f32)
        grads = []
        for w, tokens in enumerate(split_windows(x_ref[...].astype(f32))):
            normed, inverse = layer_stats(tokens)
            d_first = dh1t_s[w].T
            gain += jnp.sum(d_first * normed, axis=0, keepdims=True)
            shift += jnp.sum(d_first, axis=0, keepdims=True)
            grads.append(dmid_s[w] + norm_backward(d_first, normed, inverse, vec_ref[0:1]))
        din_ref[...] = join_windows(*grads).astype(bf16)
        base = HEADS * SPAN
        lines = {0: gain, 1: shift, 2: sums_s[0, 0:1, :], 3: sums_s[2, 0:1, :]}
        lines.update({v: rows_s[v : v + 1] for v in range(4, vec_ref.shape[0])})
        for v, row in lines.items():
            for half in range(2):
                line_at = base + 2 * v + half
                small_ref[line_at : line_at + 1, :] = row[:, half * HALF : (half + 1) * HALF]
        spare = base + 2 * vec_ref.shape[0]
        small_ref[spare:, :] = jnp.zeros((small_ref.shape[0] - spare, HALF), f32)
        total = jnp.zeros((base, HALF), f32)
        for key in range(WIN_T):
            total += mm(wide_s[:, key, :].astype(bf16), pattern_ref[key * 128 : (key + 1) * 128, :])
        small_ref[:base, :] = total
        for copy in halo_back(spot, result_s, out_s, halo_send, halo_recv, halo_own.at[0]):
            copy.wait()
        outputs()[2].start()
        last_exchanges()
        for copy in outputs()[:2]:
            copy.start()
        if early:
            early_end()
        for copy in outputs():
            copy.wait()


def chunk_of(step, chips):
    first = lax.axis_index("seq") // 2 // (chips // GROUPS) + 1
    return (first + jnp.minimum(step, GROUPS - 1)) % GROUPS


def momentum_slice(refs, unit, spot, rows, dst, sem):
    _, _, first, second = refs
    share, tall = spot.seqs // 8, spot.seqs // 2
    if unit == 1:
        at = pl.ds(pl.multiple_of((spot.seq % share) * rows, rows), rows)
        cols = pl.ds(pl.multiple_of((spot.seq // share) * HALF, HALF), HALF)
        return pltpu.make_async_copy(first.at[at, cols], dst, sem)
    at = pl.ds(pl.multiple_of((spot.seq % tall) * rows, rows), rows)
    cols = pl.ds(pl.multiple_of((spot.seq // tall) * HALF, HALF), HALF)
    return pltpu.make_async_copy(second.at[at, cols], dst, sem)


def fc_owners(clips, chips):
    return [[owner_of(u, k, clips, chips) for k in range(2)] for u in (1, 2)]


def core(saved, middle, x_cells, cot_cells, packed0, packed12, vectors, pattern, momenta):
    probs, inv, qt, kt, vt, mt, h1t = saved
    clips, seqs, rows = packed0.shape[:3]
    chips, share = seqs // 2, seqs // 8
    rows_z = seqs * rows // 8
    width = x_cells.shape[-1]
    lanes = width // GROUPS
    tokens = 2 * WINDOW
    frames = x_cells.shape[1]
    first = packed12.reshape(2, clips, 8, rows_z, HALF)
    second = packed12.reshape(2, clips, 2, 4 * rows_z, HALF)
    early = share == 1
    split = (2, 2, rows // 2) if early else (1, 2, rows_z)
    mats = packed0.reshape(clips, 4, *split, HALF)
    z_step = clips // GROUPS
    unit = (clips, chips, 2, rows, HALF)
    tile = (SIDE, SIDE, frames, width)
    dma = pltpu.SemaphoreType.DMA

    def const(shape):
        return pl.BlockSpec(shape, lambda s: (0,) * len(shape), pipeline_mode=pl.Buffered(1))

    def hidden(s):
        return chunk_of(s, chips)

    def heads(s):
        return jnp.maximum(s - GROUPS, 0)

    group_block = pl.BlockSpec((2, lanes, WINDOW), lambda s: (0, heads(s), 0))
    vmem = pltpu.VMEM
    return pl.pallas_call(
        core_kernel,
        grid=(2 * GROUPS,),
        in_specs=[
            const(middle.shape),
            const(cot_cells.shape),
            pl.BlockSpec((1, clips, 2, rows_z, HALF), lambda s: (0, 0, hidden(s), 0, 0)),
            pl.BlockSpec((1, z_step, 2, 4 * rows_z, HALF), lambda s: (1, hidden(s), 0, 0, 0)),
            const(vectors.shape),
            pl.BlockSpec((GROUP_HEADS, 2, WINDOW, WINDOW), lambda s: (heads(s), 0, 0, 0)),
            pl.BlockSpec((GROUP_HEADS, 2, 1, WINDOW), lambda s: (heads(s), 0, 0, 0)),
            group_block,
            group_block,
            group_block,
            const(mt.shape),
            const(h1t.shape),
            const(x_cells.shape),
            pl.BlockSpec(
                (clips, 3, split[0], 1, split[2], lanes), lambda s: (0, 0, 0, heads(s) // 2, 0, heads(s) % 2)
            ),
            pl.BlockSpec((z_step, 1, *split, HALF), lambda s: (heads(s), 3, 0, 0, 0, 0)),
            const(pattern.shape),
            *[ANY] * 4,
        ],
        out_specs=[
            const(x_cells.shape),
            const(unit),
            const((SMALL, HALF)),
            const((rows // 2, HALF)),
            ANY,
            ANY,
            ANY,
        ],
        out_shape=[
            jax.ShapeDtypeStruct(x_cells.shape, bf16),
            jax.ShapeDtypeStruct(unit, bf16),
            jax.ShapeDtypeStruct((SMALL, HALF), f32),
            jax.ShapeDtypeStruct((rows // 2, HALF), f32),
            jax.ShapeDtypeStruct(tile, bf16),
            jax.ShapeDtypeStruct((clips, seqs, rows, HALF), bf16),
            jax.ShapeDtypeStruct((2, seqs, rows, HALF), bf16),
        ],
        scratch_shapes=[
            vmem((clips, seqs, rows, HALF), bf16),
            vmem((2, seqs, rows, HALF), bf16),
            vmem(tile, bf16),
            dma((3,)),
            vmem((tokens, width), bf16),
            vmem((width, tokens), bf16),
            vmem((tokens, width), bf16),
            vmem((tokens, width), f32),
            vmem((tokens, width), f32),
            vmem((16, width), f32),
            vmem((2, WINDOW, width), f32),
            vmem((2, WINDOW, width), bf16),
            vmem(tile, bf16),
            vmem(unit, bf16),
            vmem(unit, bf16),
            vmem((2, lanes, WINDOW), f32),
            vmem((2, 3, lanes, WINDOW), bf16),
            vmem((2, width, WINDOW), f32),
            vmem((WINDOW, WINDOW), f32),
            vmem((ROW, WIDE), f32),
            vmem((HEADS * SPAN, WIN_T, 128), f32),
            vmem((3, 8, width), f32),
            vmem((2, clips, chips, rows, HALF), bf16),
            vmem((2, clips, chips, rows, HALF), bf16),
            vmem((2, chips - 1, clips, rows, HALF), bf16),
            vmem((2, clips, rows, HALF), bf16),
            vmem((2, clips - 1, rows, HALF), bf16),
            vmem((2, rows, HALF), bf16),
            vmem((2, rows, HALF), bf16),
            vmem((2, rows, HALF), f32),
            vmem((clips, chips, rows // 2, HALF), bf16),
            vmem((clips, chips, rows // 2, HALF), bf16),
            vmem((chips - 1, clips, rows // 2, HALF), bf16),
            vmem((clips, rows // 2, HALF), bf16),
            vmem((clips - 1, rows // 2, HALF), bf16),
            dma((2, GROUPS)),
            dma((2, GROUPS)),
            dma((chips - 1,)),
            dma((chips - 1,)),
            dma((GROUPS, chips - 1)),
            dma((GROUPS, chips - 1)),
            dma((2, clips - 1)),
            dma((2, clips - 1)),
            dma((2, chips - 1)),
            dma((2, chips - 1)),
            dma((2, chips)),
            dma((2, chips)),
            dma((2, 2)),
            dma((2,)),
            dma((4,)),
            dma((1,)),
            dma((1,)),
            dma((chips - 1,)),
            dma((chips - 1,)),
            dma((clips - 1,)),
            dma((clips - 1,)),
            dma((3,)),
            dma((3,)),
            dma((1,)),
        ],
        compiler_params=pltpu.CompilerParams(
            collective_id=1, has_side_effects=True, vmem_limit_bytes=VMEM_LIMIT
        ),
        name="core",
    )(
        middle, cot_cells, first, second, vectors, probs, inv, qt, kt, vt, mt, h1t, x_cells, mats, mats, pattern,
        *momenta,
    )


def product_of(left, right):
    (lh, ll), (rh, rl) = left, right
    return mm(lh, rh) + (mm(lh, rl) + mm(ll, rh))


def ortho_square(whole_ref, update_ref, square_s, number):
    clips, seqs, rows = whole_ref.shape[:3]
    size = clips * seqs * rows // 8
    places = [matrix_at(number, half, seqs // 8, rows) for half in range(2)]
    parts = [whole_ref[(slice(None), *at)].reshape(size, HALF) for at, _ in places]
    low = jnp.concatenate(parts, axis=1)
    matrix = low.astype(f32)
    norm = jnp.sqrt(jnp.sum(matrix * matrix)) + frobenius_epsilon
    square_s[...] = matrix / norm
    for sweep in range(5):
        current = square_s[...]
        if sweep < 2:
            brief = current.astype(bf16)
            gram = mm_nt(brief, brief)
            short = gram.astype(bf16)
            poly = quintic_second * gram + quintic_third * mm(short, short)
            square_s[...] = quintic_first * current + mm(poly.astype(bf16), brief)
        else:
            high, low = halves(current)
            gram = mm_nt(high, high) + (mm_nt(high, low) + mm_nt(low, high))
            split = halves(gram)
            poly = quintic_second * gram + quintic_third * product_of(split, split)
            square_s[...] = quintic_first * current + product_of(halves(poly), (high, low))
    final = square_s[...].astype(bf16)
    for half, (at, shape) in enumerate(places):
        piece = final[:, half * HALF : (half + 1) * HALF].reshape(clips, *shape, HALF)
        update_ref[(slice(None), *at)] = piece


def gram_start(whole_ref, gram_s, norm_s, wide):
    clips, seqs, rows = whole_ref.shape[:3]
    size = clips * seqs * rows // 8
    gram = jnp.zeros((size, size), f32)
    for block in range(8 if wide else 4):
        piece = (wide_block if wide else tall_block)(whole_ref, block, size)
        gram += mm_nt(piece, piece) if wide else mm_tn(piece, piece)
    norm = jnp.sqrt(jnp.sum(jnp.where(diagonal(size), gram, 0.0))) + frobenius_epsilon
    inverse = 1.0 / norm
    norm_s[...] = jnp.zeros_like(norm_s) + inverse
    gram_s[...] = gram * (inverse * inverse)


def diagonal(size):
    shape = (size, size)
    return lax.broadcasted_iota(jnp.int32, shape, 0) == lax.broadcasted_iota(jnp.int32, shape, 1)


def gram_sweep(gram_s, poly_s, sweep):
    gram = gram_s[...]
    split = halves(gram)
    square = quintic_second * gram + quintic_third * product_of(split, split)
    poly = square + jnp.where(diagonal(gram.shape[0]), quintic_first, 0.0)
    parts = halves(poly)
    poly_s[...] = poly if sweep == 0 else product_of(parts, halves(poly_s[...]))
    if sweep < 4:
        gram_s[...] = product_of(parts, halves(product_of(parts, split)))


def gram_finish(whole_ref, update_ref, poly_s, norm_s, wide):
    clips, seqs, rows = whole_ref.shape[:3]
    size = clips * seqs * rows // 8
    high, low = halves(poly_s[...])
    inverse = norm_s[0:1, 0:1]
    for block in range(8 if wide else 4):
        if wide:
            piece = wide_block(whole_ref, block, size)
            store_wide(update_ref, block, ((mm(high, piece) + mm(low, piece)) * inverse).astype(bf16))
        else:
            piece = tall_block(whole_ref, block, size)
            done = (mm(piece, high) + mm(piece, low)) * (2.0 * inverse)
            store_tall(update_ref, block, done.astype(bf16))


def wide_block(ref, block, size):
    clips, seqs, rows = ref.shape[:3]
    count = seqs // 8
    return ref[:, block * count : (block + 1) * count].reshape(size, HALF)


def store_wide(ref, block, values):
    clips, seqs, rows = ref.shape[:3]
    count = seqs // 8
    ref[:, block * count : (block + 1) * count] = values.reshape(clips, count, rows, HALF)


def tall_block(ref, block, size):
    clips, seqs, rows = ref.shape[:3]
    span = slice(block * clips // 4, (block + 1) * clips // 4)
    count = seqs // 2
    parts = [ref[span, half * count : (half + 1) * count].reshape(size, HALF) for half in range(2)]
    return jnp.concatenate(parts, axis=1)


def store_tall(ref, block, values):
    clips, seqs, rows = ref.shape[:3]
    span = slice(block * clips // 4, (block + 1) * clips // 4)
    count = seqs // 2
    for half in range(2):
        piece = values[:, half * HALF : (half + 1) * HALF]
        ref[span, half * count : (half + 1) * count] = piece.reshape(clips // 4, count, rows, HALF)


def tail_kernel(
    g0_ref, small_ref, early_ref, wide_ref, qkv_ref, proj_ref, din_ref,
    dout_ref, shard_ref, step_ref, total_ref,
    near0, near1, sums0, sums1, far0, far1, held0, held1, line0, line1,
    moved, mom_s, edge_s, whole_s, update_s, gram_s, poly_s, norm_s,
    sa, ra, sb, rb, sc, rc, sd, rd, se, re, sf, rf, sg, rg, sh, rh, si, ri, sj, rj,
    halo_send, halo_recv, halo_own, mom_sem,
):
    spot = Spot()
    chips, clips, seqs = spot.chips, spot.clips, spot.seqs
    rows = moved.shape[0]
    share, quarter = seqs // 8, seqs // 4
    early = share == 1
    near, sums = (near0, near1), (sums0, sums1)
    far, held, line = (far0, far1), (held0, held1), (line0, line1)

    part = rows // 2 if early else rows
    rest = pl.ds(rows - part, part)
    matrix = spot.seq // (2 * share)
    if early:
        sub = pl.ds(pl.multiple_of(spot.core * part, part), part)
        cuts = [(sub, pl.ds(half * HALF, HALF), pl.ds(half * part, part)) for half in range(2)]
    else:
        sub = pl.ds(pl.multiple_of((spot.seq % share) * rows, rows), rows)
        cuts = [(sub, pl.ds(pl.multiple_of((spot.seq // share % 2) * HALF, HALF), HALF), pl.ds(0, rows))]

    @pl.when(matrix < 3)
    def _():
        for k, (sub, cols, to) in enumerate(cuts):
            pltpu.make_async_copy(qkv_ref.at[matrix, sub, cols], mom_s.at[to], mom_sem.at[k]).start()

    @pl.when(matrix == 3)
    def _():
        for k, (sub, cols, to) in enumerate(cuts):
            pltpu.make_async_copy(proj_ref.at[sub, cols], mom_s.at[to], mom_sem.at[k]).start()

    greet_all(spot)

    def at_place(place):
        return jnp.logical_and(place[0] == spot.seq, place[1] == spot.clip)

    owners = {(u, m): owner_of(u, m, clips, chips) for u in range(3) for m in range(2 if u else 4)}
    taker = owner_of(0, spot.seq // quarter, clips, chips)

    def hand_over(total, k):
        sub, cols, span = cuts[k]
        pltpu.make_async_copy(proj_ref.at[sub, cols], mom_s.at[span], mom_sem.at[k]).wait()
        moved[span] = (momentum_decay * mom_s[span] + total).astype(bf16)
        shard_ref[0, spot.seq, span] = total.astype(bf16)
        spare = whole_s.at[spot.clip, spot.seq, span]

        @pl.when(at_place(taker))
        def _():
            pltpu.make_async_copy(moved.at[span], spare, rg.at[0]).start()

        @pl.when(jnp.logical_not(at_place(taker)))
        def _():
            send(moved.at[span], spare, sg.at[k], rg.at[0], taker)

    def slot(u, seq):
        return total_ref.at[seq] if u == 1 else shard_ref.at[0, seq]

    def spread(u):
        here = slot(u, spot.seq)
        for e in range(1, chips):
            send(here, here, sd.at[u, e - 1], rd.at[u, e - 1], spot.across(e))
        send(here, here, se.at[u, 0], re.at[u, 0], spot.sibling)

    def forward(u):
        for e in range(1, chips):
            here = slot(u, spot.across(-e)[0])
            landing(here, rd.at[u, e - 1], spot).wait_recv()
            send(here, here, se.at[u, e], re.at[u, e], spot.sibling)

    def for_wide_owners(work):
        for u in (1, 2):

            @pl.when(jnp.logical_or(at_place(owners[u, 0]), at_place(owners[u, 1])))
            def _():
                work(u)

    def wide_sweep(sweep):
        mine = [at_place(owners[u, k]) for u in (1, 2) for k in range(2)]

        @pl.when(functools.reduce(jnp.logical_or, mine))
        def _():
            gram_sweep(gram_s, poly_s, sweep)

    def deal(u, number, settle):
        width, planes = (quarter, clips) if u == 0 else (seqs, clips // 2)

        def one(t):
            if u == 0:
                clip, seq = t // width, number * quarter + t % width
            else:
                clip, seq = number * planes + t // width, t % width
            src, dst = update_s.at[clip, seq], step_ref.at[u, seq]
            mine = at_place((seq, clip))
            if settle:

                @pl.when(jnp.logical_not(mine))
                def _():
                    landing(src, sh.at[clip, seq], spot).wait_send()

            else:

                @pl.when(mine)
                def _():
                    pltpu.make_async_copy(src, dst, rh.at[u]).start()

                @pl.when(jnp.logical_not(mine))
                def _():
                    send(src, dst, sh.at[clip, seq], rh.at[u], (seq, clip))

        if planes * width <= 16:
            for t in range(planes * width):
                one(t)
        else:

            def step(t, carry):
                one(t)
                return carry

            lax.fori_loop(0, planes * width, step, 0)

    send(g0_ref.at[:, :, 1 - spot.core, rest], near0, sa.at[0], ra.at[0], spot.sibling)
    send(small_ref.at[:, :, 1 - spot.core], near1, sa.at[1], ra.at[1], spot.sibling)
    if early:
        hand_over(early_ref[...], 0)

    def plane_send(k):
        landing(near[k], ra.at[k], spot).wait_recv()
        mine = g0_ref[:, :, spot.core, rest] if k == 0 else small_ref[:, :, spot.core]
        total = mine.astype(f32) + near[k][...].astype(f32)
        sums[k][...] = total.astype(sums[k].dtype)
        for e in range(1, chips):
            to = spot.across(e)
            send(sums[k].at[:, to[0] // 2], far[k].at[e - 1], sb.at[k, e - 1], rb.at[k, e - 1], to)

    def line_send(k):
        total = sums[k][:, spot.chip].astype(f32)
        for e in range(1, chips):
            landing(far[k].at[e - 1], rb.at[k, e - 1], spot).wait_recv()
            total += far[k][e - 1].astype(f32)
        held[k][...] = total.astype(held[k].dtype)
        for d in range(1, clips):
            to = spot.along(d)
            send(held[k].at[to[1]], line[k].at[d - 1], sc.at[k, d - 1], rc.at[k, d - 1], to)

    def line_sum(k):
        total = held[k][spot.clip].astype(f32)
        for d in range(1, clips):
            landing(line[k].at[d - 1], rc.at[k, d - 1], spot).wait_recv()
            total += line[k][d - 1].astype(f32)
        return total

    for_wide_owners(lambda u: gram_start(wide_ref, gram_s, norm_s, u == 1))
    for k in range(2):
        plane_send(k)
    wide_sweep(0)
    for k in range(2):
        line_send(k)
    wide_sweep(1)
    copies = halo_out(spot, din_ref, dout_ref, halo_send, halo_recv, halo_own.at[0])
    hand_over(line_sum(0), len(cuts) - 1)
    spread(0)
    edge_s[spot.clip] = line_sum(1)
    for d in range(1, clips):
        here = edge_s.at[spot.clip]
        send(here, here, sf.at[d - 1], rf.at[d - 1], spot.along(d))

    for sweep in range(2, 5):
        wide_sweep(sweep)

    def conclude(u):
        gram_finish(wide_ref, update_s, poly_s, norm_s, u == 1)
        for number in range(2):

            @pl.when(at_place(owners[u, number]))
            def _():
                deal(u, number, False)

    for_wide_owners(conclude)

    @pl.when(functools.reduce(jnp.logical_or, [at_place(owners[0, m]) for m in range(4)]))
    def _():
        number = spot.seq // quarter
        landing(whole_s.at[:, pl.ds(number * quarter, quarter)], rg.at[0], spot).wait_recv()
        ortho_square(whole_s, update_s, gram_s, number)

    for number in range(4):

        @pl.when(at_place(owners[0, number]))
        def _():
            deal(0, number, False)

    for d in range(1, clips):
        landing(edge_s.at[0], rf.at[d - 1], spot).wait_recv()
    total_ref[spot.seq] = edge_s[...]
    spread(1)
    forward(0)
    forward(1)

    order = (1, 2, 0)
    for u in order:
        here = step_ref.at[u, spot.seq]
        landing(here, rh.at[u], spot).wait_recv()
        for e in range(1, chips):
            send(here, here, si.at[u, e - 1], ri.at[u, e - 1], spot.across(e))
        send(here, here, sj.at[u, 0], rj.at[u, 0], spot.sibling)
    for u in order:
        for e in range(1, chips):
            here = step_ref.at[u, spot.across(-e)[0]]
            landing(here, ri.at[u, e - 1], spot).wait_recv()
            send(here, here, sj.at[u, e], rj.at[u, e], spot.sibling)

    for u in range(2):
        for e in range(chips):
            landing(slot(u, 0), re.at[u, e], spot).wait_recv()
            landing(slot(u, 0), se.at[u, e], spot).wait_send()
            if e > 0:
                landing(slot(u, 0), sd.at[u, e - 1], spot).wait_send()

    @pl.when(jnp.logical_not(at_place(taker)))
    def _():
        for k, (_, _, span) in enumerate(cuts):
            landing(moved.at[span], sg.at[k], spot).wait_send()

    for (u, number), place in owners.items():

        @pl.when(at_place(place))
        def _():
            deal(u, number, True)

    for k in range(2):
        landing(near[k], sa.at[k], spot).wait_send()
        for e in range(1, chips):
            landing(far[k].at[e - 1], sb.at[k, e - 1], spot).wait_send()
        for d in range(1, clips):
            landing(line[k].at[d - 1], sc.at[k, d - 1], spot).wait_send()
    for u in range(3):
        for e in range(chips):
            if e > 0:
                landing(step_ref.at[u, 0], si.at[u, e - 1], spot).wait_send()
            landing(step_ref.at[u, 0], sj.at[u, e], spot).wait_send()
            landing(step_ref.at[u, 0], rj.at[u, e], spot).wait_recv()
    for d in range(1, clips):
        landing(edge_s.at[0], sf.at[d - 1], spot).wait_send()
    for copy in copies:
        copy.wait()


def tail(grad, small, early, wide, qkv_m, proj_m, d_input):
    clips, seqs, rows, _ = wide.shape
    chips = seqs // 2
    size = clips * seqs * rows // 8
    small_rows = 8 * clips * seqs
    small = jnp.pad(small, ((0, small_rows - small.shape[0]), (0, 0)))
    cut = [grad, small.reshape(clips, chips, 2, 8, HALF)]
    kinds = [(bf16, rows // 2 if seqs == 8 else rows), (f32, 8)]
    dma = pltpu.SemaphoreType.DMA
    scratch = [pltpu.VMEM((clips, chips, r, HALF), t) for t, r in kinds]
    scratch += [pltpu.VMEM((clips, chips, r, HALF), t) for t, r in kinds]
    scratch += [pltpu.VMEM((chips - 1, clips, r, HALF), t) for t, r in kinds]
    scratch += [pltpu.VMEM((clips, r, HALF), t) for t, r in kinds]
    scratch += [pltpu.VMEM((clips - 1, r, HALF), t) for t, r in kinds]
    scratch += [
        pltpu.VMEM((rows, HALF), bf16),
        pltpu.VMEM((rows, HALF), f32),
        pltpu.VMEM((clips, 8, HALF), f32),
        pltpu.VMEM((clips, seqs, rows, HALF), bf16),
        pltpu.VMEM((clips, seqs, rows, HALF), bf16),
        pltpu.VMEM((size, size), f32),
        pltpu.VMEM((size, size), f32),
        pltpu.VMEM((8, 128), f32),
    ]
    scratch += [dma((2,)), dma((2,))]
    scratch += [dma((2, chips - 1)), dma((2, chips - 1))]
    scratch += [dma((2, clips - 1)), dma((2, clips - 1))]
    scratch += [dma((2, chips - 1)), dma((2, chips - 1))]
    scratch += [dma((2, chips)), dma((2, chips))]
    scratch += [dma((clips - 1,)), dma((clips - 1,))]
    scratch += [dma((2,)), dma((1,))]
    scratch += [dma((clips, seqs)), dma((3,))]
    scratch += [dma((3, chips - 1)), dma((3, chips - 1))]
    scratch += [dma((3, chips)), dma((3, chips))]
    scratch += [dma((3,)), dma((3,)), dma((1,)), dma((2,))]
    return pl.pallas_call(
        tail_kernel,
        in_specs=[WHOLE] * 4 + [ANY] * 2 + [WHOLE],
        out_specs=[WHOLE] * 4,
        out_shape=[
            jax.ShapeDtypeStruct(d_input.shape, bf16),
            jax.ShapeDtypeStruct((1, seqs, rows, HALF), bf16),
            jax.ShapeDtypeStruct((3, seqs, rows, HALF), bf16),
            jax.ShapeDtypeStruct((seqs, clips, 8, HALF), f32),
        ],
        scratch_shapes=scratch,
        compiler_params=pltpu.CompilerParams(
            collective_id=2, has_side_effects=True, vmem_limit_bytes=VMEM_LIMIT
        ),
        name="tail",
    )(*cut, early, wide, qkv_m, proj_m, d_input)


def blocks_of(shard, unit, at=None):
    seqs, rows = shard.shape[1:3]
    count = 2 if unit == 2 else 8
    share = seqs // count
    at = unit if at is None else at
    if unit == 0:
        places = [matrix_at(b // 2, b % 2, share, rows) for b in range(8)]
        return [shard[(at, *place)].reshape(share * rows, HALF) for place, _ in places]
    return [shard[at, b * share : (b + 1) * share].reshape(share * rows, HALF) for b in range(count)]


def places_of(refs):
    qkv, proj, first, second = refs
    cols = [slice(b * HALF, (b + 1) * HALF) for b in range(8)]
    mats = [(qkv, (b // 2, slice(None), cols[b % 2])) for b in range(6)]
    mats += [(proj, (slice(None), cols[b])) for b in range(2)]
    return (
        mats,
        [(first, (slice(None), cols[b])) for b in range(8)],
        [(second, (slice(None), cols[b])) for b in range(2)],
    )


def finish_kernel(
    first_ref, shard_ref, step_ref, *refs,
):
    old_refs, (out_ref, din_ref, total_ref, vec_ref, vecm_ref, table_ref, tablem_ref) = refs[:8], refs[8:15]
    new_refs, (new_out, new_din, new_vecm, new_vec, new_tablem, new_table) = refs[15:23], refs[23:29]
    first_s, shard_s, step_s = refs[29:32]
    old_s, new_s = refs[32:40], refs[40:48]
    tile_s, flat_s, grad_s, in_sem, old_sem, new_sem, tile_sem = refs[48:]
    slices = [
        pltpu.make_async_copy(src, dst, in_sem.at[k])
        for k, (src, dst) in enumerate(((first_ref, first_s), (shard_ref, shard_s), (step_ref, step_s)))
    ]
    loads = [pltpu.make_async_copy(old_refs[k], old_s[k], old_sem.at[k]) for k in range(8)]
    stores = [pltpu.make_async_copy(new_s[k], new_refs[k], new_sem.at[k]) for k in range(8)]
    arrivals = [pltpu.make_async_copy(src, tile_s.at[k], tile_sem.at[k]) for k, src in enumerate((out_ref, din_ref))]
    tiles = [pltpu.make_async_copy(tile_s.at[k], dst, tile_sem.at[2 + k]) for k, dst in enumerate((new_out, new_din))]
    slices[0].start()
    loads[0].start()
    loads[1].start()
    slices[1].start()
    loads[2].start()
    loads[3].start()
    slices[2].start()
    for k in range(4, 8):
        loads[k].start()
    for copy in arrivals:
        copy.start()

    def place_of(unit, refs):
        return places_of(refs)[unit]

    for group in range(2):
        old, new = old_s[4 * group : 4 * group + 4], new_s[4 * group : 4 * group + 4]
        if group == 1:
            slices[2].wait()
        for unit in range(3):
            if group == 0 and unit < 2:
                slices[unit].wait()
            arrays = ((0, 1), (2,), (3,))[unit]
            for k in arrays:
                loads[4 * group + k].wait()
            if group == 1:
                blocks = blocks_of(step_s, unit)
            else:
                blocks = blocks_of(shard_s, unit, unit - 1) if unit else blocks_of(first_s, 0)
            for block, (src, at), (dst, _) in zip(blocks, place_of(unit, old), place_of(unit, new)):
                if group == 0:
                    dst[at] = momentum_decay * src[at] + block.astype(f32)
                else:
                    dst[at] = src[at] - matrix_rate * block.astype(f32)
            for k in arrays:
                stores[4 * group + k].start()

    for arrival, tile in zip(arrivals, tiles):
        arrival.wait()
        tile.start()
    seqs = total_ref.shape[0]
    for q in range(SMALL // 8):
        flat_s[q * 8 : (q + 1) * 8, :] = total_ref[q % seqs, q // seqs]
    base = HEADS * SPAN
    for v in range(vec_ref.shape[0]):
        for half in range(2):
            line_at = base + 2 * v + half
            grad_s[v : v + 1, half * HALF : (half + 1) * HALF] = flat_s[line_at : line_at + 1, :]
    moved = vector_decay * vecm_ref[...] + grad_s[...]
    new_vecm[...] = moved
    new_vec[...] = vec_ref[...] - vector_rate * moved
    for time in range(SPAN_T):
        for step in range(SPAN):
            offset = time * SPAN * SPAN + step * SPAN
            piece = flat_s[step * HEADS : (step + 1) * HEADS, time * SPAN : (time + 1) * SPAN]
            new_tablem[:, offset : offset + SPAN] = piece
    moved = vector_decay * tablem_ref[...] + new_tablem[...]
    new_tablem[...] = moved
    new_table[...] = table_ref[...] - table_rate * moved
    for copy in stores + tiles:
        copy.wait()


def finish(first, shard, step, momenta, weights, tiles, total, vectors, vector_m, table_t, table_mt):
    olds = (*momenta, *weights)
    small = (vector_m, vectors, table_mt, table_t)
    dma = pltpu.SemaphoreType.DMA
    return pl.pallas_call(
        finish_kernel,
        in_specs=[ANY] * 13 + [WHOLE] * 5,
        out_specs=[ANY] * 10 + [WHOLE] * 4,
        out_shape=[jax.ShapeDtypeStruct(a.shape, a.dtype) for a in (*olds, *tiles, *small)],
        scratch_shapes=[
            *[pltpu.VMEM(a.shape, a.dtype) for a in (first, shard, step, *olds, *olds)],
            pltpu.VMEM((2, *tiles[0].shape), bf16),
            pltpu.VMEM((SMALL, HALF), f32),
            pltpu.VMEM(vectors.shape, f32),
            dma((3,)),
            dma((8,)),
            dma((8,)),
            dma((4,)),
        ],
        compiler_params=pltpu.CompilerParams(vmem_limit_bytes=VMEM_LIMIT),
        name="finish",
    )(first, shard, step, *olds, *tiles, total, vectors, vector_m, table_t, table_mt)


def local(
    clips, cotangent, qkv_w, proj_w, fc1_w, fc2_w, qkv_m, proj_m, fc1_m, fc2_m,
    vectors, vector_m, table, table_m,
):
    frames = clips.shape[2]
    width = clips.shape[-1]
    weights = (qkv_w, proj_w, fc1_w, fc2_w)
    momenta = (qkv_m, proj_m, fc1_m, fc2_m)
    tile_in = clips[0, 0].transpose(1, 2, 0, 3)
    tile_cot = cotangent[0, 0].transpose(1, 2, 0, 3)
    pattern = time_pattern()
    probs, inv, qt, kt, vt, mt, middle, h1t, x_tile, cot_tile, packed0, packed12 = front(
        tile_in, tile_cot, weights, vectors, table.T, pattern
    )
    x_cells = x_tile.reshape(CELLS, frames, width)
    cot_cells = cot_tile.reshape(CELLS, frames, width)
    saved = (probs, inv, qt, kt, vt, mt, h1t)
    d_input, g0, small, early, output, wide, shard = core(
        saved, middle, x_cells, cot_cells, packed0, packed12, vectors, pattern, momenta
    )
    input_grad, first, step, total = tail(g0, small, early, wide, qkv_m, proj_m, d_input.reshape(tile_in.shape))
    *rest, output, input_grad, new_vector_m, new_vectors, new_table_m, new_table = finish(
        first, shard, step, momenta, weights, (output, input_grad), total, vectors, vector_m, table.T, table_m.T
    )
    output = output.transpose(2, 0, 1, 3)[None, None]
    input_grad = input_grad.transpose(2, 0, 1, 3)[None, None]
    return (output, input_grad, *rest, new_vector_m, new_vectors, new_table_m.T, new_table.T)


def solution(mesh):
    tile = P("clip", "seq", None, None, None, None)
    stack = P(None, "clip", None)
    rows = P("clip", None)
    weights = (stack, rows, rows, rows)
    return jax.shard_map(
        local,
        mesh=mesh,
        in_specs=(tile, tile, *weights, *weights, P(), P(), P(), P()),
        out_specs=(tile, tile, *weights, *weights, P(), P(), P(), P()),
        check_vma=False,
    )
```
